32 devices in a mesh: dp: 32 (over z, y, x, core).
Axes of the slice: x: 2, y: 2, z: 4, core: 2. Of those that a mesh axis runs over, the one named last changes fastest.
Arguments:
- tokens: bfloat16 [16384, 896], P('dp'), may hold values from -8 to 8
- segment_ids: int32 [16384], P('dp'), may hold values from 0 to 512, as said below
- live_counts: int32 [32], P('dp'), may hold values from 256 to 512, as said below
- first_gain: bfloat16 [896], P('dp'), may hold values from 0.099609375 to 1.8984375
- query_weight: bfloat16 [896, 896], P('dp'), may hold values from -0.1875 to 0.1875
- query_bias: bfloat16 [896], P('dp'), may hold values from -3 to 3
- key_weight: bfloat16 [128, 896], P('dp'), may hold values from -0.1875 to 0.1875
- value_weight: bfloat16 [128, 896], P('dp'), may hold values from -0.1875 to 0.1875
- key_value_bias: bfloat16 [128, 2], P('dp'), may hold values from -3 to 3
- output_weight: bfloat16 [896, 896], P('dp'), may hold values from -0.75 to 0.75
- second_gain: bfloat16 [896], P('dp'), may hold values from 0.099609375 to 1.8984375
- gate_weight: bfloat16 [4864, 896], P('dp'), may hold values from -0.1875 to 0.1875
- up_weight: bfloat16 [4864, 896], P('dp'), may hold values from -0.1875 to 0.1875
- down_weight: bfloat16 [896, 4864], P('dp'), may hold values from -0.078125 to 0.078125
- cotangent: bfloat16 [16384, 896], P('dp'), may hold values from -6 to 6
Outputs:
- layer_out: float32 [16384, 896], P('dp')
- input_grad: float32 [16384, 896], P('dp')
- first_gain_grad: float32 [896], P('dp')
- query_weight_grad: float32 [896, 896], P('dp')
- query_bias_grad: float32 [896], P('dp')
- key_weight_grad: float32 [128, 896], P('dp')
- value_weight_grad: float32 [128, 896], P('dp')
- key_value_bias_grad: float32 [128, 2], P('dp')
- output_weight_grad: float32 [896, 896], P('dp')
- second_gain_grad: float32 [896], P('dp')
- gate_weight_grad: float32 [4864, 896], P('dp')
- up_weight_grad: float32 [4864, 896], P('dp')
- down_weight_grad: float32 [896, 4864], P('dp')
The draws below stay inside these ranges and needn't reach their ends.
Inputs may be any that keep to these rules, and one draw needn't show every extreme that they name: `live_counts`: each device's block of 512 slots holds its live slots first; some device in every draw has all 512 slots live and some has half of 512. `segment_ids`: within a device's block the ids never fall and start at 0; each id below 512 is one sequence of live slots; slots past the live count hold 512; some device holds one sequence of 512 tokens.
All inputs are finite; a program needn't handle non-finite values.
Results may differ from the reference program's by a relative error of at most 0.012.
Values may be sent and summed in bfloat16 or wider, within the bound.
A program may use at most 256 MiB of HBM per device.

```python
import math
import jax
import jax.numpy as jnp
from jax import lax

D = 896
HEADS = 14
KV = 2
HD = 64
FF = 4864
TOK_DEV = 512
TOKENS = 16384


def draw_tokens(key, part):
    first_key, second_key = jax.random.split(key, 2)
    row_scale = jnp.exp(jax.random.uniform(second_key, (TOKENS, 1), minval=math.log(0.3), maxval=math.log(3.0)))
    base_values = jax.random.normal(first_key, (TOKENS, D), dtype=jnp.float32)
    return jnp.clip(base_values * row_scale, -8.0, 8.0).astype(jnp.bfloat16)


def layout_draw(key):
    layout_key = jax.random.fold_in(key, 11)
    count_key, order_key, start_key = jax.random.split(layout_key, 3)
    device_count = TOKENS // TOK_DEV
    counts = jax.random.randint(count_key, (device_count,), TOK_DEV // 2, TOK_DEV + 1)
    order = jax.random.permutation(order_key, device_count)
    counts = jnp.where(order == 0, TOK_DEV, counts)
    counts = jnp.where(order == 1, TOK_DEV // 2, counts)
    starts = (jax.random.randint(start_key, (device_count, TOK_DEV), 0, 128) == 0).astype(jnp.int32)
    slot_index = jnp.arange(TOK_DEV)[None, :]
    starts = jnp.where(slot_index == 0, 0, starts)
    starts = jnp.where((order == 0)[:, None], 0, starts)
    segment_values = jnp.cumsum(starts, axis=1)
    segment_values = jnp.where(slot_index < counts[:, None], segment_values, TOK_DEV)
    return (counts.astype(jnp.int32), segment_values.reshape(-1).astype(jnp.int32))


def draw_live_counts(key, part):
    return layout_draw(key)[0]


def draw_segment_ids(key, part):
    return layout_draw(key)[1]


def spiked(drawn, key, source, target, blocks, factor):
    owner, partner = [(jnp.arange(drawn.shape[axis_at]) // (drawn.shape[axis_at] // blocks)).reshape([-1 if axis == axis_at else 1 for axis in range(drawn.ndim)]) for axis_at in (source, target)]
    chosen = jax.random.permutation(key, blocks)[partner]
    strong = (owner == chosen) | (owner == (partner + blocks // 2) % blocks)
    return jnp.where(strong, factor * drawn, drawn)


def levels(rng, extent, cuts, least, high):
    factor_of = 1.0
    for axis_at, shards_of in cuts:
        heights = jax.random.uniform(jax.random.fold_in(jax.random.fold_in(rng, 6), axis_at), (shards_of,), jnp.float32, least / len(cuts), high / len(cuts))
        factor_of = factor_of * jnp.repeat(jnp.exp(heights), extent[axis_at] // shards_of).reshape((-1,) + (1,) * (len(extent) - 1 - axis_at))
    return factor_of


def scatter_about(rng, shape, width, bound, cuts=(), held_as=jnp.bfloat16):
    factor_of = levels(rng, shape, cuts, -0.22, 0.18) if cuts else 1.0
    result = jax.random.normal(rng, shape, jnp.float32) * width * factor_of
    return jnp.minimum(jnp.maximum(result, -bound), bound).astype(held_as)


def bell_draw_with(key, extent, width, most, pieces, heavy, kind=jnp.bfloat16):
    array = width * jax.random.normal(key, extent, jnp.float32)
    if pieces:
        array = array * levels(key, extent, pieces, -0.22, 0.18)
    return jnp.clip(spiked(array, jax.random.fold_in(key, 3), *heavy), -most, most).astype(kind)


def setup_inputs(seed: int = 0) -> dict:
    key_of = jax.random.split(jax.random.key(seed), 16)
    tokens = draw_tokens(jax.random.fold_in(key_of[15], 71), 0)
    segment_ids = draw_segment_ids(jax.random.fold_in(key_of[15], 71), 0)
    live_counts = draw_live_counts(jax.random.fold_in(key_of[15], 71), 0)
    first_gain = jnp.clip(1.0 + 0.18 * jax.random.normal(key_of[3], (D,), jnp.float32), 0.099609375, 1.8984375).astype(jnp.bfloat16)
    query_weight = scatter_about(key_of[4], (D, D), D ** -0.5, 0.1875, ((0, 32),))
    query_bias = scatter_about(key_of[5], (D,), 0.5, 3.0, ((0, 32),))
    key_weight = scatter_about(key_of[6], (KV * HD, D), D ** -0.5, 0.1875, ((0, 32),))
    value_weight = scatter_about(key_of[7], (KV * HD, D), D ** -0.5, 0.1875, ((0, 32),))
    key_value_bias = scatter_about(key_of[8], (KV * HD, 2), 0.5, 3.0, ((0, 32),))
    output_weight = scatter_about(key_of[9], (D, D), (D // 16) ** -0.5, 0.75, ((0, 32),))
    second_gain = jnp.clip(1.0 + 0.18 * jax.random.normal(key_of[10], (D,), jnp.float32), 0.099609375, 1.8984375).astype(jnp.bfloat16)
    gate_weight = scatter_about(key_of[11], (FF, D), D ** -0.5, 0.1875, ((0, 32),))
    up_weight = scatter_about(key_of[12], (FF, D), D ** -0.5, 0.1875, ((0, 32),))
    down_weight = scatter_about(key_of[13], (D, FF), FF ** -0.5, 0.078125, ((0, 32),))
    cotangent = bell_draw_with(key_of[14], (TOKENS, D), 1.0, 6.0, ((0, 32),), (0, 1, 32, 2.75))
    return {"tokens": tokens, "segment_ids": segment_ids, "live_counts": live_counts, "first_gain": first_gain, "query_weight": query_weight, "query_bias": query_bias, "key_weight": key_weight, "value_weight": value_weight, "key_value_bias": key_value_bias, "output_weight": output_weight, "second_gain": second_gain, "gate_weight": gate_weight, "up_weight": up_weight, "down_weight": down_weight, "cotangent": cotangent}


@jax.custom_vjp
def low(v):
    return lax.optimization_barrier(v.astype(jnp.bfloat16)).astype(jnp.float32)

@jax.custom_vjp
def low_back(v):
    return v

def low_keep(v):
    return (low(v), None)

def low_pass(kept, grad):
    return (grad,)

def back_keep(v):
    return (v, None)

def back_low(kept, grad):
    return (low(grad),)
low.defvjp(low_keep, low_pass)
low_back.defvjp(back_keep, back_low)
eps_norm = 1e-06
rope_base = 1000000.0
masked_value = -1e+30
highest = lax.Precision.HIGHEST

def apply_weight(left, weight):
    return jnp.dot(left, weight.T, precision=highest, preferred_element_type=jnp.float32)

def rms_scale(field_rows):
    return lax.rsqrt(lax.optimization_barrier(jnp.mean(field_rows * field_rows, axis=1, keepdims=True)) + eps_norm)

def rope_tables(block_segments):
    slot_index = jnp.arange(block_segments.shape[0])
    same_segment = block_segments[:, None] == block_segments[None, :]
    earlier = slot_index[None, :] < slot_index[:, None]
    positions = lax.optimization_barrier(jnp.sum((same_segment & earlier).astype(jnp.float32), axis=1))
    frequency = jnp.exp(jnp.arange(HD // 2, dtype=jnp.float32) * (-2.0 * math.log(rope_base) / HD))
    angles = positions[:, None] * frequency[None, :]
    return (jnp.cos(angles)[:, None, :], jnp.sin(angles)[:, None, :])

def rotate(vectors, cosine_table, sine_table):
    first_half = vectors[..., :HD // 2]
    second_half = vectors[..., HD // 2:]
    return jnp.concatenate([first_half * cosine_table - second_half * sine_table, second_half * cosine_table + first_half * sine_table], axis=-1)

def block_forward(params, block_tokens, block_segments, block_live):
    first_gain, query_weight, query_bias, key_weight, value_weight, key_value_bias, output_weight, second_gain, gate_weight, up_weight, down_weight = params
    slot_count = block_tokens.shape[0]
    slot_index = jnp.arange(slot_count)
    allowed = (block_segments[:, None] == block_segments[None, :]) & (slot_index[None, :] <= slot_index[:, None]) & (block_live[None, :] > 0.5) | (slot_index[None, :] == slot_index[:, None])
    cosine_table, sine_table = rope_tables(block_segments)
    normed = low(block_tokens * rms_scale(block_tokens) * first_gain)
    query_pre = low_back(apply_weight(normed, query_weight) + query_bias)
    key_pre = low_back(apply_weight(normed, key_weight) + key_value_bias[:, 0])
    values = low(low_back(apply_weight(normed, value_weight) + key_value_bias[:, 1])).reshape(slot_count, KV, HD)
    rotated_queries = low(rotate(query_pre.reshape(slot_count, HEADS, HD), cosine_table, sine_table))
    rotated_queries = rotated_queries.reshape(slot_count, KV, HEADS // KV, HD)
    rotated_keys = low(rotate(key_pre.reshape(slot_count, KV, HD), cosine_table, sine_table))
    scores = low_back(jnp.einsum('ikgd,jkd->kgij', rotated_queries, rotated_keys, precision=highest))
    logits = jnp.where(allowed[None, None], scores * HD ** (-0.5), masked_value)
    weights = low(jax.nn.softmax(logits, axis=-1))
    mixed_heads = jnp.einsum('kgij,jkd->ikgd', weights, values, precision=highest).reshape(slot_count, D)
    mixed_heads = low(low_back(mixed_heads))
    residual = block_tokens + low_back(apply_weight(mixed_heads, output_weight))
    second = low(residual * rms_scale(residual) * second_gain)
    gate_value = low_back(apply_weight(second, gate_weight))
    up_value = low_back(apply_weight(second, up_weight))
    hidden = low(jax.nn.silu(gate_value) * up_value)
    return (residual + low_back(apply_weight(hidden, down_weight))) * block_live[:, None]

def reference(tokens, segment_ids, live_counts, first_gain, query_weight, query_bias, key_weight, value_weight, key_value_bias, output_weight, second_gain, gate_weight, up_weight, down_weight, cotangent):
    params = tuple((weight.astype(jnp.float32) for weight in (first_gain, query_weight, query_bias, key_weight, value_weight, key_value_bias, output_weight, second_gain, gate_weight, up_weight, down_weight)))
    device_count = live_counts.shape[0]
    token_blocks = tokens.astype(jnp.float32).reshape(device_count, TOK_DEV, D)
    segment_blocks = segment_ids.reshape(device_count, TOK_DEV)
    live_blocks = (jnp.arange(TOK_DEV)[None, :] < live_counts[:, None]).astype(jnp.float32)
    cot_blocks = cotangent.astype(jnp.float32).reshape(device_count, TOK_DEV, D)
    checked = jax.checkpoint(block_forward)

    def one_block(carry, block_items):
        block_tokens, block_segments, block_live, block_cot = block_items

        def local_layer(weights, inputs):
            return checked(weights, inputs, block_segments, block_live)
        outputs, pullback = jax.vjp(local_layer, params, block_tokens)
        block_weight_grads, block_input_grads = pullback(block_cot)
        carry = tuple((total + part for total, part in zip(carry, block_weight_grads)))
        return (carry, (outputs, block_input_grads))
    start = tuple((jnp.zeros_like(weight) for weight in params))
    weight_grads, (outputs, input_grads) = lax.scan(one_block, start, (token_blocks, segment_blocks, live_blocks, cot_blocks))
    return (outputs.reshape(TOKENS, D), input_grads.reshape(TOKENS, D), weight_grads[0], weight_grads[1], weight_grads[2], weight_grads[3], weight_grads[4], weight_grads[5], weight_grads[6], weight_grads[7], weight_grads[8], weight_grads[9], weight_grads[10])
```

```python
import functools
import math

import jax
import jax.numpy as jnp
from jax import lax
from jax.experimental import pallas as pl
from jax.experimental.pallas import tpu as pltpu
from jax.sharding import PartitionSpec as P

MESH = pl.DeviceIdType.MESH
F32 = jnp.float32
BF16 = jnp.bfloat16

HEADS = 14
KV = 2
HD = 64
GROUP = HEADS // KV
PAIRS = HEADS // 2
LANES = 128
EPS = 1e-06
ROPE_BASE = 1000000.0
MASKED = -1e30
SCALE = HD ** (-0.5)


def up16(n):
    return -(-n // 16) * 16


def nn(a, b):
    return jnp.dot(a, b, preferred_element_type=F32)


def nt(a, b):
    return lax.dot_general(a, b, (((1,), (1,)), ((), ())), preferred_element_type=F32)


def tn(a, b):
    return lax.dot_general(a, b, (((0,), (0,)), ((), ())), preferred_element_type=F32)


class Geometry:
    def __init__(self, devices, slots, width, hidden):
        self.n = devices
        self.R = devices // 4
        self.T = slots
        self.D = width
        self.FS = hidden // devices
        self.FP = up16(self.FS)
        self.U = self.R * self.FP
        self.DS = width // devices
        self.DSP = up16(self.DS)
        self.DP = 4 * self.DS
        self.DA = up16(self.DP // 2)
        self.KS = KV * HD // devices
        self.AR = 2 * self.DS + 2 * self.KS
        self.OFF = -(self.R // 4)
        self.CUT = 3 * self.U // 5 // 256 * 256

    def fits(self):
        return (
            self.n % 32 == 0
            and self.DP % 16 == 0
            and self.AR % 32 == 0
            and (4 * self.KS) % 16 == 0
            and self.U % 256 == 0
            and self.R * self.AR == self.T
            and 2 * self.D + 2 * KV * HD == 4 * self.T
            and 3 * self.DS + 2 * self.KS <= LANES
            and 4 * self.T * self.U * 6 <= 16 * 2**20
        )


def ring_place(g, R):
    odd = lax.rem(g, 2)
    half = lax.div(g, 2)
    return (1 - odd) * half + odd * (R - 1 - half)


def ring_group(place, R):
    high = lax.div(place, R // 2)
    return (1 - high) * (2 * place) + high * (2 * (R - 1 - place) + 1)


class Net:
    def __init__(self, send_sems, recv_sems, local_sems):
        self.send_sems, self.recv_sems, self.local_sems = send_sems, recv_sems, local_sems
        self.count = 0
        self.local_count = 0
        self.open = []

    def copy(self, src, dst, device):
        i = self.count
        self.count += 1
        made = pltpu.make_async_remote_copy(
            src_ref=src,
            dst_ref=dst,
            send_sem=self.send_sems.at[i],
            recv_sem=self.recv_sems.at[i],
            device_id=(device,),
            device_id_type=MESH,
        )
        self.open.append(made)
        return made

    def sent(self, copies):
        for c in copies:
            c.wait_send()
        self.open = [x for x in self.open if all(x is not c for c in copies)]

    def local(self, src, dst):
        i = self.local_count
        self.local_count += 1
        return pltpu.make_async_copy(src, dst, self.local_sems.at[i])


def parts(lo, hi, step):
    return [slice(at, min(at + step, hi)) for at in range(lo, hi, step)]


def iota(shape, axis):
    return lax.broadcasted_iota(jnp.int32, shape, axis)


def kernel_body(geo, names, *refs):
    v = dict(zip(names, refs))
    R, T, D, FP, FS, U = geo.R, geo.T, geo.D, geo.FP, geo.FS, geo.U
    DSP, DS, DP, DA, KS, AR, CUT = geo.DSP, geo.DS, geo.DP, geo.DA, geo.KS, geo.AR, geo.CUT
    H = AR // 2
    me = lax.axis_index("dp")
    m, g = lax.rem(me, 4), lax.div(me, 4)
    r = ring_place(g, R)

    def place_group(k):
        return ring_group(lax.rem(r + k + 2 * R, R), R)

    right = place_group(1) * 4 + m
    left = place_group(-1) * 4 + m
    m1 = m + 1 - 2 * lax.rem(m, 2)
    m2 = m + 2 - 4 * lax.div(m, 2)
    m3 = m1 + 2 - 4 * lax.div(m1, 2)
    core, beside, across = g * 4 + m1, g * 4 + m2, g * 4 + m3
    net = Net(v["send_sems"], v["recv_sems"], v["local_sems"])

    barrier = pltpu.get_barrier_semaphore()
    for peer in (right, left, core, beside, across):
        pl.semaphore_signal(barrier, inc=1, device_id=(peer,), device_id_type=MESH)

    AW, SM = v["AW"], v["SM"]
    tmp = v["tmp"]

    tmp[0:DS, 0:D] = v["wq"][...].astype(F32)
    tmp[DS : 2 * DS, 0:D] = v["wo"][...].astype(F32)
    tmp[2 * DS : 2 * DS + KS, 0:D] = v["wk"][...].astype(F32)
    tmp[2 * DS + KS : AR, 0:D] = v["wv"][...].astype(F32)

    def arow(dev_m, k, lo=0, size=AR):
        return pl.ds(pl.multiple_of((dev_m * R + place_group(k)) * AR + lo, 16), size)

    AW[arow(m, 0), :] = tmp[0:AR, 0:D].astype(BF16)

    def srow(dev_m, k):
        return pl.ds(pl.multiple_of((dev_m * R + place_group(k)) * 8, 8), 8)

    SM[srow(m, 0), :] = v["small"][...]
    pl.semaphore_wait(barrier, 5)

    long_way, short_way = R // 2, R // 2 - 1
    classes = {"A": (long_way, short_way), "B": (short_way, long_way)}

    class Gather:
        def __init__(self, cls, src, dst, arrive=None):
            self.nf, self.nb = classes[cls]
            self.f = [net.copy(src(-(s - 1)), dst(-s, s), right) for s in range(1, self.nf + 1)]
            self.b = [net.copy(src(s - 1), dst(s, s), left) for s in range(1, self.nb + 1)]
            self.arrive = arrive

        def begin(self):
            self.f[0].start()
            self.b[0].start()

        def serve(self, s):
            if s <= self.nf:
                self.f[s - 1].wait_recv()
            if s <= self.nb:
                self.b[s - 1].wait_recv()
            if self.arrive and s <= self.nf:
                self.arrive(-s, s)
            if self.arrive and s <= self.nb:
                self.arrive(s, s)
            if s < self.nf:
                self.f[s].start()
            if s < self.nb:
                self.b[s].start()

    dx = v["dx"]
    down_copies = [
        net.copy(v["down_p"].at[dst_m], dx.at[m], dev)
        for dst_m, dev in ((m1, core), (m2, beside), (m3, across))
    ]

    def nearer(k):
        return k + 1 if k < 0 else k - 1

    def attn_gather(cls, lo):
        def at(k):
            return AW.at[arow(m, k, lo, H)]

        return Gather(cls, at, lambda k, s: at(nearer(k)))

    gaA, gaB = attn_gather("A", 0), attn_gather("B", H)
    gsm = Gather("A", lambda k: SM.at[srow(m, k)], lambda k, s: SM.at[srow(m, nearer(k))])
    ks = [0]
    for s in range(1, long_way + 1):
        ks += [-s, s] if s < long_way else [s]
    to_beside = {k: net.copy(AW.at[arow(m, k)], AW.at[arow(m, k)], beside) for k in ks}
    to_core = {k: net.copy(AW.at[arow(m, k)], AW.at[arow(m, k)], core) for k in ks}
    on_core = {k: net.copy(AW.at[arow(m2, k)], AW.at[arow(m2, k)], core) for k in ks}

    def small_rows(dev_m):
        return SM.at[pl.ds(pl.multiple_of(dev_m * R * 8, 8), R * 8)]

    small_beside = net.copy(small_rows(m), small_rows(m), beside)
    small_core = net.copy(small_rows(m), small_rows(m), core)
    small_on = net.copy(small_rows(m2), small_rows(m2), core)
    attn_copies = gaA.f + gaA.b + gaB.f + gaB.b + gsm.f + gsm.b
    attn_copies += list(to_beside.values()) + list(to_core.values()) + list(on_core.values())
    attn_copies += [small_beside, small_core, small_on]

    gsm.begin()
    gaA.begin()
    gaB.begin()

    def fan_out(k):
        to_beside[k].start()
        to_core[k].start()

    bring_cot = net.local(v["cot"], v["dO"].at[pl.ds(0, T)])
    bring_cot.start()
    fan_out(0)
    for c in down_copies:
        c.start()

    S, dO = v["S"], v["dO"]
    aux = v["aux"]

    stats, bias = v["stats"], v["bias"]
    frequency = jnp.exp(
        lax.rem(iota((1, LANES), 1), HD // 2).astype(F32) * (-2.0 * math.log(ROPE_BASE) / HD)
    )
    PT = 128

    def prepare(i, _):
        start = pl.multiple_of(i * PT, PT)
        rows = pl.ds(start, PT)
        seg_row, live_row = aux[0:1, :], aux[1:2, :]
        ii, jj = iota((PT, T), 0) + start, iota((PT, T), 1)
        seg_col = jnp.sum(jnp.where(ii == jj, seg_row, 0.0), axis=1, keepdims=True)
        live_col = jnp.sum(jnp.where(ii == jj, live_row, 0.0), axis=1, keepdims=True)
        same = seg_col == seg_row
        position = jnp.sum(jnp.where(same & (jj < ii), 1.0, 0.0), axis=1, keepdims=True)
        allowed = (same & (jj <= ii) & (live_row > 0.5)) | (ii == jj)
        bias[rows, :] = jnp.where(allowed, 0.0, MASKED).astype(BF16)
        dO[rows, :] = (dO[rows, :].astype(F32) * live_col).astype(BF16)
        lane = iota((PT, LANES), 1)
        angles = position * frequency
        v["cos"][rows, :] = jnp.cos(angles)
        sine = jnp.sin(angles)
        v["sin"][rows, :] = jnp.where(lax.rem(lane, HD) < HD // 2, -sine, sine)
        x = v["tok"][rows, :].astype(F32)
        r1 = lax.rsqrt(jnp.mean(x * x, axis=1, keepdims=True) + EPS)
        stats[rows, :] = jnp.where(lane == 126, r1, jnp.where(lane == 125, live_col, 0.0))
        return 0

    bring_cot.wait()
    lax.fori_loop(0, T // PT // 2, prepare, 0)

    gaA.serve(1)
    gaB.serve(1)
    gsm.serve(1)
    fan_out(-1)
    fan_out(1)

    lax.fori_loop(T // PT // 2, T // PT, prepare, 0)

    for s in range(2, long_way + 1):
        gaA.serve(s)
        gaB.serve(s)
        gsm.serve(s)
        for k in [-s, s] if s < long_way else [s]:
            fan_out(k)
    small_beside.start()
    small_core.start()

    def group_gather(buf):
        return [
            net.copy(buf.at[pl.ds(0, T)], buf.at[pl.ds(2 * T, T)], beside),
            net.copy(buf.at[pl.ds(0, T)], buf.at[pl.ds(T, T)], core),
            net.copy(buf.at[pl.ds(2 * T, T)], buf.at[pl.ds(3 * T, T)], core),
        ]

    gS, gO = group_gather(S), group_gather(dO)
    gO[0].start()
    gO[1].start()

    Wg, Wu, Wd = v["Wg"], v["Wu"], v["Wd"]

    def jslot(k):
        return (k - geo.OFF) % R

    def unit_rows(j):
        return slice(j * FP, (j + 1) * FP)

    def drow(k, lo=0, size=DP):
        return pl.ds(pl.multiple_of(place_group(k) * DP + lo, 16), size)

    def turn(block, forward):
        return pltpu.roll(block.astype(F32), U - FP if forward else FP, 1)

    def box(s, forward):
        return (s % 2) * 2 + (0 if forward else 1)

    def down_gather(cls, buf, lo, size):
        def arrive(k, s):
            Wd[drow(k, lo, size), :] = turn(buf[box(s, k < 0)], k < 0).astype(BF16)

        return Gather(
            cls, lambda k: Wd.at[drow(k, lo, size)], lambda k, s: buf.at[box(s, k < 0)], arrive
        )

    def unit_gather(cls, ref):
        def at(k):
            return ref.at[pl.ds(jslot(k) * FP, FP)]

        return Gather(cls, at, lambda k, s: at(k))

    gDA = down_gather("A", v["bufA"], 0, DA)
    gDB = down_gather("B", v["bufB"], DA, DP - DA)
    gG, gU = unit_gather("A", Wg), unit_gather("B", Wu)
    own = jslot(0)
    for ref, mine in ((Wg, v["gate"]), (Wu, v["up"])):
        if FP > FS:
            ref[unit_rows(own), :] = jnp.zeros((FP, D), BF16)
        ref[own * FP : own * FP + FS, :] = mine[...]
    dx[m] = v["down_p"][m]
    for c in down_copies:
        c.wait_recv()
    for i in range(4):
        tmp[i * DS : (i + 1) * DS, :] = dx[i].astype(F32)[0:DS, :]
    Wd[drow(0), :] = tmp[0:DP, :].astype(BF16)
    gather_steps = []
    for s in range(1, long_way + 1):
        gather_steps += [(gDA, s), (gDB, s)]
    down_steps = len(gather_steps)
    for s in range(1, long_way + 1):
        gather_steps += [(gG, s), (gU, s)]
    gather_done = [0]

    def serve_gather(upto):
        while gather_done[0] < upto:
            x, s = gather_steps[gather_done[0]]
            x.serve(s)
            gather_done[0] += 1

    gDA.begin()
    gDB.begin()
    gG.begin()
    gU.begin()

    for i, k in enumerate(ks):
        to_beside[k].wait_recv()
        on_core[k].start()
        if i == 5:
            serve_gather(2)
    small_beside.wait_recv()
    small_on.start()
    serve_gather(4)
    for c in (small_core, small_on):
        c.wait_recv()
    for k in ks:
        to_core[k].wait_recv()
        on_core[k].wait_recv()

    W = v["W"]
    WQ, WO, WK, WV = 0, D, 2 * D, 2 * D + KV * HD

    def unpack(gi, _):
        for i in range(4):
            at = pl.ds(pl.multiple_of((i * R + gi) * AR, 16), AR)
            block = AW[at, :].astype(F32)
            tmp[i * DS : (i + 1) * DS, 0:D] = block[0:DS]
            v["tmp2"][i * DS : (i + 1) * DS, :] = block[DS : 2 * DS]
            v["tmp3"][i * KS : (i + 1) * KS, :] = block[2 * DS : 2 * DS + KS]
            v["tmp3"][4 * KS + i * KS : 4 * KS + (i + 1) * KS, :] = block[2 * DS + KS : AR]
        W[pl.ds(pl.multiple_of(WQ + gi * DP, 16), DP), 0:D] = tmp[0:DP, 0:D].astype(BF16)
        W[pl.ds(pl.multiple_of(WO + gi * DP, 16), DP), 0:D] = v["tmp2"][...].astype(BF16)
        W[pl.ds(pl.multiple_of(WK + gi * 4 * KS, 16), 4 * KS), 0:D] = v["tmp3"][0 : 4 * KS, :].astype(BF16)
        W[pl.ds(pl.multiple_of(WV + gi * 4 * KS, 16), 4 * KS), 0:D] = v["tmp3"][4 * KS :, :].astype(BF16)
        return 0

    lax.fori_loop(0, R, unpack, 0)

    rows_n = 4 * R * 8
    ST = 64

    def owner_of(lanes, size):
        block = jnp.floor((lanes.astype(F32) + 0.5) * (1.0 / size)).astype(jnp.int32)
        return block, lanes - block * size

    def row_device(start):
        i = lax.div(iota((ST, 1), 0) + start, 8)
        return lax.rem(i, R) * 4 + lax.div(i, R)

    def spread(width, size, offset, stride):
        owner, inner = owner_of(iota((1, width), 1), size)
        pick = (iota((LANES, width), 0) == inner * stride + offset).astype(BF16)

        def tile(i, total):
            start = pl.multiple_of(i * ST, ST)
            full = nn(SM[pl.ds(start, ST), :].astype(BF16), pick)
            full = jnp.where(row_device(start) == owner, full, 0.0)
            return total + jnp.sum(full, axis=0, keepdims=True)

        return lax.fori_loop(0, rows_n // ST, tile, jnp.zeros((1, width), F32))

    vec = v["vec"]
    vec[0:1, :] = spread(D, DS, 0, 1)
    vec[1:2, :] = spread(D, DS, DS, 1)
    vec[2:3, :] = spread(D, DS, 2 * DS, 1)
    vec[3:4, 0:LANES] = spread(LANES, KS, 3 * DS, 2)
    vec[4:5, 0:LANES] = spread(LANES, KS, 3 * DS + 1, 2)

    cosine, sine = v["cos"], v["sin"]
    normed, Q, mixed = v["normed"], v["Q"], v["mixed"]
    KX, VX, res = v["KX"], v["VX"], v["res"]

    def swap_halves(block):
        lanes = iota(block.shape, 1)
        return jnp.where(
            lax.rem(lanes, HD) < HD // 2,
            pltpu.roll(block, LANES - HD // 2, 1),
            pltpu.roll(block, HD // 2, 1),
        )

    def rotate(block, rows):
        return block * cosine[rows, :] + swap_halves(block) * sine[rows, :]

    def rotate_back(block, rows):
        return block * cosine[rows, :] - swap_halves(block) * sine[rows, :]

    HB = T // 2

    def project(i, _):
        rows = pl.ds(pl.multiple_of(i * HB, HB), HB)
        xb = v["tok"][rows, :].astype(F32)
        nb = (xb * stats[rows, 126:127] * vec[0:1, :]).astype(BF16)
        normed[rows, :] = nb
        q = nt(nb, W[WQ : WQ + D, 0:D]) + vec[1:2, :]
        for p in range(PAIRS):
            lanes = slice(p * LANES, (p + 1) * LANES)
            Q[rows, lanes] = rotate(q[:, lanes], rows).astype(BF16)
        key = rotate(nt(nb, W[WK : WK + KV * HD, 0:D]) + vec[3:4, 0:LANES], rows)
        value = nt(nb, W[WV : WV + KV * HD, 0:D]) + vec[4:5, 0:LANES]
        low_half = iota((HB, LANES), 1) < HD
        for ref, full in ((KX, key), (VX, value)):
            other = pltpu.roll(full, HD, 1)
            ref[0, rows, :] = jnp.where(low_half, full, 0.0).astype(BF16)
            ref[1, rows, :] = jnp.where(low_half, 0.0, other).astype(BF16)
            ref[2, rows, :] = jnp.where(low_half, other, 0.0).astype(BF16)
            ref[3, rows, :] = jnp.where(low_half, 0.0, full).astype(BF16)
        return 0

    lax.fori_loop(0, 2, project, 0)
    serve_gather(6)

    def head_index(p, odd):
        h = 2 * p + odd
        return h, lax.div(h, GROUP) * 2 + odd

    def scores(q_pair, idx, rb, cols):
        s = nt(q_pair, KX[idx, 0:cols, :])
        return s * SCALE + bias[rb * HB : (rb + 1) * HB, 0:cols].astype(F32)

    def attend(p, _):
        lanes = pl.ds(pl.multiple_of(p * LANES, LANES), LANES)
        for rb in range(2):
            rows, cols = slice(rb * HB, (rb + 1) * HB), (rb + 1) * HB
            q_pair = Q[rows, lanes]
            total = None
            for odd in range(2):
                h, idx = head_index(p, odd)
                s = scores(q_pair, idx, rb, cols)
                top = jnp.max(s, axis=1, keepdims=True)
                e = jnp.exp(s - top)
                norm = jnp.sum(e, axis=1, keepdims=True)
                low = (e * (1.0 / norm)).astype(BF16)
                part = nn(low, VX[idx, 0:cols, :])
                total = part if total is None else total + part
                lse = top + jnp.log(norm)
                stats[rows, :] = jnp.where(iota((HB, LANES), 1) == h, lse, stats[rows, :])
            mixed[rows, lanes] = total.astype(BF16)
        return 0

    lax.fori_loop(0, PAIRS // 2, attend, 0)
    serve_gather(down_steps)
    lax.fori_loop(PAIRS // 2, PAIRS, attend, 0)

    def close_attention(i, _):
        rows = pl.ds(pl.multiple_of(i * HB, HB), HB)
        out = v["tok"][rows, :].astype(F32) + nt(mixed[rows, :], W[WO : WO + D, 0:D])
        res[rows, :] = out
        r2 = lax.rsqrt(jnp.mean(out * out, axis=1, keepdims=True) + EPS)
        stats[rows, :] = jnp.where(iota((HB, LANES), 1) == 127, r2, stats[rows, :])
        S[rows, :] = (out * r2 * vec[2:3, :]).astype(BF16)
        return 0

    lax.fori_loop(0, 2, close_attention, 0)
    keep_w = net.local(W.at[:, pl.ds(0, D)], v["spill"])
    keep_w.start()
    net.sent(attn_copies)
    gS[0].start()
    gS[1].start()
    gO[0].wait_recv()
    gO[2].start()
    serve_gather(down_steps + 4)
    keep_w.wait()
    for c in (gO[1], gO[2], gS[1]):
        c.wait_recv()

    hid, dg, du = v["hid"], v["dg"], v["du"]
    TT, CT = 512, 256

    def phase_one(lo, hi, first, last):
        across_n = (hi - lo) // CT

        def tile(i, _):
            rows = pl.ds(pl.multiple_of(first + lax.div(i, across_n) * TT, TT), TT)
            cols = pl.ds(pl.multiple_of(lo + lax.rem(i, across_n) * CT, CT), CT)
            s_rows, o_rows = S[rows, :], dO[rows, :]
            gate = nt(s_rows, Wg[cols, :])
            up = nt(s_rows, Wu[cols, :])
            dh = nn(o_rows, Wd[:, cols])
            sg = jax.nn.sigmoid(gate)
            gs = gate * sg
            hid[rows, cols] = (gs * up).astype(BF16)
            du[rows, cols] = (dh * gs).astype(BF16)
            dg[rows, cols] = (dh * up * (sg + gs * (1.0 - sg))).astype(BF16)
            return 0

        lax.fori_loop(0, (last - first) // TT * across_n, tile, 0)

    rG, rU, rD = v["gG"], v["gU"], v["gD"]

    def phase_grads(lo, hi):
        cols = slice(lo, hi)
        for part in parts(lo, hi, 384):
            rG[part, :] = tn(dg[:, part], S[...]).astype(BF16)
            rU[part, :] = tn(du[:, part], S[...]).astype(BF16)
        for part in parts(0, D, 384):
            rD[part, cols] = tn(dO[:, part], hid[:, cols]).astype(BF16)

    phase_one(0, CUT, 0, 2 * T)
    gS[0].wait_recv()
    gS[2].start()
    gS[2].wait_recv()
    phase_one(0, CUT, 2 * T, 4 * T)
    serve_gather(len(gather_steps) - 2)
    phase_grads(0, CUT)
    serve_gather(len(gather_steps))
    phase_one(CUT, U, 0, 4 * T)
    phase_grads(CUT, U)

    class Scatter:
        def __init__(self, cls, at, buf, add):
            self.nf, self.nb = classes[cls]
            self.at, self.buf, self.add = at, buf, add
            nf, nb = self.nf, self.nb
            self.f = [net.copy(at(nf - t + 1), buf.at[box(t, True)], right) for t in range(1, nf + 1)]
            self.b = [net.copy(at(-(nb - t + 1)), buf.at[box(t, False)], left) for t in range(1, nb + 1)]

        def begin(self):
            self.f[0].start()
            self.b[0].start()

        def serve(self, t):
            nf, nb = self.nf, self.nb
            if t <= nf:
                self.f[t - 1].wait_recv()
            if t <= nb:
                self.b[t - 1].wait_recv()
            if t < nf:
                self.add(nf - t, box(t, True), True)
            if t < nb:
                self.add(-(nb - t), box(t, False), False)
            if t < nf:
                self.f[t].start()
            if t < nb:
                self.b[t].start()

        def last(self, value):
            return value(box(self.nf, True), True) + value(box(self.nb, False), False)

    def unit_scatter(cls, grad, buf):
        def at(k):
            return grad.at[pl.ds(jslot(k) * FP, FP)]

        def add(k, slot, forward):
            rows = unit_rows(jslot(k))
            grad[rows, :] = (grad[rows, :].astype(F32) + buf[slot].astype(F32)).astype(BF16)

        return Scatter(cls, at, buf, add)

    def down_scatter(cls, grad, buf, lo, size):
        def add(k, slot, forward):
            rows = drow(k, lo, size)
            grad[rows, :] = (grad[rows, :].astype(F32) + turn(buf[slot], forward)).astype(BF16)

        return Scatter(cls, lambda k: grad.at[drow(k, lo, size)], buf, add)

    sDA = down_scatter("A", rD, v["bufA"], 0, DA)
    sDB = down_scatter("B", rD, v["bufB"], DA, DP - DA)
    sG = unit_scatter("A", rG, v["bufG"])
    sU = unit_scatter("B", rU, v["bufU"])
    scatters = (sDA, sDB, sG, sU)
    for x in scatters:
        x.begin()
    scatter_steps = [(x, t) for t in range(1, long_way + 1) for x in scatters]
    scatter_done = [0]

    def serve_scatter(upto):
        while scatter_done[0] < min(upto, len(scatter_steps)):
            x, t = scatter_steps[scatter_done[0]]
            x.serve(t)
            scatter_done[0] += 1

    def block(ref, i):
        return ref.at[pl.ds(i * T, T)]

    def group_sum(stage_buf, inbox, part, out, between):
        far = net.copy(block(stage_buf, 3), inbox[0], core)
        over = net.copy(block(stage_buf, 2), inbox[1], beside)
        near = net.copy(block(stage_buf, 1), inbox[2], core)
        def fill(q):
            for c in parts(0, D, 512):
                stage_buf[q * T : (q + 1) * T, c] = part(q, c).astype(BF16)

        fill(3)
        far.start()
        fill(2)
        far.wait_recv()
        for c in parts(0, D, 512):
            stage_buf[2 * T : 3 * T, c] = (
                stage_buf[2 * T : 3 * T, c].astype(F32) + inbox[0][:, c].astype(F32)
            ).astype(BF16)
        over.start()
        between()
        fill(1)
        near.start()
        for c in parts(0, D, 512):
            out[:, c] = part(0, c)

        def finish():
            near.wait_recv()
            over.wait_recv()
            out[...] = out[...] + inbox[1][...].astype(F32) + inbox[2][...].astype(F32)
            net.sent([far, over, near])

        return finish

    def ds_part(q, c):
        rows = slice(q * T, (q + 1) * T)
        return nn(dg[rows, :], Wg[:, c]) + nn(du[rows, :], Wu[:, c])

    def y_part(q, c):
        rows = slice(q * T, (q + 1) * T)
        return nt(hid[rows, :], Wd[c, :])

    y_out, ds_out = v["y_out"], v["x_out"]
    net.sent(gS + gO)
    ds_in = [block(AW, 0), block(AW, 1), block(AW, 2)]
    y_in = [
        dg.at[pl.ds(3 * T, T), pl.ds(0, D)],
        block(AW, 3),
        dg.at[pl.ds(0, T), pl.ds(0, D)],
    ]
    finish_ds = group_sum(S, ds_in, ds_part, ds_out, lambda: serve_scatter(1))
    back_w = net.local(v["spill"], W.at[:, pl.ds(0, D)])
    back_w.start()
    serve_scatter(2)
    finish_y = group_sum(dO, y_in, y_part, y_out, lambda: serve_scatter(3))
    back_w.wait()
    finish_ds()
    serve_scatter(4)

    dq_rows = slice(2 * T, 3 * T)
    gains = v["gains"]
    gains[...] = jnp.zeros_like(gains)

    def open_back(i, _):
        rows = pl.ds(pl.multiple_of(i * HB, HB), HB)
        low_rows = pl.ds(pl.multiple_of(T + i * HB, HB), HB)
        r2 = stats[rows, 127:128]
        resid, dsec = res[rows, :], ds_out[rows, :]
        gains[2:3, :] += jnp.sum(dsec * resid * r2, axis=0, keepdims=True)
        scaled = dsec * vec[2:3, :]
        inner = jnp.mean(scaled * resid, axis=1, keepdims=True)
        dres = dO[rows, :].astype(F32) + scaled * r2 - resid * (r2 * r2 * r2 * inner)
        ds_out[rows, :] = dres
        low = dres.astype(BF16)
        hid[low_rows, 0:D] = low
        hid[rows, 0:D] = nn(low, W[WO : WO + D, 0:D]).astype(BF16)
        return 0

    finish_y()
    live_now = stats[:, 125:126]
    y_out[...] = (y_out[...] + res[...]) * live_now
    lax.fori_loop(0, 2, open_back, 0)
    serve_scatter(5)
    wgrad = v["wgrad"]
    for c in parts(0, D, 256):
        wgrad[D : 2 * D, c] = tn(hid[T : 2 * T, 0:D], mixed[:, c]).astype(BF16)
    serve_scatter(6)

    acc = v["acc"]
    res[...] = jnp.zeros_like(res)
    acc[...] = jnp.zeros_like(acc)

    def attend_back(p, _):
        lanes = pl.ds(pl.multiple_of(p * LANES, LANES), LANES)
        for rb in range(2):
            rows, cols = slice(rb * HB, (rb + 1) * HB), (rb + 1) * HB
            q_pair, dm = Q[rows, lanes], hid[rows, lanes]
            total = None
            for odd in range(2):
                h, idx = head_index(p, odd)
                lse = jnp.sum(
                    jnp.where(iota((HB, LANES), 1) == h, stats[rows, :], 0.0), axis=1, keepdims=True
                )
                prob = jnp.exp(scores(q_pair, idx, rb, cols) - lse)
                dp = nt(dm, VX[idx, 0:cols, :])
                t = prob * dp
                delta = jnp.sum(t, axis=1, keepdims=True)
                ds = ((t - prob * delta) * SCALE).astype(BF16)
                acc[idx, 0:cols, :] += tn(prob.astype(BF16), dm)
                k_lanes = pl.ds(pl.multiple_of(idx * LANES, LANES), LANES)
                res[0:cols, k_lanes] += tn(ds, q_pair)
                part = nn(ds, KX[idx, 0:cols, :])
                total = part if total is None else total + part
            hid[2 * T + rb * HB : 2 * T + (rb + 1) * HB, lanes] = rotate_back(total, rows).astype(BF16)
        return 0

    for lo, hi, upto in ((0, 2, 8), (2, 4, 9), (4, 6, 10), (6, 7, 11)):
        lax.fori_loop(lo, hi, attend_back, 0)
        serve_scatter(upto)

    low_half = iota((T, LANES), 1) < HD

    def joined(part):
        return jnp.where(
            low_half, part(0) + pltpu.roll(part(1), HD, 1), pltpu.roll(part(2), HD, 1) + part(3)
        )

    dkv = v["dkv"]
    dkv[:, 0:LANES] = rotate_back(joined(lambda i: res[:, i * LANES : (i + 1) * LANES]), slice(0, T)).astype(BF16)
    dkv[:, LANES : 2 * LANES] = joined(lambda i: acc[i]).astype(BF16)
    for c in parts(0, D, 256):
        wgrad[0:D, c] = tn(hid[dq_rows, 0:D], normed[:, c]).astype(BF16)
        wgrad[2 * D :, c] = tn(dkv[...], normed[:, c]).astype(BF16)
    gains[1:2, :] = jnp.sum(hid[dq_rows, 0:D].astype(F32), axis=0, keepdims=True)
    gains[3:4, 0 : 2 * LANES] = jnp.sum(dkv[...].astype(F32), axis=0, keepdims=True)
    serve_scatter(12)

    def close_back(i, _):
        rows = pl.ds(pl.multiple_of(i * HB, HB), HB)
        dn = nn(hid[pl.ds(pl.multiple_of(2 * T + i * HB, HB), HB), 0:D], W[WQ : WQ + D, 0:D])
        dn += nn(dkv[rows, :], W[WK : WK + 2 * KV * HD, 0:D])
        xb = v["tok"][rows, :].astype(F32)
        r1 = stats[rows, 126:127]
        gains[0:1, :] += jnp.sum(dn * xb * r1, axis=0, keepdims=True)
        scaled = dn * vec[0:1, :]
        inner = jnp.mean(scaled * xb, axis=1, keepdims=True)
        ds_out[rows, :] = ds_out[rows, :] + scaled * r1 - xb * (r1 * r1 * r1 * inner)
        return 0

    def pack(gi, _):
        q_rows = wgrad[pl.ds(pl.multiple_of(gi * DP, 16), DP), :].astype(F32)
        o_rows = wgrad[pl.ds(pl.multiple_of(D + gi * DP, 16), DP), :].astype(F32)
        k_rows = wgrad[pl.ds(pl.multiple_of(2 * D + gi * 4 * KS, 16), 4 * KS), :].astype(F32)
        v_rows = wgrad[pl.ds(pl.multiple_of(2 * D + KV * HD + gi * 4 * KS, 16), 4 * KS), :].astype(F32)
        for i in range(4):
            tmp[0:DS, 0:D] = q_rows[i * DS : (i + 1) * DS]
            tmp[DS : 2 * DS, 0:D] = o_rows[i * DS : (i + 1) * DS]
            tmp[2 * DS : 2 * DS + KS, 0:D] = k_rows[i * KS : (i + 1) * KS]
            tmp[2 * DS + KS : AR, 0:D] = v_rows[i * KS : (i + 1) * KS]
            AW[pl.ds(pl.multiple_of((i * R + gi) * AR, 16), AR), :] = tmp[0:AR, 0:D].astype(BF16)
        return 0

    lax.fori_loop(0, R, pack, 0)
    def inbox_rows(i, k):
        at = pl.multiple_of(T + (i * R + place_group(k)) * AR, 16)
        return pl.ds(at, AR)

    order = [long_way]
    for s in range(long_way - 1, 0, -1):
        order += [s, -s]
    order += [0]
    c_far = {k: net.copy(AW.at[arow(m3, k)], dg.at[inbox_rows(0, k), pl.ds(0, D)], core) for k in order}
    c_near = {k: net.copy(AW.at[arow(m1, k)], dg.at[inbox_rows(1, k), pl.ds(0, D)], core) for k in order}
    c_over = {k: net.copy(AW.at[arow(m2, k)], dg.at[inbox_rows(2, k), pl.ds(0, D)], beside) for k in order}
    for k in order:
        c_far[k].start()
    for k in order:
        c_near[k].start()
    for k in order:
        c_far[k].wait_recv()
        AW[arow(m2, k), :] = (
            AW[arow(m2, k), :].astype(F32) + dg[inbox_rows(0, k), 0:D].astype(F32)
        ).astype(BF16)
        c_over[k].start()
    lax.fori_loop(0, 2, close_back, 0)
    serve_scatter(13)

    SG = v["SG"]
    def collect_tile(i, _):
        start = pl.multiple_of(i * ST, ST)
        first = lax.rem(iota((ST, 1), 0), 8) == 0
        total = None
        for row, width, size, offset, stride in (
            (gains[0:1, :], D, DS, 0, 1),
            (gains[1:2, :], D, DS, DS, 1),
            (gains[2:3, :], D, DS, 2 * DS, 1),
            (gains[3:4, 0:LANES], LANES, KS, 3 * DS, 2),
            (gains[3:4, LANES : 2 * LANES], LANES, KS, 3 * DS + 1, 2),
        ):
            owner, _ = owner_of(iota((1, width), 1), size)
            _, inner = owner_of(iota((width, LANES), 0), size)
            pick = (iota((width, LANES), 1) == inner * stride + offset).astype(BF16)
            full = jnp.where((row_device(start) == owner) & first, row, 0.0)
            high = full.astype(BF16)
            part = nn(high, pick) + nn((full - high.astype(F32)).astype(BF16), pick)
            total = part if total is None else total + part
        SG[pl.ds(start, ST), :] = total
        return 0

    lax.fori_loop(0, rows_n // ST, collect_tile, 0)

    def sg_rows(dev_m):
        return pl.ds(pl.multiple_of(dev_m * R * 8, 8), R * 8)

    sg_in = v["sg_in"]
    s_far = net.copy(SG.at[sg_rows(m3)], sg_in.at[0], core)
    s_near = net.copy(SG.at[sg_rows(m1)], sg_in.at[1], core)
    s_over = net.copy(SG.at[sg_rows(m2)], sg_in.at[2], beside)
    s_far.start()
    s_near.start()
    s_far.wait_recv()
    SG[sg_rows(m2), :] = SG[sg_rows(m2), :] + sg_in[0]
    s_over.start()
    serve_scatter(14)
    s_near.wait_recv()
    s_over.wait_recv()
    SG[sg_rows(m), :] = SG[sg_rows(m), :] + sg_in[1] + sg_in[2]

    aring = v["aring"]

    def attn_scatter(cls, lo, base):
        def add(k, slot, forward):
            rows = arow(m, k, lo, H)
            AW[rows, :] = (AW[rows, :].astype(F32) + aring[base + slot].astype(F32)).astype(BF16)

        return Scatter(cls, lambda k: AW.at[arow(m, k, lo, H)], aring.at[pl.ds(base, 4)], add)

    def small_add(k, slot, forward):
        SG[srow(m, k), :] = SG[srow(m, k), :] + v["sring"][slot]

    saA, saB = attn_scatter("A", 0, 0), attn_scatter("B", H, 4)
    ssm = Scatter("A", lambda k: SG.at[srow(m, k)], v["sring"], small_add)

    def settle(k):
        c_near[k].wait_recv()
        c_over[k].wait_recv()
        AW[arow(m, k), :] = (
            AW[arow(m, k), :].astype(F32)
            + dg[inbox_rows(1, k), 0:D].astype(F32)
            + dg[inbox_rows(2, k), 0:D].astype(F32)
        ).astype(BF16)

    settle(long_way)
    for s in (long_way - 1, -(long_way - 1)):
        settle(s)
    serve_scatter(16)
    for x in (ssm, saA, saB):
        x.begin()
    for t in range(1, long_way + 1):
        if t < long_way:
            k = long_way - t - 1
            for s in (k, -k) if k else (0,):
                settle(s)
        for x in (ssm, saA, saB):
            x.serve(t)
    mine = arow(m, 0)
    low = AW[mine, :].astype(F32)
    v["attn_out"][0:H, :] = low[0:H] + saA.last(lambda i, f: aring[i].astype(F32))
    v["attn_out"][H:AR, :] = low[H:AR] + saB.last(lambda i, f: aring[4 + i].astype(F32))
    v["small_out"][...] = SG[srow(m, 0), :] + ssm.last(lambda i, f: v["sring"][i])

    mine = unit_rows(own)
    v["gate_out"][...] = rG[mine, :].astype(F32) + sG.last(lambda i, f: v["bufG"][i].astype(F32))
    v["up_out"][...] = rU[mine, :].astype(F32) + sU.last(lambda i, f: v["bufU"][i].astype(F32))
    tmp[0:DA, :] = rD[drow(0, 0, DA), :].astype(F32) + sDA.last(lambda i, f: turn(v["bufA"][i], f))
    tmp[DA:DP, :] = rD[drow(0, DA, DP - DA), :].astype(F32) + sDB.last(
        lambda i, f: turn(v["bufB"][i], f)
    )
    down_in = v["down_in"]
    for i in range(4):
        dx[i, 0:DS, :] = tmp[i * DS : (i + 1) * DS, :].astype(BF16)
    home = [
        net.copy(dx.at[dst_m], down_in.at[m], dev)
        for dst_m, dev in ((m1, core), (m2, beside), (m3, across))
    ]
    for c in home:
        c.start()
    down_in[m] = dx[m]
    for c in home:
        c.wait_recv()
    v["down_out"][...] = down_in[...]
    net.sent(net.open)


def layer(geo, ins):
    R, T, D, FP, U, DSP, DP, DA = geo.R, geo.T, geo.D, geo.FP, geo.U, geo.DSP, geo.DP, geo.DA
    AR = geo.AR
    outs = {
        "y_out": ((T, D), F32),
        "x_out": ((T, D), F32),
        "gate_out": ((FP, D), F32),
        "up_out": ((FP, D), F32),
        "down_out": ((4, DSP, U), BF16),
        "attn_out": ((AR, D), F32),
        "small_out": ((8, LANES), F32),
        "spill": ((2 * D + 2 * KV * HD, D), BF16),
    }
    scratch = {
        "dx": ((4, DSP, U), BF16),
        "down_in": ((4, DSP, U), BF16),
        "AW": ((4 * R * AR, D), BF16),
        "SM": ((4 * R * 8, LANES), F32),
        "SG": ((4 * R * 8, LANES), F32),
        "sg_in": ((3, R * 8, LANES), F32),
        "sring": ((4, 8, LANES), F32),
        "aring": ((8, AR // 2, D), BF16),
        "S": ((4 * T, D), BF16),
        "dO": ((4 * T, D), BF16),
        "tmp": ((DP, U), F32),
        "tmp2": ((DP, D), F32),
        "tmp3": ((8 * geo.KS, D), F32),
        "Wg": ((U, D), BF16),
        "Wu": ((U, D), BF16),
        "Wd": ((D, U), BF16),
        "hid": ((4 * T, U), BF16),
        "dg": ((4 * T, U), BF16),
        "du": ((4 * T, U), BF16),
        "gG": ((U, D), BF16),
        "gU": ((U, D), BF16),
        "gD": ((D, U), BF16),
        "bufG": ((4, FP, D), BF16),
        "bufU": ((4, FP, D), BF16),
        "bufA": ((4, DA, U), BF16),
        "bufB": ((4, DP - DA, U), BF16),
        "stats": ((T, LANES), F32),
        "bias": ((T, T), BF16),
        "cos": ((T, LANES), F32),
        "sin": ((T, LANES), F32),
        "vec": ((8, D), F32),
        "gains": ((8, D), F32),
        "normed": ((T, D), BF16),
        "Q": ((T, D), BF16),
        "mixed": ((T, D), BF16),
        "KX": ((4, T, LANES), BF16),
        "VX": ((4, T, LANES), BF16),
        "res": ((T, D), F32),
        "acc": ((4, T, LANES), F32),
        "dkv": ((T, 2 * LANES), BF16),
    }
    alias = {"W": "du"}
    names = list(ins) + list(outs) + list(scratch) + ["send_sems", "recv_sems", "local_sems"]
    vm = pl.BlockSpec(memory_space=pltpu.VMEM)
    hbm = pl.BlockSpec(memory_space=pl.ANY)

    def body(*refs):
        table = dict(zip(names, refs))
        for new, old in alias.items():
            table[new] = table[old]
        table["wgrad"] = table["S"]
        kernel_body(geo, list(table), *table.values())

    res = pl.pallas_call(
        body,
        out_shape=[jax.ShapeDtypeStruct(s, d) for s, d in outs.values()],
        in_specs=[hbm if n == "cot" else vm for n in ins],
        out_specs=[hbm if n == "spill" else vm for n in outs],
        scratch_shapes=[pltpu.VMEM(s, d) for s, d in scratch.values()]
        + [pltpu.SemaphoreType.DMA((64 + 48 * R,))] * 2
        + [pltpu.SemaphoreType.DMA((4,))],
        compiler_params=pltpu.CompilerParams(
            collective_id=0, has_side_effects=True, vmem_limit_bytes=64 * 2**20
        ),
    )(*ins.values())
    return dict(zip(outs, res))


D = 896
eps_norm = 1e-06
rope_base = 1000000.0
masked_value = -1e30


def apply_weight(left, weight):
    return lax.dot_general(
        left, weight, (((1,), (1,)), ((), ())), preferred_element_type=jnp.float32
    )


def apply_transpose(left, weight):
    return jnp.dot(left, weight, preferred_element_type=jnp.float32)


def weight_grad(grad_rows, input_rows):
    return lax.dot_general(
        grad_rows, input_rows, (((0,), (0,)), ((), ())), preferred_element_type=jnp.float32
    )


def rms_scale(field_rows):
    return lax.rsqrt(jnp.mean(field_rows * field_rows, axis=1, keepdims=True) + eps_norm)


def norm_backward(grad_rows, field_rows, scale_rows, gain_values):
    scaled = grad_rows * gain_values
    return scaled * scale_rows - field_rows * scale_rows**3 * jnp.mean(
        scaled * field_rows, axis=1, keepdims=True
    )


def rope_tables(block_segments):
    slot_index = jnp.arange(block_segments.shape[0])
    same_segment = block_segments[:, None] == block_segments[None, :]
    earlier = slot_index[None, :] < slot_index[:, None]
    positions = jnp.sum((same_segment & earlier).astype(jnp.float32), axis=1)
    frequency = jnp.exp(jnp.arange(HD // 2, dtype=jnp.float32) * (-2.0 * math.log(rope_base) / HD))
    angles = positions[:, None] * frequency[None, :]
    return (jnp.cos(angles)[:, None, :], jnp.sin(angles)[:, None, :])


def rotate(vectors, cosine_table, sine_table):
    first_half = vectors[..., : HD // 2]
    second_half = vectors[..., HD // 2 :]
    return jnp.concatenate(
        [
            first_half * cosine_table - second_half * sine_table,
            second_half * cosine_table + first_half * sine_table,
        ],
        axis=-1,
    )


def rotate_back(vectors, cosine_table, sine_table):
    first_half = vectors[..., : HD // 2]
    second_half = vectors[..., HD // 2 :]
    return jnp.concatenate(
        [
            first_half * cosine_table + second_half * sine_table,
            second_half * cosine_table - first_half * sine_table,
        ],
        axis=-1,
    )


def plain_local(
    tokens,
    segment_ids,
    live_counts,
    first_gain,
    query_weight,
    query_bias,
    key_weight,
    value_weight,
    key_value_bias,
    output_weight,
    second_gain,
    gate_weight,
    up_weight,
    down_weight,
    cotangent,
):
    attention_set = (
        lax.all_gather(first_gain, "dp", axis=0, tiled=True),
        lax.all_gather(query_weight, "dp", axis=0, tiled=True),
        lax.all_gather(query_bias, "dp", axis=0, tiled=True),
        lax.all_gather(key_weight, "dp", axis=0, tiled=True),
        lax.all_gather(value_weight, "dp", axis=0, tiled=True),
        lax.all_gather(key_value_bias, "dp", axis=0, tiled=True),
        lax.all_gather(output_weight, "dp", axis=0, tiled=True),
    )
    first_full, query_full, query_bias_full, key_full, value_full, pair_bias_full, output_full = (
        attention_set
    )
    slot_count = tokens.shape[0]
    group_size = HEADS // KV
    scale_factor = HD ** (-0.5)
    slot_index = jnp.arange(slot_count)
    live_rows = (slot_index < live_counts[0]).astype(jnp.float32)
    allowed = (segment_ids[:, None] == segment_ids[None, :]) & (
        slot_index[None, :] <= slot_index[:, None]
    ) & (live_rows[None, :] > 0.5) | (slot_index[None, :] == slot_index[:, None])
    cosine_table, sine_table = rope_tables(segment_ids)
    token_rows = tokens.astype(jnp.float32)
    first_scale = rms_scale(token_rows)
    normed = (token_rows * first_scale * first_full.astype(jnp.float32)).astype(jnp.bfloat16)
    pair_bias_values = pair_bias_full.astype(jnp.float32)
    query_pre = apply_weight(normed, query_full) + query_bias_full.astype(jnp.float32)
    key_pre = apply_weight(normed, key_full) + pair_bias_values[:, 0]
    values = (apply_weight(normed, value_full) + pair_bias_values[:, 1]).astype(jnp.bfloat16)
    values = values.reshape(slot_count, KV, HD)
    rotated_queries = rotate(query_pre.reshape(slot_count, HEADS, HD), cosine_table, sine_table)
    rotated_queries = rotated_queries.astype(jnp.bfloat16).reshape(slot_count, KV, group_size, HD)
    rotated_keys = rotate(key_pre.reshape(slot_count, KV, HD), cosine_table, sine_table).astype(
        jnp.bfloat16
    )

    def attention_logits():
        scores = jnp.einsum(
            "ikgd,jkd->kgij", rotated_queries, rotated_keys, preferred_element_type=jnp.float32
        )
        return jnp.where(allowed[None, None], scores * scale_factor, masked_value)

    logits = attention_logits()
    row_top = jnp.max(logits, axis=-1, keepdims=True)
    exponent = jnp.exp(logits - row_top)
    row_total = jnp.sum(exponent, axis=-1, keepdims=True)
    weights_low = (exponent / row_total).astype(jnp.bfloat16)
    mixed_heads = jnp.einsum(
        "kgij,jkd->ikgd", weights_low, values, preferred_element_type=jnp.float32
    )
    mixed_heads = mixed_heads.reshape(slot_count, D).astype(jnp.bfloat16)
    residual = token_rows + apply_weight(mixed_heads, output_full)
    feed_set = (
        lax.all_gather(second_gain, "dp", axis=0, tiled=True),
        lax.all_gather(gate_weight, "dp", axis=0, tiled=True),
        lax.all_gather(up_weight, "dp", axis=0, tiled=True),
        lax.all_gather(down_weight, "dp", axis=0, tiled=True),
    )
    second_full, gate_full, up_full, down_full = feed_set
    second_scale = rms_scale(residual)
    second = (residual * second_scale * second_full.astype(jnp.float32)).astype(jnp.bfloat16)
    gate_value = apply_weight(second, gate_full)
    up_value = apply_weight(second, up_full)
    hidden = (jax.nn.silu(gate_value) * up_value).astype(jnp.bfloat16)
    layer_out = (residual + apply_weight(hidden, down_full)) * live_rows[:, None]
    feed_back = (
        lax.all_gather(second_gain, "dp", axis=0, tiled=True),
        lax.all_gather(gate_weight, "dp", axis=0, tiled=True),
        lax.all_gather(up_weight, "dp", axis=0, tiled=True),
        lax.all_gather(down_weight, "dp", axis=0, tiled=True),
    )
    back_second, back_gate, back_up, back_down = feed_back
    out_grad = cotangent.astype(jnp.float32) * live_rows[:, None]
    out_grad_low = out_grad.astype(jnp.bfloat16)
    down_shard = lax.psum_scatter(
        weight_grad(out_grad_low, hidden), "dp", scatter_dimension=0, tiled=True
    )
    hidden_grad = apply_transpose(out_grad_low, back_down)
    sigmoid_gate = jax.nn.sigmoid(gate_value)
    up_grad_rows = (hidden_grad * (gate_value * sigmoid_gate)).astype(jnp.bfloat16)
    gate_grad_rows = (
        hidden_grad * up_value * sigmoid_gate * (1.0 + gate_value * (1.0 - sigmoid_gate))
    ).astype(jnp.bfloat16)
    gate_part = weight_grad(gate_grad_rows, second)
    up_part = weight_grad(up_grad_rows, second)
    gate_up_shard = lax.psum_scatter(
        jnp.concatenate([gate_part, up_part], axis=1), "dp", scatter_dimension=0, tiled=True
    )
    model_width = second.shape[1]
    gate_shard = gate_up_shard[:, :model_width]
    up_shard = gate_up_shard[:, model_width:]
    second_grad_rows = apply_transpose(gate_grad_rows, back_gate) + apply_transpose(
        up_grad_rows, back_up
    )
    second_gain_grad = jnp.sum(second_grad_rows * residual * second_scale, axis=0)
    residual_grad = out_grad + norm_backward(
        second_grad_rows, residual, second_scale, back_second.astype(jnp.float32)
    )
    attention_back = (
        lax.all_gather(first_gain, "dp", axis=0, tiled=True),
        lax.all_gather(query_weight, "dp", axis=0, tiled=True),
        lax.all_gather(query_bias, "dp", axis=0, tiled=True),
        lax.all_gather(key_weight, "dp", axis=0, tiled=True),
        lax.all_gather(value_weight, "dp", axis=0, tiled=True),
        lax.all_gather(key_value_bias, "dp", axis=0, tiled=True),
        lax.all_gather(output_weight, "dp", axis=0, tiled=True),
    )
    back_first = attention_back[0]
    back_query = attention_back[1]
    back_key = attention_back[3]
    back_value = attention_back[4]
    back_output = attention_back[6]
    branch_grad = residual_grad.astype(jnp.bfloat16)
    output_grad = weight_grad(branch_grad, mixed_heads)
    mixed_grad = apply_transpose(branch_grad, back_output).astype(jnp.bfloat16)
    mixed_grad = mixed_grad.reshape(slot_count, KV, group_size, HD)
    probs = jnp.exp(attention_logits() - row_top) / row_total
    probs_low = probs.astype(jnp.bfloat16)
    value_grad_rows = jnp.einsum(
        "kgij,ikgd->jkd", probs_low, mixed_grad, preferred_element_type=jnp.float32
    )
    prob_grad = jnp.einsum("ikgd,jkd->kgij", mixed_grad, values, preferred_element_type=jnp.float32)
    logit_grad = probs * (prob_grad - jnp.sum(probs * prob_grad, axis=-1, keepdims=True))
    score_grad = (logit_grad * scale_factor).astype(jnp.bfloat16)
    query_rot_grad = jnp.einsum(
        "kgij,jkd->ikgd", score_grad, rotated_keys, preferred_element_type=jnp.float32
    )
    key_rot_grad = jnp.einsum(
        "kgij,ikgd->jkd", score_grad, rotated_queries, preferred_element_type=jnp.float32
    )
    query_grad_rows = rotate_back(
        query_rot_grad.reshape(slot_count, HEADS, HD), cosine_table, sine_table
    )
    query_grad_rows = query_grad_rows.astype(jnp.bfloat16).reshape(slot_count, D)
    key_grad_rows = (
        rotate_back(key_rot_grad, cosine_table, sine_table)
        .astype(jnp.bfloat16)
        .reshape(slot_count, KV * HD)
    )
    value_grad_low = value_grad_rows.astype(jnp.bfloat16).reshape(slot_count, KV * HD)
    query_grad = weight_grad(query_grad_rows, normed)
    query_bias_grad = jnp.sum(query_grad_rows.astype(jnp.float32), axis=0)
    key_grad = weight_grad(key_grad_rows, normed)
    value_grad = weight_grad(value_grad_low, normed)
    pair_bias_grad = jnp.stack(
        [
            jnp.sum(key_grad_rows.astype(jnp.float32), axis=0),
            jnp.sum(value_grad_low.astype(jnp.float32), axis=0),
        ],
        axis=1,
    )
    first_grad_rows = (
        apply_transpose(query_grad_rows, back_query)
        + apply_transpose(key_grad_rows, back_key)
        + apply_transpose(value_grad_low, back_value)
    )
    first_gain_grad = jnp.sum(first_grad_rows * token_rows * first_scale, axis=0)
    input_grad = residual_grad + norm_backward(
        first_grad_rows, token_rows, first_scale, back_first.astype(jnp.float32)
    )
    attention_shards = (
        lax.psum_scatter(first_gain_grad, "dp", scatter_dimension=0, tiled=True),
        lax.psum_scatter(query_grad, "dp", scatter_dimension=0, tiled=True),
        lax.psum_scatter(query_bias_grad, "dp", scatter_dimension=0, tiled=True),
        lax.psum_scatter(key_grad, "dp", scatter_dimension=0, tiled=True),
        lax.psum_scatter(value_grad, "dp", scatter_dimension=0, tiled=True),
        lax.psum_scatter(pair_bias_grad, "dp", scatter_dimension=0, tiled=True),
        lax.psum_scatter(output_grad, "dp", scatter_dimension=0, tiled=True),
        lax.psum_scatter(second_gain_grad, "dp", scatter_dimension=0, tiled=True),
    )
    return (layer_out, input_grad) + tuple(attention_shards) + (gate_shard, up_shard, down_shard)


def fused_local(
    geo,
    tokens,
    segment_ids,
    live_counts,
    first_gain,
    query_weight,
    query_bias,
    key_weight,
    value_weight,
    key_value_bias,
    output_weight,
    second_gain,
    gate_weight,
    up_weight,
    down_weight,
    cotangent,
):
    R, T, D, DS, DSP, FS, FP, KS = geo.R, geo.T, geo.D, geo.DS, geo.DSP, geo.FS, geo.FP, geo.KS
    place = ring_place(lax.axis_index("dp") // 4, R)
    live = (jnp.arange(T) < live_counts[0]).astype(F32)
    aux = jnp.concatenate(
        [segment_ids.astype(F32)[None], live[None], jnp.zeros((6, T), F32)], axis=0
    )
    vectors = jnp.concatenate(
        [first_gain, query_bias, second_gain, key_value_bias.reshape(-1)]
    ).astype(F32)
    small = jnp.pad(vectors[None], ((0, 7), (0, LANES - vectors.shape[0])))
    x = down_weight.reshape(DS, R, 4, FS)
    x = jnp.concatenate([x[:, 0::2], x[:, 1::2][:, ::-1]], axis=1)
    x = lax.dynamic_slice_in_dim(
        jnp.concatenate([x, x], axis=1), (place + geo.OFF + R) % R, R, axis=1
    )
    x = jnp.pad(x, ((0, DSP - DS), (0, 0), (0, 0), (0, FP - FS)))
    down_p = x.transpose(2, 0, 1, 3).reshape(4, DSP, geo.U)
    res = layer(
        geo,
        {
            "tok": tokens,
            "cot": cotangent,
            "wq": query_weight,
            "wo": output_weight,
            "wk": key_weight,
            "wv": value_weight,
            "gate": gate_weight,
            "up": up_weight,
            "down_p": down_p,
            "small": small,
            "aux": aux,
        },
    )
    x = res["down_out"][:, :DS].reshape(4, DS, R, FP)[..., :FS].transpose(1, 2, 0, 3)
    x = lax.dynamic_slice_in_dim(
        jnp.concatenate([x, x], axis=1), (2 * R - place - geo.OFF) % R, R, axis=1
    )
    x = jnp.stack([x[:, : R // 2], x[:, R // 2 :][:, ::-1]], axis=2)
    down_shard = x.reshape(DS, R * 4 * FS).astype(F32)
    attn, vec = res["attn_out"], res["small_out"][0]
    return (
        res["y_out"],
        res["x_out"],
        vec[:DS],
        attn[:DS],
        vec[DS : 2 * DS],
        attn[2 * DS : 2 * DS + KS],
        attn[2 * DS + KS :],
        vec[3 * DS : 3 * DS + 2 * KS].reshape(KS, 2),
        attn[DS : 2 * DS],
        vec[2 * DS : 3 * DS],
        res["gate_out"][:FS],
        res["up_out"][:FS],
        down_shard,
    )


def local(tokens, segment_ids, live_counts, first_gain, *rest):
    geo = Geometry(
        lax.axis_size("dp"), tokens.shape[0], tokens.shape[1], rest[9].shape[1]
    )
    layer_of = functools.partial(fused_local, geo) if geo.fits() else plain_local
    return layer_of(tokens, segment_ids, live_counts, first_gain, *rest)


def solution(mesh):
    in_specs = (
        P("dp", None),
        P("dp"),
        P("dp"),
        P("dp"),
        P("dp", None),
        P("dp"),
        P("dp", None),
        P("dp", None),
        P("dp", None),
        P("dp", None),
        P("dp"),
        P("dp", None),
        P("dp", None),
        P("dp", None),
        P("dp", None),
    )
    out_specs = (
        P("dp", None),
        P("dp", None),
        P("dp"),
        P("dp", None),
        P("dp"),
        P("dp", None),
        P("dp", None),
        P("dp", None),
        P("dp", None),
        P("dp"),
        P("dp", None),
        P("dp", None),
        P("dp", None),
    )
    return jax.shard_map(local, mesh=mesh, in_specs=in_specs, out_specs=out_specs, check_vma=False)
```

```python
import functools
import math

import jax
import jax.numpy as jnp
from jax import lax
from jax.experimental import pallas as pl
from jax.experimental.pallas import tpu as pltpu
from jax.sharding import PartitionSpec as P

MESH = pl.DeviceIdType.MESH
F32 = jnp.float32
BF16 = jnp.bfloat16

HEADS = 14
KV = 2
HD = 64
GROUP = HEADS // KV
PAIRS = HEADS // 2
LANES = 128
EPS = 1e-06
ROPE_BASE = 1000000.0
MASKED = -1e30
SCALE = HD ** (-0.5)


def up16(n):
    return -(-n // 16) * 16


def nn(a, b):
    return jnp.dot(a, b, preferred_element_type=F32)


def nt(a, b):
    return lax.dot_general(a, b, (((1,), (1,)), ((), ())), preferred_element_type=F32)


def tn(a, b):
    return lax.dot_general(a, b, (((0,), (0,)), ((), ())), preferred_element_type=F32)


class Geometry:
    def __init__(self, devices, slots, width, hidden):
        self.n = devices
        self.R = devices // 4
        self.T = slots
        self.D = width
        self.FS = hidden // devices
        self.FP = up16(self.FS)
        self.U = self.R * self.FP
        self.DS = width // devices
        self.DSP = up16(self.DS)
        self.DP = 4 * self.DS
        self.DA = up16(self.DP // 2)
        self.KS = KV * HD // devices
        self.AR = 2 * self.DS + 2 * self.KS
        self.OFF = -(self.R // 4)
        self.CUT = 3 * self.U // 5 // 256 * 256

    def fits(self):
        return (
            self.n % 32 == 0
            and self.DP % 16 == 0
            and self.AR % 32 == 0
            and (4 * self.KS) % 16 == 0
            and self.U % 256 == 0
            and self.R * self.AR == self.T
            and self.R & (self.R - 1) == 0
            and 2 * self.D + 2 * KV * HD == 4 * self.T
            and 3 * self.DS + 2 * self.KS <= LANES
            and 4 * self.T * self.U * 6 <= 16 * 2**20
        )


def ring_place(g, R):
    odd = lax.rem(g, 2)
    half = lax.div(g, 2)
    return (1 - odd) * half + odd * (R - 1 - half)


def ring_group(place, R):
    high = lax.div(place, R // 2)
    return (1 - high) * (2 * place) + high * (2 * (R - 1 - place) + 1)


class Net:
    def __init__(self, send_sems, recv_sems, local_sems):
        self.send_sems, self.recv_sems, self.local_sems = send_sems, recv_sems, local_sems
        self.count = 0
        self.local_count = 0
        self.open = []

    def copy(self, src, dst, device):
        i = self.count
        self.count += 1
        made = pltpu.make_async_remote_copy(
            src_ref=src,
            dst_ref=dst,
            send_sem=self.send_sems.at[i],
            recv_sem=self.recv_sems.at[i],
            device_id=(device,),
            device_id_type=MESH,
        )
        self.open.append(made)
        return made

    def sent(self, copies):
        for c in copies:
            c.wait_send()
        self.open = [x for x in self.open if all(x is not c for c in copies)]

    def local(self, src, dst):
        i = self.local_count
        self.local_count += 1
        return pltpu.make_async_copy(src, dst, self.local_sems.at[i])


def parts(lo, hi, step):
    return [slice(at, min(at + step, hi)) for at in range(lo, hi, step)]


def iota(shape, axis):
    return lax.broadcasted_iota(jnp.int32, shape, axis)


def kernel_body(geo, names, *refs):
    v = dict(zip(names, refs))
    R, T, D, FP, FS, U = geo.R, geo.T, geo.D, geo.FP, geo.FS, geo.U
    DSP, DS, DP, DA, KS, AR, CUT = geo.DSP, geo.DS, geo.DP, geo.DA, geo.KS, geo.AR, geo.CUT
    H = AR // 2
    me = lax.axis_index("dp")
    m, g = lax.rem(me, 4), lax.div(me, 4)
    r = ring_place(g, R)

    def place_group(k):
        return ring_group(lax.rem(r + k + 2 * R, R), R)

    right = place_group(1) * 4 + m
    left = place_group(-1) * 4 + m
    m1 = m + 1 - 2 * lax.rem(m, 2)
    m2 = m + 2 - 4 * lax.div(m, 2)
    m3 = m1 + 2 - 4 * lax.div(m1, 2)
    core, beside, across = g * 4 + m1, g * 4 + m2, g * 4 + m3
    net = Net(v["send_sems"], v["recv_sems"], v["local_sems"])

    barrier = pltpu.get_barrier_semaphore()
    for peer in (right, left, core, beside, across):
        pl.semaphore_signal(barrier, inc=1, device_id=(peer,), device_id_type=MESH)

    AW, SM = v["AW"], v["SM"]
    tmp = v["tmp"]

    tmp[0:DS, 0:D] = v["wq"][...].astype(F32)
    tmp[DS : 2 * DS, 0:D] = v["wo"][...].astype(F32)
    tmp[2 * DS : 2 * DS + KS, 0:D] = v["wk"][...].astype(F32)
    tmp[2 * DS + KS : AR, 0:D] = v["wv"][...].astype(F32)

    def arow(dev_m, k, lo=0, size=AR):
        return pl.ds(pl.multiple_of((dev_m * R + place_group(k)) * AR + lo, 16), size)

    AW[arow(m, 0), :] = tmp[0:AR, 0:D].astype(BF16)

    seat = lax.rem(r + geo.OFF + R, R)

    def turn_by_seat(block, back):
        b = 1
        while b < R:
            odd = lax.rem(lax.div(seat, b), 2) == 1
            block = jnp.where(odd, pltpu.roll(block, b * FP if back else U - b * FP, 1), block)
            b *= 2
        return block

    def owned_units(place, i):
        half = R // 2
        group = 2 * place if place < half else 2 * (R - 1 - place) + 1
        return slice((4 * group + i) * FS, (4 * group + i + 1) * FS)

    down_p = v["down_p"]
    for i in range(4):
        for place in range(R):
            rows = slice(i * DS, (i + 1) * DS)
            if FP > FS:
                tmp[rows, place * FP + FS : (place + 1) * FP] = jnp.zeros((DS, FP - FS), F32)
            tmp[rows, place * FP : place * FP + FS] = v["down"][:, owned_units(place, i)].astype(F32)
    tmp[...] = turn_by_seat(tmp[...], False)
    for i in range(4):
        down_p[i, 0:DS, :] = tmp[i * DS : (i + 1) * DS, :].astype(BF16)

    def srow(dev_m, k):
        return pl.ds(pl.multiple_of((dev_m * R + place_group(k)) * 8, 8), 8)

    aux = v["aux"]
    SM[srow(m, 0), :] = jnp.where(iota((8, LANES), 0) == 0, aux[2:3, 0:LANES], 0.0)
    pl.semaphore_wait(barrier, 5)

    long_way, short_way = R // 2, R // 2 - 1
    classes = {"A": (long_way, short_way), "B": (short_way, long_way)}

    class Gather:
        def __init__(self, cls, src, dst, arrive=None):
            self.nf, self.nb = classes[cls]
            self.f = [net.copy(src(-(s - 1)), dst(-s, s), right) for s in range(1, self.nf + 1)]
            self.b = [net.copy(src(s - 1), dst(s, s), left) for s in range(1, self.nb + 1)]
            self.arrive = arrive

        def begin(self):
            self.f[0].start()
            self.b[0].start()

        def serve(self, s):
            if s <= self.nf:
                self.f[s - 1].wait_recv()
            if s <= self.nb:
                self.b[s - 1].wait_recv()
            if self.arrive and s <= self.nf:
                self.arrive(-s, s)
            if self.arrive and s <= self.nb:
                self.arrive(s, s)
            if s < self.nf:
                self.f[s].start()
            if s < self.nb:
                self.b[s].start()

    dx = v["dx"]
    down_copies = [
        net.copy(down_p.at[dst_m], dx.at[m], dev)
        for dst_m, dev in ((m1, core), (m2, beside), (m3, across))
    ]

    def nearer(k):
        return k + 1 if k < 0 else k - 1

    def attn_gather(cls, lo):
        def at(k):
            return AW.at[arow(m, k, lo, H)]

        return Gather(cls, at, lambda k, s: at(nearer(k)))

    gaA, gaB = attn_gather("A", 0), attn_gather("B", H)
    gsm = Gather("A", lambda k: SM.at[srow(m, k)], lambda k, s: SM.at[srow(m, nearer(k))])
    ks = [0]
    for s in range(1, long_way + 1):
        ks += [-s, s] if s < long_way else [s]
    to_beside = {k: net.copy(AW.at[arow(m, k)], AW.at[arow(m, k)], beside) for k in ks}
    to_core = {k: net.copy(AW.at[arow(m, k)], AW.at[arow(m, k)], core) for k in ks}
    on_core = {k: net.copy(AW.at[arow(m2, k)], AW.at[arow(m2, k)], core) for k in ks}

    def small_rows(dev_m):
        return SM.at[pl.ds(pl.multiple_of(dev_m * R * 8, 8), R * 8)]

    small_beside = net.copy(small_rows(m), small_rows(m), beside)
    small_core = net.copy(small_rows(m), small_rows(m), core)
    small_on = net.copy(small_rows(m2), small_rows(m2), core)
    attn_copies = gaA.f + gaA.b + gaB.f + gaB.b + gsm.f + gsm.b
    attn_copies += list(to_beside.values()) + list(to_core.values()) + list(on_core.values())
    attn_copies += [small_beside, small_core, small_on]

    gsm.begin()
    gaA.begin()
    gaB.begin()

    def fan_out(k):
        to_beside[k].start()
        to_core[k].start()

    bring_cot = net.local(v["cot"], v["dO"].at[pl.ds(0, T)])
    bring_cot.start()
    fan_out(0)
    for c in down_copies:
        c.start()

    S, dO = v["S"], v["dO"]

    stats, bias = v["stats"], v["bias"]
    frequency = jnp.exp(
        lax.rem(iota((1, LANES), 1), HD // 2).astype(F32) * (-2.0 * math.log(ROPE_BASE) / HD)
    )
    PT = 128

    def prepare(i, _):
        start = pl.multiple_of(i * PT, PT)
        rows = pl.ds(start, PT)
        seg_row, live_row = aux[0:1, :], aux[1:2, :]
        ii, jj = iota((PT, T), 0) + start, iota((PT, T), 1)
        seg_col = jnp.sum(jnp.where(ii == jj, seg_row, 0.0), axis=1, keepdims=True)
        live_col = jnp.sum(jnp.where(ii == jj, live_row, 0.0), axis=1, keepdims=True)
        same = seg_col == seg_row
        position = jnp.sum(jnp.where(same & (jj < ii), 1.0, 0.0), axis=1, keepdims=True)
        allowed = (same & (jj <= ii) & (live_row > 0.5)) | (ii == jj)
        bias[rows, :] = jnp.where(allowed, 0.0, MASKED).astype(BF16)
        dO[rows, :] = (dO[rows, :].astype(F32) * live_col).astype(BF16)
        lane = iota((PT, LANES), 1)
        angles = position * frequency
        v["cos"][rows, :] = jnp.cos(angles)
        sine = jnp.sin(angles)
        v["sin"][rows, :] = jnp.where(lax.rem(lane, HD) < HD // 2, -sine, sine)
        x = v["tok"][rows, :].astype(F32)
        r1 = lax.rsqrt(jnp.mean(x * x, axis=1, keepdims=True) + EPS)
        stats[rows, :] = jnp.where(lane == 126, r1, jnp.where(lane == 125, live_col, 0.0))
        return 0

    bring_cot.wait()
    lax.fori_loop(0, T // PT // 2, prepare, 0)

    gaA.serve(1)
    gaB.serve(1)
    gsm.serve(1)
    fan_out(-1)
    fan_out(1)

    lax.fori_loop(T // PT // 2, T // PT, prepare, 0)

    for s in range(2, long_way + 1):
        gaA.serve(s)
        gaB.serve(s)
        gsm.serve(s)
        for k in [-s, s] if s < long_way else [s]:
            fan_out(k)
    small_beside.start()
    small_core.start()

    def group_gather(buf):
        return [
            net.copy(buf.at[pl.ds(0, T)], buf.at[pl.ds(2 * T, T)], beside),
            net.copy(buf.at[pl.ds(0, T)], buf.at[pl.ds(T, T)], core),
            net.copy(buf.at[pl.ds(2 * T, T)], buf.at[pl.ds(3 * T, T)], core),
        ]

    gS, gO = group_gather(S), group_gather(dO)
    gO[0].start()
    gO[1].start()

    Wg, Wu, Wd = v["Wg"], v["Wu"], v["Wd"]

    def jslot(k):
        return (k - geo.OFF) % R

    def unit_rows(j):
        return slice(j * FP, (j + 1) * FP)

    def drow(k, lo=0, size=DP):
        return pl.ds(pl.multiple_of(place_group(k) * DP + lo, 16), size)

    def turn(block, forward):
        return pltpu.roll(block.astype(F32), U - FP if forward else FP, 1)

    def box(s, forward):
        return (s % 2) * 2 + (0 if forward else 1)

    def down_gather(cls, buf, lo, size):
        def arrive(k, s):
            Wd[drow(k, lo, size), :] = turn(buf[box(s, k < 0)], k < 0).astype(BF16)

        return Gather(
            cls, lambda k: Wd.at[drow(k, lo, size)], lambda k, s: buf.at[box(s, k < 0)], arrive
        )

    def unit_gather(cls, ref):
        def at(k):
            return ref.at[pl.ds(jslot(k) * FP, FP)]

        return Gather(cls, at, lambda k, s: at(k))

    gDA = down_gather("A", v["bufA"], 0, DA)
    gDB = down_gather("B", v["bufB"], DA, DP - DA)
    gG, gU = unit_gather("A", Wg), unit_gather("B", Wu)
    own = jslot(0)
    for ref, mine in ((Wg, v["gate"]), (Wu, v["up"])):
        if FP > FS:
            ref[unit_rows(own), :] = jnp.zeros((FP, D), BF16)
        ref[own * FP : own * FP + FS, :] = mine[...]
    dx[m] = down_p[m]
    for c in down_copies:
        c.wait_recv()
    for i in range(4):
        tmp[i * DS : (i + 1) * DS, :] = dx[i].astype(F32)[0:DS, :]
    Wd[drow(0), :] = tmp[0:DP, :].astype(BF16)
    gather_steps = []
    for s in range(1, long_way + 1):
        gather_steps += [(gDA, s), (gDB, s)]
    down_steps = len(gather_steps)
    for s in range(1, long_way + 1):
        gather_steps += [(gG, s), (gU, s)]
    gather_done = [0]

    def serve_gather(upto):
        while gather_done[0] < upto:
            x, s = gather_steps[gather_done[0]]
            x.serve(s)
            gather_done[0] += 1

    gDA.begin()
    gDB.begin()
    gG.begin()
    gU.begin()

    for i, k in enumerate(ks):
        to_beside[k].wait_recv()
        on_core[k].start()
        if i == 5:
            serve_gather(2)
    small_beside.wait_recv()
    small_on.start()
    serve_gather(4)
    for c in (small_core, small_on):
        c.wait_recv()
    for k in ks:
        to_core[k].wait_recv()
        on_core[k].wait_recv()

    W = v["W"]
    WQ, WO, WK, WV = 0, D, 2 * D, 2 * D + KV * HD

    def unpack(gi, _):
        for i in range(4):
            at = pl.ds(pl.multiple_of((i * R + gi) * AR, 16), AR)
            block = AW[at, :].astype(F32)
            tmp[i * DS : (i + 1) * DS, 0:D] = block[0:DS]
            v["tmp2"][i * DS : (i + 1) * DS, :] = block[DS : 2 * DS]
            v["tmp3"][i * KS : (i + 1) * KS, :] = block[2 * DS : 2 * DS + KS]
            v["tmp3"][4 * KS + i * KS : 4 * KS + (i + 1) * KS, :] = block[2 * DS + KS : AR]
        W[pl.ds(pl.multiple_of(WQ + gi * DP, 16), DP), 0:D] = tmp[0:DP, 0:D].astype(BF16)
        W[pl.ds(pl.multiple_of(WO + gi * DP, 16), DP), 0:D] = v["tmp2"][...].astype(BF16)
        W[pl.ds(pl.multiple_of(WK + gi * 4 * KS, 16), 4 * KS), 0:D] = v["tmp3"][0 : 4 * KS, :].astype(BF16)
        W[pl.ds(pl.multiple_of(WV + gi * 4 * KS, 16), 4 * KS), 0:D] = v["tmp3"][4 * KS :, :].astype(BF16)
        return 0

    lax.fori_loop(0, R, unpack, 0)

    rows_n = 4 * R * 8
    ST = 64

    def owner_of(lanes, size):
        block = jnp.floor((lanes.astype(F32) + 0.5) * (1.0 / size)).astype(jnp.int32)
        return block, lanes - block * size

    def row_device(start):
        i = lax.div(iota((ST, 1), 0) + start, 8)
        return lax.rem(i, R) * 4 + lax.div(i, R)

    def spread(width, size, offset, stride):
        owner, inner = owner_of(iota((1, width), 1), size)
        pick = (iota((LANES, width), 0) == inner * stride + offset).astype(BF16)

        def tile(i, total):
            start = pl.multiple_of(i * ST, ST)
            full = nn(SM[pl.ds(start, ST), :].astype(BF16), pick)
            full = jnp.where(row_device(start) == owner, full, 0.0)
            return total + jnp.sum(full, axis=0, keepdims=True)

        return lax.fori_loop(0, rows_n // ST, tile, jnp.zeros((1, width), F32))

    vec = v["vec"]
    vec[0:1, :] = spread(D, DS, 0, 1)
    vec[1:2, :] = spread(D, DS, DS, 1)
    vec[2:3, :] = spread(D, DS, 2 * DS, 1)
    vec[3:4, 0:LANES] = spread(LANES, KS, 3 * DS, 2)
    vec[4:5, 0:LANES] = spread(LANES, KS, 3 * DS + 1, 2)

    cosine, sine = v["cos"], v["sin"]
    normed, Q, mixed = v["normed"], v["Q"], v["mixed"]
    KX, VX, res = v["KX"], v["VX"], v["res"]

    def swap_halves(block):
        lanes = iota(block.shape, 1)
        return jnp.where(
            lax.rem(lanes, HD) < HD // 2,
            pltpu.roll(block, LANES - HD // 2, 1),
            pltpu.roll(block, HD // 2, 1),
        )

    def rotate(block, rows):
        return block * cosine[rows, :] + swap_halves(block) * sine[rows, :]

    def rotate_back(block, rows):
        return block * cosine[rows, :] - swap_halves(block) * sine[rows, :]

    HB = T // 2

    def project(i, _):
        rows = pl.ds(pl.multiple_of(i * HB, HB), HB)
        xb = v["tok"][rows, :].astype(F32)
        nb = (xb * stats[rows, 126:127] * vec[0:1, :]).astype(BF16)
        normed[rows, :] = nb
        q = nt(nb, W[WQ : WQ + D, 0:D]) + vec[1:2, :]
        for p in range(PAIRS):
            lanes = slice(p * LANES, (p + 1) * LANES)
            Q[rows, lanes] = rotate(q[:, lanes], rows).astype(BF16)
        key = rotate(nt(nb, W[WK : WK + KV * HD, 0:D]) + vec[3:4, 0:LANES], rows)
        value = nt(nb, W[WV : WV + KV * HD, 0:D]) + vec[4:5, 0:LANES]
        low_half = iota((HB, LANES), 1) < HD
        for ref, full in ((KX, key), (VX, value)):
            other = pltpu.roll(full, HD, 1)
            ref[0, rows, :] = jnp.where(low_half, full, 0.0).astype(BF16)
            ref[1, rows, :] = jnp.where(low_half, 0.0, other).astype(BF16)
            ref[2, rows, :] = jnp.where(low_half, other, 0.0).astype(BF16)
            ref[3, rows, :] = jnp.where(low_half, 0.0, full).astype(BF16)
        return 0

    lax.fori_loop(0, 2, project, 0)
    serve_gather(6)

    def head_index(p, odd):
        h = 2 * p + odd
        return h, lax.div(h, GROUP) * 2 + odd

    def scores(q_pair, idx, rb, cols):
        s = nt(q_pair, KX[idx, 0:cols, :])
        return s * SCALE + bias[rb * HB : (rb + 1) * HB, 0:cols].astype(F32)

    def attend(p, _):
        lanes = pl.ds(pl.multiple_of(p * LANES, LANES), LANES)
        for rb in range(2):
            rows, cols = slice(rb * HB, (rb + 1) * HB), (rb + 1) * HB
            q_pair = Q[rows, lanes]
            total = None
            for odd in range(2):
                h, idx = head_index(p, odd)
                s = scores(q_pair, idx, rb, cols)
                top = jnp.max(s, axis=1, keepdims=True)
                e = jnp.exp(s - top)
                norm = jnp.sum(e, axis=1, keepdims=True)
                low = (e * (1.0 / norm)).astype(BF16)
                part = nn(low, VX[idx, 0:cols, :])
                total = part if total is None else total + part
                lse = top + jnp.log(norm)
                stats[rows, :] = jnp.where(iota((HB, LANES), 1) == h, lse, stats[rows, :])
            mixed[rows, lanes] = total.astype(BF16)
        return 0

    lax.fori_loop(0, PAIRS // 2, attend, 0)
    serve_gather(down_steps)
    lax.fori_loop(PAIRS // 2, PAIRS, attend, 0)

    def close_attention(i, _):
        rows = pl.ds(pl.multiple_of(i * HB, HB), HB)
        out = v["tok"][rows, :].astype(F32) + nt(mixed[rows, :], W[WO : WO + D, 0:D])
        res[rows, :] = out
        r2 = lax.rsqrt(jnp.mean(out * out, axis=1, keepdims=True) + EPS)
        stats[rows, :] = jnp.where(iota((HB, LANES), 1) == 127, r2, stats[rows, :])
        S[rows, :] = (out * r2 * vec[2:3, :]).astype(BF16)
        return 0

    lax.fori_loop(0, 2, close_attention, 0)
    keep_w = net.local(W.at[:, pl.ds(0, D)], v["spill"])
    keep_w.start()
    net.sent(attn_copies)
    gS[0].start()
    gS[1].start()
    gO[0].wait_recv()
    gO[2].start()
    serve_gather(down_steps + 4)
    keep_w.wait()
    for c in (gO[1], gO[2], gS[1]):
        c.wait_recv()

    hid, dg, du = v["hid"], v["dg"], v["du"]
    TT, CT = 512, 256

    def phase_one(lo, hi, first, last):
        across_n = (hi - lo) // CT

        def tile(i, _):
            rows = pl.ds(pl.multiple_of(first + lax.div(i, across_n) * TT, TT), TT)
            cols = pl.ds(pl.multiple_of(lo + lax.rem(i, across_n) * CT, CT), CT)
            s_rows, o_rows = S[rows, :], dO[rows, :]
            gate = nt(s_rows, Wg[cols, :])
            up = nt(s_rows, Wu[cols, :])
            dh = nn(o_rows, Wd[:, cols])
            sg = jax.nn.sigmoid(gate)
            gs = gate * sg
            hid[rows, cols] = (gs * up).astype(BF16)
            du[rows, cols] = (dh * gs).astype(BF16)
            dg[rows, cols] = (dh * up * (sg + gs * (1.0 - sg))).astype(BF16)
            return 0

        lax.fori_loop(0, (last - first) // TT * across_n, tile, 0)

    rG, rU, rD = v["gG"], v["gU"], v["gD"]

    def phase_grads(lo, hi):
        cols = slice(lo, hi)
        for part in parts(lo, hi, 384):
            rG[part, :] = tn(dg[:, part], S[...]).astype(BF16)
            rU[part, :] = tn(du[:, part], S[...]).astype(BF16)
        for part in parts(0, D, 384):
            rD[part, cols] = tn(dO[:, part], hid[:, cols]).astype(BF16)

    phase_one(0, CUT, 0, 2 * T)
    gS[0].wait_recv()
    gS[2].start()
    gS[2].wait_recv()
    phase_one(0, CUT, 2 * T, 4 * T)
    serve_gather(len(gather_steps) - 2)
    phase_grads(0, CUT)
    serve_gather(len(gather_steps))
    phase_one(CUT, U, 0, 4 * T)
    phase_grads(CUT, U)

    class Scatter:
        def __init__(self, cls, at, buf, add):
            self.nf, self.nb = classes[cls]
            self.at, self.buf, self.add = at, buf, add
            nf, nb = self.nf, self.nb
            self.f = [net.copy(at(nf - t + 1), buf.at[box(t, True)], right) for t in range(1, nf + 1)]
            self.b = [net.copy(at(-(nb - t + 1)), buf.at[box(t, False)], left) for t in range(1, nb + 1)]

        def begin(self):
            self.f[0].start()
            self.b[0].start()

        def serve(self, t):
            nf, nb = self.nf, self.nb
            if t <= nf:
                self.f[t - 1].wait_recv()
            if t <= nb:
                self.b[t - 1].wait_recv()
            if t < nf:
                self.add(nf - t, box(t, True), True)
            if t < nb:
                self.add(-(nb - t), box(t, False), False)
            if t < nf:
                self.f[t].start()
            if t < nb:
                self.b[t].start()

        def last(self, value):
            return value(box(self.nf, True), True) + value(box(self.nb, False), False)

    def unit_scatter(cls, grad, buf):
        def at(k):
            return grad.at[pl.ds(jslot(k) * FP, FP)]

        def add(k, slot, forward):
            rows = unit_rows(jslot(k))
            grad[rows, :] = (grad[rows, :].astype(F32) + buf[slot].astype(F32)).astype(BF16)

        return Scatter(cls, at, buf, add)

    def down_scatter(cls, grad, buf, lo, size):
        def add(k, slot, forward):
            rows = drow(k, lo, size)
            grad[rows, :] = (grad[rows, :].astype(F32) + turn(buf[slot], forward)).astype(BF16)

        return Scatter(cls, lambda k: grad.at[drow(k, lo, size)], buf, add)

    sDA = down_scatter("A", rD, v["bufA"], 0, DA)
    sDB = down_scatter("B", rD, v["bufB"], DA, DP - DA)
    sG = unit_scatter("A", rG, v["bufG"])
    sU = unit_scatter("B", rU, v["bufU"])
    scatters = (sDA, sDB, sG, sU)
    for x in scatters:
        x.begin()
    scatter_steps = [(x, t) for t in range(1, long_way + 1) for x in scatters]
    scatter_done = [0]

    def serve_scatter(upto):
        while scatter_done[0] < min(upto, len(scatter_steps)):
            x, t = scatter_steps[scatter_done[0]]
            x.serve(t)
            scatter_done[0] += 1

    def block(ref, i):
        return ref.at[pl.ds(i * T, T)]

    def group_sum(stage_buf, inbox, part, out, between):
        far = net.copy(block(stage_buf, 3), inbox[0], core)
        over = net.copy(block(stage_buf, 2), inbox[1], beside)
        near = net.copy(block(stage_buf, 1), inbox[2], core)
        def fill(q):
            for c in parts(0, D, 512):
                stage_buf[q * T : (q + 1) * T, c] = part(q, c).astype(BF16)

        fill(3)
        far.start()
        fill(2)
        far.wait_recv()
        for c in parts(0, D, 512):
            stage_buf[2 * T : 3 * T, c] = (
                stage_buf[2 * T : 3 * T, c].astype(F32) + inbox[0][:, c].astype(F32)
            ).astype(BF16)
        over.start()
        between()
        fill(1)
        near.start()
        for c in parts(0, D, 512):
            out[:, c] = part(0, c)

        def finish():
            near.wait_recv()
            over.wait_recv()
            out[...] = out[...] + inbox[1][...].astype(F32) + inbox[2][...].astype(F32)
            net.sent([far, over, near])

        return finish

    def ds_part(q, c):
        rows = slice(q * T, (q + 1) * T)
        return nn(dg[rows, :], Wg[:, c]) + nn(du[rows, :], Wu[:, c])

    def y_part(q, c):
        rows = slice(q * T, (q + 1) * T)
        return nt(hid[rows, :], Wd[c, :])

    y_out, ds_out = v["y"], v["x"]
    net.sent(gS + gO)
    ds_in = [block(AW, 0), block(AW, 1), block(AW, 2)]
    y_in = [
        dg.at[pl.ds(3 * T, T), pl.ds(0, D)],
        block(AW, 3),
        dg.at[pl.ds(0, T), pl.ds(0, D)],
    ]
    finish_ds = group_sum(S, ds_in, ds_part, ds_out, lambda: serve_scatter(1))
    back_w = net.local(v["spill"], W.at[:, pl.ds(0, D)])
    back_w.start()
    serve_scatter(2)
    finish_y = group_sum(dO, y_in, y_part, y_out, lambda: serve_scatter(3))
    back_w.wait()
    finish_ds()
    serve_scatter(4)

    dq_rows = slice(2 * T, 3 * T)
    gains = v["gains"]
    gains[...] = jnp.zeros_like(gains)

    def open_back(i, _):
        rows = pl.ds(pl.multiple_of(i * HB, HB), HB)
        low_rows = pl.ds(pl.multiple_of(T + i * HB, HB), HB)
        r2 = stats[rows, 127:128]
        resid, dsec = res[rows, :], ds_out[rows, :]
        gains[2:3, :] += jnp.sum(dsec * resid * r2, axis=0, keepdims=True)
        scaled = dsec * vec[2:3, :]
        inner = jnp.mean(scaled * resid, axis=1, keepdims=True)
        dres = dO[rows, :].astype(F32) + scaled * r2 - resid * (r2 * r2 * r2 * inner)
        ds_out[rows, :] = dres
        low = dres.astype(BF16)
        hid[low_rows, 0:D] = low
        hid[rows, 0:D] = nn(low, W[WO : WO + D, 0:D]).astype(BF16)
        return 0

    finish_y()
    live_now = stats[:, 125:126]
    y_out[...] = (y_out[...] + res[...]) * live_now
    keep_y = net.local(y_out, v["y_out"])
    keep_y.start()
    lax.fori_loop(0, 2, open_back, 0)
    serve_scatter(5)
    wgrad = v["wgrad"]
    for c in parts(0, D, 256):
        wgrad[D : 2 * D, c] = tn(hid[T : 2 * T, 0:D], mixed[:, c]).astype(BF16)
    serve_scatter(6)

    acc = v["acc"]
    res[...] = jnp.zeros_like(res)
    acc[...] = jnp.zeros_like(acc)

    def attend_back(p, _):
        lanes = pl.ds(pl.multiple_of(p * LANES, LANES), LANES)
        for rb in range(2):
            rows, cols = slice(rb * HB, (rb + 1) * HB), (rb + 1) * HB
            q_pair, dm = Q[rows, lanes], hid[rows, lanes]
            total = None
            for odd in range(2):
                h, idx = head_index(p, odd)
                lse = jnp.sum(
                    jnp.where(iota((HB, LANES), 1) == h, stats[rows, :], 0.0), axis=1, keepdims=True
                )
                prob = jnp.exp(scores(q_pair, idx, rb, cols) - lse)
                dp = nt(dm, VX[idx, 0:cols, :])
                t = prob * dp
                delta = jnp.sum(t, axis=1, keepdims=True)
                ds = ((t - prob * delta) * SCALE).astype(BF16)
                acc[idx, 0:cols, :] += tn(prob.astype(BF16), dm)
                k_lanes = pl.ds(pl.multiple_of(idx * LANES, LANES), LANES)
                res[0:cols, k_lanes] += tn(ds, q_pair)
                part = nn(ds, KX[idx, 0:cols, :])
                total = part if total is None else total + part
            hid[2 * T + rb * HB : 2 * T + (rb + 1) * HB, lanes] = rotate_back(total, rows).astype(BF16)
        return 0

    for lo, hi, upto in ((0, 2, 8), (2, 4, 9), (4, 6, 10), (6, 7, 11)):
        lax.fori_loop(lo, hi, attend_back, 0)
        serve_scatter(upto)

    low_half = iota((T, LANES), 1) < HD

    def joined(part):
        return jnp.where(
            low_half, part(0) + pltpu.roll(part(1), HD, 1), pltpu.roll(part(2), HD, 1) + part(3)
        )

    dkv = v["dkv"]
    dkv[:, 0:LANES] = rotate_back(joined(lambda i: res[:, i * LANES : (i + 1) * LANES]), slice(0, T)).astype(BF16)
    dkv[:, LANES : 2 * LANES] = joined(lambda i: acc[i]).astype(BF16)
    for c in parts(0, D, 256):
        wgrad[0:D, c] = tn(hid[dq_rows, 0:D], normed[:, c]).astype(BF16)
        wgrad[2 * D :, c] = tn(dkv[...], normed[:, c]).astype(BF16)
    gains[1:2, :] = jnp.sum(hid[dq_rows, 0:D].astype(F32), axis=0, keepdims=True)
    gains[3:4, 0 : 2 * LANES] = jnp.sum(dkv[...].astype(F32), axis=0, keepdims=True)
    serve_scatter(12)

    def close_back(i, _):
        rows = pl.ds(pl.multiple_of(i * HB, HB), HB)
        dn = nn(hid[pl.ds(pl.multiple_of(2 * T + i * HB, HB), HB), 0:D], W[WQ : WQ + D, 0:D])
        dn += nn(dkv[rows, :], W[WK : WK + 2 * KV * HD, 0:D])
        xb = v["tok"][rows, :].astype(F32)
        r1 = stats[rows, 126:127]
        gains[0:1, :] += jnp.sum(dn * xb * r1, axis=0, keepdims=True)
        scaled = dn * vec[0:1, :]
        inner = jnp.mean(scaled * xb, axis=1, keepdims=True)
        ds_out[rows, :] = ds_out[rows, :] + scaled * r1 - xb * (r1 * r1 * r1 * inner)
        return 0

    def pack(gi, _):
        q_rows = wgrad[pl.ds(pl.multiple_of(gi * DP, 16), DP), :].astype(F32)
        o_rows = wgrad[pl.ds(pl.multiple_of(D + gi * DP, 16), DP), :].astype(F32)
        k_rows = wgrad[pl.ds(pl.multiple_of(2 * D + gi * 4 * KS, 16), 4 * KS), :].astype(F32)
        v_rows = wgrad[pl.ds(pl.multiple_of(2 * D + KV * HD + gi * 4 * KS, 16), 4 * KS), :].astype(F32)
        for i in range(4):
            tmp[0:DS, 0:D] = q_rows[i * DS : (i + 1) * DS]
            tmp[DS : 2 * DS, 0:D] = o_rows[i * DS : (i + 1) * DS]
            tmp[2 * DS : 2 * DS + KS, 0:D] = k_rows[i * KS : (i + 1) * KS]
            tmp[2 * DS + KS : AR, 0:D] = v_rows[i * KS : (i + 1) * KS]
            AW[pl.ds(pl.multiple_of((i * R + gi) * AR, 16), AR), :] = tmp[0:AR, 0:D].astype(BF16)
        return 0

    lax.fori_loop(0, R, pack, 0)
    def inbox_rows(i, k):
        at = pl.multiple_of(T + (i * R + place_group(k)) * AR, 16)
        return pl.ds(at, AR)

    order = [long_way]
    for s in range(long_way - 1, 0, -1):
        order += [s, -s]
    order += [0]
    c_far = {k: net.copy(AW.at[arow(m3, k)], dg.at[inbox_rows(0, k), pl.ds(0, D)], core) for k in order}
    c_near = {k: net.copy(AW.at[arow(m1, k)], dg.at[inbox_rows(1, k), pl.ds(0, D)], core) for k in order}
    c_over = {k: net.copy(AW.at[arow(m2, k)], dg.at[inbox_rows(2, k), pl.ds(0, D)], beside) for k in order}
    for k in order:
        c_far[k].start()
    for k in order:
        c_near[k].start()
    for k in order:
        c_far[k].wait_recv()
        AW[arow(m2, k), :] = (
            AW[arow(m2, k), :].astype(F32) + dg[inbox_rows(0, k), 0:D].astype(F32)
        ).astype(BF16)
        c_over[k].start()
    lax.fori_loop(0, 2, close_back, 0)
    keep_x = net.local(ds_out, v["x_out"])
    keep_x.start()
    serve_scatter(13)

    SG = v["SG"]
    def collect_tile(i, _):
        start = pl.multiple_of(i * ST, ST)
        first = lax.rem(iota((ST, 1), 0), 8) == 0
        total = None
        for row, width, size, offset, stride in (
            (gains[0:1, :], D, DS, 0, 1),
            (gains[1:2, :], D, DS, DS, 1),
            (gains[2:3, :], D, DS, 2 * DS, 1),
            (gains[3:4, 0:LANES], LANES, KS, 3 * DS, 2),
            (gains[3:4, LANES : 2 * LANES], LANES, KS, 3 * DS + 1, 2),
        ):
            owner, _ = owner_of(iota((1, width), 1), size)
            _, inner = owner_of(iota((width, LANES), 0), size)
            pick = (iota((width, LANES), 1) == inner * stride + offset).astype(BF16)
            full = jnp.where((row_device(start) == owner) & first, row, 0.0)
            high = full.astype(BF16)
            part = nn(high, pick) + nn((full - high.astype(F32)).astype(BF16), pick)
            total = part if total is None else total + part
        SG[pl.ds(start, ST), :] = total
        return 0

    lax.fori_loop(0, rows_n // ST, collect_tile, 0)

    def sg_rows(dev_m):
        return pl.ds(pl.multiple_of(dev_m * R * 8, 8), R * 8)

    sg_in = v["sg_in"]
    s_far = net.copy(SG.at[sg_rows(m3)], sg_in.at[0], core)
    s_near = net.copy(SG.at[sg_rows(m1)], sg_in.at[1], core)
    s_over = net.copy(SG.at[sg_rows(m2)], sg_in.at[2], beside)
    s_far.start()
    s_near.start()
    s_far.wait_recv()
    SG[sg_rows(m2), :] = SG[sg_rows(m2), :] + sg_in[0]
    s_over.start()
    serve_scatter(14)
    s_near.wait_recv()
    s_over.wait_recv()
    SG[sg_rows(m), :] = SG[sg_rows(m), :] + sg_in[1] + sg_in[2]

    aring = v["aring"]

    def attn_scatter(cls, lo, base):
        def add(k, slot, forward):
            rows = arow(m, k, lo, H)
            AW[rows, :] = (AW[rows, :].astype(F32) + aring[base + slot].astype(F32)).astype(BF16)

        return Scatter(cls, lambda k: AW.at[arow(m, k, lo, H)], aring.at[pl.ds(base, 4)], add)

    def small_add(k, slot, forward):
        SG[srow(m, k), :] = SG[srow(m, k), :] + v["sring"][slot]

    saA, saB = attn_scatter("A", 0, 0), attn_scatter("B", H, 4)
    ssm = Scatter("A", lambda k: SG.at[srow(m, k)], v["sring"], small_add)

    def settle(k):
        c_near[k].wait_recv()
        c_over[k].wait_recv()
        AW[arow(m, k), :] = (
            AW[arow(m, k), :].astype(F32)
            + dg[inbox_rows(1, k), 0:D].astype(F32)
            + dg[inbox_rows(2, k), 0:D].astype(F32)
        ).astype(BF16)

    settle(long_way)
    for s in (long_way - 1, -(long_way - 1)):
        settle(s)
    serve_scatter(16)
    for x in (ssm, saA, saB):
        x.begin()
    for t in range(1, long_way + 1):
        if t < long_way:
            k = long_way - t - 1
            for s in (k, -k) if k else (0,):
                settle(s)
        for x in (ssm, saA, saB):
            x.serve(t)
    mine = arow(m, 0)
    low = AW[mine, :].astype(F32)
    res[0:H, :] = low[0:H] + saA.last(lambda i, f: aring[i].astype(F32))
    res[H:AR, :] = low[H:AR] + saB.last(lambda i, f: aring[4 + i].astype(F32))
    v["small_out"][...] = SG[srow(m, 0), :] + ssm.last(lambda i, f: v["sring"][i])

    mine = unit_rows(own)
    res[AR : AR + FP, :] = rG[mine, :].astype(F32) + sG.last(lambda i, f: v["bufG"][i].astype(F32))
    res[AR + FP : AR + 2 * FP, :] = rU[mine, :].astype(F32) + sU.last(
        lambda i, f: v["bufU"][i].astype(F32)
    )
    keep_rows = net.local(res.at[pl.ds(0, AR + 2 * FP)], v["rows_out"])
    keep_rows.start()
    tmp[0:DA, :] = rD[drow(0, 0, DA), :].astype(F32) + sDA.last(lambda i, f: turn(v["bufA"][i], f))
    tmp[DA:DP, :] = rD[drow(0, DA, DP - DA), :].astype(F32) + sDB.last(
        lambda i, f: turn(v["bufB"][i], f)
    )
    down_in = v["down_in"]
    for i in range(4):
        dx[i, 0:DS, :] = tmp[i * DS : (i + 1) * DS, :].astype(BF16)
    home = [
        net.copy(dx.at[dst_m], down_in.at[m], dev)
        for dst_m, dev in ((m1, core), (m2, beside), (m3, across))
    ]
    for c in home:
        c.start()
    down_in[m] = dx[m]
    for c in home:
        c.wait_recv()
    for i in range(4):
        full = turn_by_seat(down_in[i].astype(F32), True)
        for place in range(R):
            v["down_out"][:, owned_units(place, i)] = full[0:DS, place * FP : place * FP + FS]
    net.sent(net.open)
    for c in (keep_y, keep_x, keep_rows):
        c.wait()


def layer(geo, ins):
    R, T, D, FP, U, DSP, DP, DA = geo.R, geo.T, geo.D, geo.FP, geo.U, geo.DSP, geo.DP, geo.DA
    AR = geo.AR
    outs = {
        "y_out": ((T, D), F32),
        "x_out": ((T, D), F32),
        "rows_out": ((AR + 2 * FP, D), F32),
        "down_out": ((geo.DS, R * 4 * geo.FS), F32),
        "small_out": ((8, LANES), F32),
        "spill": ((2 * D + 2 * KV * HD, D), BF16),
    }
    scratch = {
        "down_p": ((4, DSP, U), BF16),
        "y": ((T, D), F32),
        "x": ((T, D), F32),
        "dx": ((4, DSP, U), BF16),
        "down_in": ((4, DSP, U), BF16),
        "AW": ((4 * R * AR, D), BF16),
        "SM": ((4 * R * 8, LANES), F32),
        "SG": ((4 * R * 8, LANES), F32),
        "sg_in": ((3, R * 8, LANES), F32),
        "sring": ((4, 8, LANES), F32),
        "aring": ((8, AR // 2, D), BF16),
        "S": ((4 * T, D), BF16),
        "dO": ((4 * T, D), BF16),
        "tmp": ((DP, U), F32),
        "tmp2": ((DP, D), F32),
        "tmp3": ((8 * geo.KS, D), F32),
        "Wg": ((U, D), BF16),
        "Wu": ((U, D), BF16),
        "Wd": ((D, U), BF16),
        "hid": ((4 * T, U), BF16),
        "dg": ((4 * T, U), BF16),
        "du": ((4 * T, U), BF16),
        "gG": ((U, D), BF16),
        "gU": ((U, D), BF16),
        "gD": ((D, U), BF16),
        "bufG": ((4, FP, D), BF16),
        "bufU": ((4, FP, D), BF16),
        "bufA": ((4, DA, U), BF16),
        "bufB": ((4, DP - DA, U), BF16),
        "stats": ((T, LANES), F32),
        "bias": ((T, T), BF16),
        "cos": ((T, LANES), F32),
        "sin": ((T, LANES), F32),
        "vec": ((8, D), F32),
        "gains": ((8, D), F32),
        "normed": ((T, D), BF16),
        "Q": ((T, D), BF16),
        "mixed": ((T, D), BF16),
        "KX": ((4, T, LANES), BF16),
        "VX": ((4, T, LANES), BF16),
        "res": ((T, D), F32),
        "acc": ((4, T, LANES), F32),
        "dkv": ((T, 2 * LANES), BF16),
    }
    alias = {"W": "du"}
    names = list(ins) + list(outs) + list(scratch) + ["send_sems", "recv_sems", "local_sems"]
    vm = pl.BlockSpec(memory_space=pltpu.VMEM)
    hbm = pl.BlockSpec(memory_space=pl.ANY)

    def body(*refs):
        table = dict(zip(names, refs))
        for new, old in alias.items():
            table[new] = table[old]
        table["wgrad"] = table["S"]
        kernel_body(geo, list(table), *table.values())

    res = pl.pallas_call(
        body,
        out_shape=[jax.ShapeDtypeStruct(s, d) for s, d in outs.values()],
        in_specs=[hbm if n == "cot" else vm for n in ins],
        out_specs=[vm if n in ("small_out", "down_out") else hbm for n in outs],
        scratch_shapes=[pltpu.VMEM(s, d) for s, d in scratch.values()]
        + [pltpu.SemaphoreType.DMA((20 * R + 10,))] * 2
        + [pltpu.SemaphoreType.DMA((6,))],
        compiler_params=pltpu.CompilerParams(
            collective_id=0, has_side_effects=True, vmem_limit_bytes=64 * 2**20
        ),
    )(*ins.values())
    return dict(zip(outs, res))


D = 896
eps_norm = 1e-06
rope_base = 1000000.0
masked_value = -1e30


def apply_weight(left, weight):
    return lax.dot_general(
        left, weight, (((1,), (1,)), ((), ())), preferred_element_type=jnp.float32
    )


def apply_transpose(left, weight):
    return jnp.dot(left, weight, preferred_element_type=jnp.float32)


def weight_grad(grad_rows, input_rows):
    return lax.dot_general(
        grad_rows, input_rows, (((0,), (0,)), ((), ())), preferred_element_type=jnp.float32
    )


def rms_scale(field_rows):
    return lax.rsqrt(jnp.mean(field_rows * field_rows, axis=1, keepdims=True) + eps_norm)


def norm_backward(grad_rows, field_rows, scale_rows, gain_values):
    scaled = grad_rows * gain_values
    return scaled * scale_rows - field_rows * scale_rows**3 * jnp.mean(
        scaled * field_rows, axis=1, keepdims=True
    )


def rope_tables(block_segments):
    slot_index = jnp.arange(block_segments.shape[0])
    same_segment = block_segments[:, None] == block_segments[None, :]
    earlier = slot_index[None, :] < slot_index[:, None]
    positions = jnp.sum((same_segment & earlier).astype(jnp.float32), axis=1)
    frequency = jnp.exp(jnp.arange(HD // 2, dtype=jnp.float32) * (-2.0 * math.log(rope_base) / HD))
    angles = positions[:, None] * frequency[None, :]
    return (jnp.cos(angles)[:, None, :], jnp.sin(angles)[:, None, :])


def rotate(vectors, cosine_table, sine_table):
    first_half = vectors[..., : HD // 2]
    second_half = vectors[..., HD // 2 :]
    return jnp.concatenate(
        [
            first_half * cosine_table - second_half * sine_table,
            second_half * cosine_table + first_half * sine_table,
        ],
        axis=-1,
    )


def rotate_back(vectors, cosine_table, sine_table):
    first_half = vectors[..., : HD // 2]
    second_half = vectors[..., HD // 2 :]
    return jnp.concatenate(
        [
            first_half * cosine_table + second_half * sine_table,
            second_half * cosine_table - first_half * sine_table,
        ],
        axis=-1,
    )


def plain_local(
    tokens,
    segment_ids,
    live_counts,
    first_gain,
    query_weight,
    query_bias,
    key_weight,
    value_weight,
    key_value_bias,
    output_weight,
    second_gain,
    gate_weight,
    up_weight,
    down_weight,
    cotangent,
):
    attention_set = (
        lax.all_gather(first_gain, "dp", axis=0, tiled=True),
        lax.all_gather(query_weight, "dp", axis=0, tiled=True),
        lax.all_gather(query_bias, "dp", axis=0, tiled=True),
        lax.all_gather(key_weight, "dp", axis=0, tiled=True),
        lax.all_gather(value_weight, "dp", axis=0, tiled=True),
        lax.all_gather(key_value_bias, "dp", axis=0, tiled=True),
        lax.all_gather(output_weight, "dp", axis=0, tiled=True),
    )
    first_full, query_full, query_bias_full, key_full, value_full, pair_bias_full, output_full = (
        attention_set
    )
    slot_count = tokens.shape[0]
    group_size = HEADS // KV
    scale_factor = HD ** (-0.5)
    slot_index = jnp.arange(slot_count)
    live_rows = (slot_index < live_counts[0]).astype(jnp.float32)
    allowed = (segment_ids[:, None] == segment_ids[None, :]) & (
        slot_index[None, :] <= slot_index[:, None]
    ) & (live_rows[None, :] > 0.5) | (slot_index[None, :] == slot_index[:, None])
    cosine_table, sine_table = rope_tables(segment_ids)
    token_rows = tokens.astype(jnp.float32)
    first_scale = rms_scale(token_rows)
    normed = (token_rows * first_scale * first_full.astype(jnp.float32)).astype(jnp.bfloat16)
    pair_bias_values = pair_bias_full.astype(jnp.float32)
    query_pre = apply_weight(normed, query_full) + query_bias_full.astype(jnp.float32)
    key_pre = apply_weight(normed, key_full) + pair_bias_values[:, 0]
    values = (apply_weight(normed, value_full) + pair_bias_values[:, 1]).astype(jnp.bfloat16)
    values = values.reshape(slot_count, KV, HD)
    rotated_queries = rotate(query_pre.reshape(slot_count, HEADS, HD), cosine_table, sine_table)
    rotated_queries = rotated_queries.astype(jnp.bfloat16).reshape(slot_count, KV, group_size, HD)
    rotated_keys = rotate(key_pre.reshape(slot_count, KV, HD), cosine_table, sine_table).astype(
        jnp.bfloat16
    )

    def attention_logits():
        scores = jnp.einsum(
            "ikgd,jkd->kgij", rotated_queries, rotated_keys, preferred_element_type=jnp.float32
        )
        return jnp.where(allowed[None, None], scores * scale_factor, masked_value)

    logits = attention_logits()
    row_top = jnp.max(logits, axis=-1, keepdims=True)
    exponent = jnp.exp(logits - row_top)
    row_total = jnp.sum(exponent, axis=-1, keepdims=True)
    weights_low = (exponent / row_total).astype(jnp.bfloat16)
    mixed_heads = jnp.einsum(
        "kgij,jkd->ikgd", weights_low, values, preferred_element_type=jnp.float32
    )
    mixed_heads = mixed_heads.reshape(slot_count, D).astype(jnp.bfloat16)
    residual = token_rows + apply_weight(mixed_heads, output_full)
    feed_set = (
        lax.all_gather(second_gain, "dp", axis=0, tiled=True),
        lax.all_gather(gate_weight, "dp", axis=0, tiled=True),
        lax.all_gather(up_weight, "dp", axis=0, tiled=True),
        lax.all_gather(down_weight, "dp", axis=0, tiled=True),
    )
    second_full, gate_full, up_full, down_full = feed_set
    second_scale = rms_scale(residual)
    second = (residual * second_scale * second_full.astype(jnp.float32)).astype(jnp.bfloat16)
    gate_value = apply_weight(second, gate_full)
    up_value = apply_weight(second, up_full)
    hidden = (jax.nn.silu(gate_value) * up_value).astype(jnp.bfloat16)
    layer_out = (residual + apply_weight(hidden, down_full)) * live_rows[:, None]
    feed_back = (
        lax.all_gather(second_gain, "dp", axis=0, tiled=True),
        lax.all_gather(gate_weight, "dp", axis=0, tiled=True),
        lax.all_gather(up_weight, "dp", axis=0, tiled=True),
        lax.all_gather(down_weight, "dp", axis=0, tiled=True),
    )
    back_second, back_gate, back_up, back_down = feed_back
    out_grad = cotangent.astype(jnp.float32) * live_rows[:, None]
    out_grad_low = out_grad.astype(jnp.bfloat16)
    down_shard = lax.psum_scatter(
        weight_grad(out_grad_low, hidden), "dp", scatter_dimension=0, tiled=True
    )
    hidden_grad = apply_transpose(out_grad_low, back_down)
    sigmoid_gate = jax.nn.sigmoid(gate_value)
    up_grad_rows = (hidden_grad * (gate_value * sigmoid_gate)).astype(jnp.bfloat16)
    gate_grad_rows = (
        hidden_grad * up_value * sigmoid_gate * (1.0 + gate_value * (1.0 - sigmoid_gate))
    ).astype(jnp.bfloat16)
    gate_part = weight_grad(gate_grad_rows, second)
    up_part = weight_grad(up_grad_rows, second)
    gate_up_shard = lax.psum_scatter(
        jnp.concatenate([gate_part, up_part], axis=1), "dp", scatter_dimension=0, tiled=True
    )
    model_width = second.shape[1]
    gate_shard = gate_up_shard[:, :model_width]
    up_shard = gate_up_shard[:, model_width:]
    second_grad_rows = apply_transpose(gate_grad_rows, back_gate) + apply_transpose(
        up_grad_rows, back_up
    )
    second_gain_grad = jnp.sum(second_grad_rows * residual * second_scale, axis=0)
    residual_grad = out_grad + norm_backward(
        second_grad_rows, residual, second_scale, back_second.astype(jnp.float32)
    )
    attention_back = (
        lax.all_gather(first_gain, "dp", axis=0, tiled=True),
        lax.all_gather(query_weight, "dp", axis=0, tiled=True),
        lax.all_gather(query_bias, "dp", axis=0, tiled=True),
        lax.all_gather(key_weight, "dp", axis=0, tiled=True),
        lax.all_gather(value_weight, "dp", axis=0, tiled=True),
        lax.all_gather(key_value_bias, "dp", axis=0, tiled=True),
        lax.all_gather(output_weight, "dp", axis=0, tiled=True),
    )
    back_first = attention_back[0]
    back_query = attention_back[1]
    back_key = attention_back[3]
    back_value = attention_back[4]
    back_output = attention_back[6]
    branch_grad = residual_grad.astype(jnp.bfloat16)
    output_grad = weight_grad(branch_grad, mixed_heads)
    mixed_grad = apply_transpose(branch_grad, back_output).astype(jnp.bfloat16)
    mixed_grad = mixed_grad.reshape(slot_count, KV, group_size, HD)
    probs = jnp.exp(attention_logits() - row_top) / row_total
    probs_low = probs.astype(jnp.bfloat16)
    value_grad_rows = jnp.einsum(
        "kgij,ikgd->jkd", probs_low, mixed_grad, preferred_element_type=jnp.float32
    )
    prob_grad = jnp.einsum("ikgd,jkd->kgij", mixed_grad, values, preferred_element_type=jnp.float32)
    logit_grad = probs * (prob_grad - jnp.sum(probs * prob_grad, axis=-1, keepdims=True))
    score_grad = (logit_grad * scale_factor).astype(jnp.bfloat16)
    query_rot_grad = jnp.einsum(
        "kgij,jkd->ikgd", score_grad, rotated_keys, preferred_element_type=jnp.float32
    )
    key_rot_grad = jnp.einsum(
        "kgij,ikgd->jkd", score_grad, rotated_queries, preferred_element_type=jnp.float32
    )
    query_grad_rows = rotate_back(
        query_rot_grad.reshape(slot_count, HEADS, HD), cosine_table, sine_table
    )
    query_grad_rows = query_grad_rows.astype(jnp.bfloat16).reshape(slot_count, D)
    key_grad_rows = (
        rotate_back(key_rot_grad, cosine_table, sine_table)
        .astype(jnp.bfloat16)
        .reshape(slot_count, KV * HD)
    )
    value_grad_low = value_grad_rows.astype(jnp.bfloat16).reshape(slot_count, KV * HD)
    query_grad = weight_grad(query_grad_rows, normed)
    query_bias_grad = jnp.sum(query_grad_rows.astype(jnp.float32), axis=0)
    key_grad = weight_grad(key_grad_rows, normed)
    value_grad = weight_grad(value_grad_low, normed)
    pair_bias_grad = jnp.stack(
        [
            jnp.sum(key_grad_rows.astype(jnp.float32), axis=0),
            jnp.sum(value_grad_low.astype(jnp.float32), axis=0),
        ],
        axis=1,
    )
    first_grad_rows = (
        apply_transpose(query_grad_rows, back_query)
        + apply_transpose(key_grad_rows, back_key)
        + apply_transpose(value_grad_low, back_value)
    )
    first_gain_grad = jnp.sum(first_grad_rows * token_rows * first_scale, axis=0)
    input_grad = residual_grad + norm_backward(
        first_grad_rows, token_rows, first_scale, back_first.astype(jnp.float32)
    )
    attention_shards = (
        lax.psum_scatter(first_gain_grad, "dp", scatter_dimension=0, tiled=True),
        lax.psum_scatter(query_grad, "dp", scatter_dimension=0, tiled=True),
        lax.psum_scatter(query_bias_grad, "dp", scatter_dimension=0, tiled=True),
        lax.psum_scatter(key_grad, "dp", scatter_dimension=0, tiled=True),
        lax.psum_scatter(value_grad, "dp", scatter_dimension=0, tiled=True),
        lax.psum_scatter(pair_bias_grad, "dp", scatter_dimension=0, tiled=True),
        lax.psum_scatter(output_grad, "dp", scatter_dimension=0, tiled=True),
        lax.psum_scatter(second_gain_grad, "dp", scatter_dimension=0, tiled=True),
    )
    return (layer_out, input_grad) + tuple(attention_shards) + (gate_shard, up_shard, down_shard)


def fused_local(
    geo,
    tokens,
    segment_ids,
    live_counts,
    first_gain,
    query_weight,
    query_bias,
    key_weight,
    value_weight,
    key_value_bias,
    output_weight,
    second_gain,
    gate_weight,
    up_weight,
    down_weight,
    cotangent,
):
    T, DS, FS, FP, KS = geo.T, geo.DS, geo.FS, geo.FP, geo.KS
    live = (jnp.arange(T) < live_counts[0]).astype(F32)
    vectors = jnp.concatenate(
        [first_gain, query_bias, second_gain, key_value_bias.reshape(-1)]
    ).astype(F32)
    aux = jnp.stack(
        [segment_ids.astype(F32), live, jnp.pad(vectors, (0, T - vectors.shape[0]))]
    )
    aux = jnp.pad(aux, ((0, 5), (0, 0)))
    res = layer(
        geo,
        {
            "tok": tokens,
            "cot": cotangent,
            "wq": query_weight,
            "wo": output_weight,
            "wk": key_weight,
            "wv": value_weight,
            "gate": gate_weight,
            "up": up_weight,
            "down": down_weight,
            "aux": aux,
        },
    )
    rows, vec = res["rows_out"], res["small_out"][0]
    AR = geo.AR
    return (
        res["y_out"],
        res["x_out"],
        vec[:DS],
        rows[:DS],
        vec[DS : 2 * DS],
        rows[2 * DS : 2 * DS + KS],
        rows[2 * DS + KS : AR],
        vec[3 * DS : 3 * DS + 2 * KS].reshape(KS, 2),
        rows[DS : 2 * DS],
        vec[2 * DS : 3 * DS],
        rows[AR : AR + FS],
        rows[AR + FP : AR + FP + FS],
        res["down_out"],
    )


def local(tokens, segment_ids, live_counts, first_gain, *rest):
    geo = Geometry(
        lax.axis_size("dp"), tokens.shape[0], tokens.shape[1], rest[9].shape[1]
    )
    layer_of = functools.partial(fused_local, geo) if geo.fits() else plain_local
    return layer_of(tokens, segment_ids, live_counts, first_gain, *rest)


def solution(mesh):
    in_specs = (
        P("dp", None),
        P("dp"),
        P("dp"),
        P("dp"),
        P("dp", None),
        P("dp"),
        P("dp", None),
        P("dp", None),
        P("dp", None),
        P("dp", None),
        P("dp"),
        P("dp", None),
        P("dp", None),
        P("dp", None),
        P("dp", None),
    )
    out_specs = (
        P("dp", None),
        P("dp", None),
        P("dp"),
        P("dp", None),
        P("dp"),
        P("dp", None),
        P("dp", None),
        P("dp", None),
        P("dp", None),
        P("dp"),
        P("dp", None),
        P("dp", None),
        P("dp", None),
    )
    return jax.shard_map(local, mesh=mesh, in_specs=in_specs, out_specs=out_specs, check_vma=False)
```

```python
import functools
import math

import jax
import jax.numpy as jnp
from jax import lax
from jax.experimental import pallas as pl
from jax.experimental.pallas import tpu as pltpu
from jax.sharding import PartitionSpec as P

MESH = pl.DeviceIdType.MESH
F32 = jnp.float32
BF16 = jnp.bfloat16

HEADS = 14
KV = 2
HD = 64
GROUP = HEADS // KV
PAIRS = HEADS // 2
LANES = 128
EPS = 1e-06
ROPE_BASE = 1000000.0
MASKED = -1e30
SCALE = HD ** (-0.5)


def up16(n):
    return -(-n // 16) * 16


def nn(a, b):
    return jnp.dot(a, b, preferred_element_type=F32)


def nt(a, b):
    return lax.dot_general(a, b, (((1,), (1,)), ((), ())), preferred_element_type=F32)


def tn(a, b):
    return lax.dot_general(a, b, (((0,), (0,)), ((), ())), preferred_element_type=F32)


class Geometry:
    def __init__(self, devices, slots, width, hidden):
        self.n = devices
        self.R = devices // 4
        self.T = slots
        self.D = width
        self.FS = hidden // devices
        self.FP = up16(self.FS)
        self.U = self.R * self.FP
        self.DS = width // devices
        self.DSP = up16(self.DS)
        self.DP = 4 * self.DS
        self.DA = up16(self.DP // 2)
        self.KS = KV * HD // devices
        self.AR = 2 * self.DS + 2 * self.KS
        self.PH = up16(self.DS + 2 * self.KS)
        self.OFF = 1 - self.R // 2

    def fits(self):
        return (
            self.n % 32 == 0
            and self.DP % 16 == 0
            and self.AR % 16 == 0
            and self.FP % 32 == 0
            and self.PH < self.AR
            and (4 * self.KS) % 16 == 0
            and self.U % 256 == 0
            and self.R * self.AR == self.T
            and self.R & (self.R - 1) == 0
            and 2 * self.D + 2 * KV * HD == 4 * self.T
            and 3 * self.DS + 2 * self.KS <= LANES
            and 4 * self.T * self.U * 6 <= 16 * 2**20
        )


def ring_place(g, R):
    odd = lax.rem(g, 2)
    half = lax.div(g, 2)
    return (1 - odd) * half + odd * (R - 1 - half)


def ring_group(place, R):
    high = lax.div(place, R // 2)
    return (1 - high) * (2 * place) + high * (2 * (R - 1 - place) + 1)


class Net:
    def __init__(self, send_sems, recv_sems, local_sems):
        self.send_sems, self.recv_sems, self.local_sems = send_sems, recv_sems, local_sems
        self.count = 0
        self.local_count = 0
        self.open = []

    def copy(self, src, dst, device):
        i = self.count
        self.count += 1
        made = pltpu.make_async_remote_copy(
            src_ref=src,
            dst_ref=dst,
            send_sem=self.send_sems.at[i],
            recv_sem=self.recv_sems.at[i],
            device_id=(device,),
            device_id_type=MESH,
        )
        self.open.append(made)
        return made

    def sent(self, copies):
        for c in copies:
            c.wait_send()
        self.open = [x for x in self.open if all(x is not c for c in copies)]

    def local(self, src, dst):
        i = self.local_count
        self.local_count += 1
        return pltpu.make_async_copy(src, dst, self.local_sems.at[i])


def parts(lo, hi, step):
    return [slice(at, min(at + step, hi)) for at in range(lo, hi, step)]


def iota(shape, axis):
    return lax.broadcasted_iota(jnp.int32, shape, axis)


def kernel_body(geo, names, *refs):
    v = dict(zip(names, refs))
    R, T, D, FP, FS, U = geo.R, geo.T, geo.D, geo.FP, geo.FS, geo.U
    DSP, DS, DP, DA, KS, AR, PH = geo.DSP, geo.DS, geo.DP, geo.DA, geo.KS, geo.AR, geo.PH
    me = lax.axis_index("dp")
    m, g = lax.rem(me, 4), lax.div(me, 4)
    r = ring_place(g, R)

    def place_group(k):
        return ring_group(lax.rem(r + k + 2 * R, R), R)

    right = place_group(1) * 4 + m
    left = place_group(-1) * 4 + m
    m1 = m + 1 - 2 * lax.rem(m, 2)
    m2 = m + 2 - 4 * lax.div(m, 2)
    m3 = m1 + 2 - 4 * lax.div(m1, 2)
    core, beside, across = g * 4 + m1, g * 4 + m2, g * 4 + m3
    net = Net(v["send_sems"], v["recv_sems"], v["local_sems"])

    barrier = pltpu.get_barrier_semaphore()
    for peer in (right, left, core, beside, across):
        pl.semaphore_signal(barrier, inc=1, device_id=(peer,), device_id_type=MESH)

    AW, SM, tmp, aux = v["AW"], v["SM"], v["tmp"], v["aux"]
    S, dO = v["S"], v["dO"]
    Wg, Wu, Wd = v["Wg"], v["Wu"], v["Wd"]
    stats, bias = v["stats"], v["bias"]

    bring_cot = net.local(v["cot"], dO.at[pl.ds(0, T)])
    bring_cot.start()

    KO, VO, OO = DS, DS + KS, DS + 2 * KS
    tmp[0:DS, 0:D] = v["wq"][...].astype(F32)
    tmp[KO:VO, 0:D] = v["wk"][...].astype(F32)
    tmp[VO:OO, 0:D] = v["wv"][...].astype(F32)
    tmp[OO:AR, 0:D] = v["wo"][...].astype(F32)

    def arow(dev_m, k, lo=0, size=AR):
        return pl.ds(pl.multiple_of((dev_m * R + place_group(k)) * AR + lo, 16), size)

    AW[arow(m, 0), :] = tmp[0:AR, 0:D].astype(BF16)

    def srow(dev_m, k):
        return pl.ds(pl.multiple_of((dev_m * R + place_group(k)) * 8, 8), 8)

    SM[srow(m, 0), :] = jnp.where(iota((8, LANES), 0) == 0, aux[2:3, 0:LANES], 0.0)

    def jslot(k):
        return (k - geo.OFF) % R

    def unit_rows(j):
        return slice(j * FP, (j + 1) * FP)

    own = jslot(0)
    for ref, mine in ((Wg, v["gate"]), (Wu, v["up"])):
        if FP > FS:
            ref[unit_rows(own), :] = jnp.zeros((FP, D), BF16)
        ref[own * FP : own * FP + FS, :] = mine[...]

    pl.semaphore_wait(barrier, 5)

    long_way, short_way = R // 2, R // 2 - 1
    classes = {"A": (long_way, short_way), "B": (short_way, long_way)}

    class Gather:
        def __init__(self, cls, src, dst, arrive=None):
            self.nf, self.nb = classes[cls]
            self.f = [net.copy(src(-(s - 1)), dst(-s, s), right) for s in range(1, self.nf + 1)]
            self.b = [net.copy(src(s - 1), dst(s, s), left) for s in range(1, self.nb + 1)]
            self.arrive = arrive

        def begin(self):
            self.f[0].start()
            self.b[0].start()

        def serve(self, s):
            if s <= self.nf:
                self.f[s - 1].wait_recv()
            if s <= self.nb:
                self.b[s - 1].wait_recv()
            if self.arrive and s <= self.nf:
                self.arrive(-s, s)
            if self.arrive and s <= self.nb:
                self.arrive(s, s)
            if s < self.nf:
                self.f[s].start()
            if s < self.nb:
                self.b[s].start()

    def nearer(k):
        return k + 1 if k < 0 else k - 1

    class Fan:
        def __init__(self, cls, lo, size):
            def at(dev_m, k):
                return AW.at[arow(dev_m, k, lo, size)]

            self.ring = Gather(cls, lambda k: at(m, k), lambda k, s: at(m, nearer(k)))
            self.beside = {k: net.copy(at(m, k), at(m, k), beside) for k in ks}
            self.core = {k: net.copy(at(m, k), at(m, k), core) for k in ks}
            self.on = {k: net.copy(at(m2, k), at(m2, k), core) for k in ks}

        def out(self, k):
            self.beside[k].start()
            self.core[k].start()

        def forward(self, k):
            self.beside[k].wait_recv()
            self.on[k].start()

        def arrived(self):
            for k in ks:
                self.core[k].wait_recv()
                self.on[k].wait_recv()

        def copies(self):
            within = [c for d in (self.beside, self.core, self.on) for c in d.values()]
            return self.ring.f + self.ring.b + within

    def both(s):
        return [-s, s] if s < long_way else [s]

    ks = [0] + [k for s in range(1, long_way + 1) for k in both(s)]
    fan_p, fan_o = Fan("A", 0, PH), Fan("B", PH, AR - PH)
    gsm = Gather("A", lambda k: SM.at[srow(m, k)], lambda k, s: SM.at[srow(m, nearer(k))])

    def small_rows(dev_m):
        return SM.at[pl.ds(pl.multiple_of(dev_m * R * 8, 8), R * 8)]

    small_beside = net.copy(small_rows(m), small_rows(m), beside)
    small_core = net.copy(small_rows(m), small_rows(m), core)
    small_on = net.copy(small_rows(m2), small_rows(m2), core)
    attn_copies = fan_p.copies() + fan_o.copies() + gsm.f + gsm.b
    attn_copies += [small_beside, small_core, small_on]

    def drow(k, lo=0, size=DP):
        return pl.ds(pl.multiple_of(place_group(k) * DP + lo, 16), size)

    def turn(block, forward):
        return pltpu.roll(block.astype(F32), U - FP if forward else FP, 1)

    def box(s, forward):
        return (s % 2) * 2 + (0 if forward else 1)

    def down_gather(cls, buf, lo, size):
        def arrive(k, s):
            Wd[drow(k, lo, size), :] = turn(buf[box(s, k < 0)], k < 0).astype(BF16)

        return Gather(
            cls, lambda k: Wd.at[drow(k, lo, size)], lambda k, s: buf.at[box(s, k < 0)], arrive
        )

    def unit_gather(cls, ref, lo):
        def at(k):
            return ref.at[pl.ds(jslot(k) * FP + lo, FP // 2)]

        return Gather(cls, at, lambda k, s: at(k))

    gDA = down_gather("A", v["bufA"], 0, DA)
    gDB = down_gather("B", v["bufB"], DA, DP - DA)
    unit_pieces = [
        unit_gather("A", Wg, 0),
        unit_gather("B", Wg, FP // 2),
        unit_gather("A", Wu, 0),
        unit_gather("B", Wu, FP // 2),
    ]

    def serve_units(s):
        for x in unit_pieces:
            x.serve(s)

    def serve_down(s):
        gDA.serve(s)
        gDB.serve(s)

    def serve_attention(s):
        fan_p.ring.serve(s)
        fan_o.ring.serve(s)
        gsm.serve(s)

    fan_p.ring.begin()
    fan_o.ring.begin()
    gsm.begin()
    fan_p.out(0)
    unit_pieces[0].begin()

    seat = lax.rem(r + geo.OFF + R, R)

    def turn_by_seat(block, back):
        b = 1
        while b < R:
            odd = lax.rem(lax.div(seat, b), 2) == 1
            block = jnp.where(odd, pltpu.roll(block, b * FP if back else U - b * FP, 1), block)
            b *= 2
        return block

    def owned_units(place, i):
        half = R // 2
        group = 2 * place if place < half else 2 * (R - 1 - place) + 1
        return slice((4 * group + i) * FS, (4 * group + i + 1) * FS)

    down_p, dx = v["down_p"], v["dx"]
    for i in range(4):
        for place in range(R):
            rows = slice(i * DS, (i + 1) * DS)
            if FP > FS:
                tmp[rows, place * FP + FS : (place + 1) * FP] = jnp.zeros((DS, FP - FS), F32)
            tmp[rows, place * FP : place * FP + FS] = v["down"][:, owned_units(place, i)].astype(F32)
    tmp[...] = turn_by_seat(tmp[...], False)
    for i in range(4):
        down_p[i, 0:DS, :] = tmp[i * DS : (i + 1) * DS, :].astype(BF16)
    down_copies = [
        net.copy(down_p.at[dst_m], dx.at[m], dev)
        for dst_m, dev in ((m1, core), (m2, beside), (m3, across))
    ]
    for c in down_copies:
        c.start()

    frequency = jnp.exp(
        lax.rem(iota((1, LANES), 1), HD // 2).astype(F32) * (-2.0 * math.log(ROPE_BASE) / HD)
    )
    PT = 128

    def prepare(i, _):
        start = pl.multiple_of(i * PT, PT)
        rows = pl.ds(start, PT)
        seg_row, live_row = aux[0:1, :], aux[1:2, :]
        ii, jj = iota((PT, T), 0) + start, iota((PT, T), 1)
        seg_col = jnp.sum(jnp.where(ii == jj, seg_row, 0.0), axis=1, keepdims=True)
        live_col = jnp.sum(jnp.where(ii == jj, live_row, 0.0), axis=1, keepdims=True)
        same = seg_col == seg_row
        position = jnp.sum(jnp.where(same & (jj < ii), 1.0, 0.0), axis=1, keepdims=True)
        allowed = (same & (jj <= ii) & (live_row > 0.5)) | (ii == jj)
        bias[rows, :] = jnp.where(allowed, 0.0, MASKED).astype(BF16)
        dO[rows, :] = (dO[rows, :].astype(F32) * live_col).astype(BF16)
        lane = iota((PT, LANES), 1)
        angles = position * frequency
        v["cos"][rows, :] = jnp.cos(angles)
        sine = jnp.sin(angles)
        v["sin"][rows, :] = jnp.where(lax.rem(lane, HD) < HD // 2, -sine, sine)
        x = v["tok"][rows, :].astype(F32)
        r1 = lax.rsqrt(jnp.mean(x * x, axis=1, keepdims=True) + EPS)
        stats[rows, :] = jnp.where(lane == 126, r1, jnp.where(lane == 125, live_col, 0.0))
        return 0

    bring_cot.wait()
    serve_attention(1)
    for k in both(1):
        fan_p.out(k)
    unit_pieces[1].begin()
    lax.fori_loop(0, T // PT // 2, prepare, 0)
    fan_p.forward(0)
    for s in range(2, long_way + 1):
        serve_attention(s)
        for k in both(s):
            fan_p.out(k)
        if s == 2:
            unit_pieces[2].begin()
            lax.fori_loop(T // PT // 2, T // PT, prepare, 0)
        if s == 3:
            unit_pieces[3].begin()
            dx[m] = down_p[m]
            for c in down_copies:
                c.wait_recv()
            for i in range(4):
                tmp[i * DS : (i + 1) * DS, :] = dx[i].astype(F32)[0:DS, :]
            Wd[drow(0), :] = tmp[0:DP, :].astype(BF16)
            net.sent(down_copies)
        for k in both(s - 1):
            fan_p.forward(k)
    gDA.begin()
    gDB.begin()

    PX = T // 2

    class GroupGather:
        def __init__(self, buf):
            def at(q, i):
                return buf.at[pl.ds(q * T + i * PX, PX)]

            self.beside = [net.copy(at(0, i), at(2, i), beside) for i in range(2)]
            self.core = [net.copy(at(0, i), at(1, i), core) for i in range(2)]
            self.on = [net.copy(at(2, i), at(3, i), core) for i in range(2)]

        def out(self, i):
            self.beside[i].start()
            self.core[i].start()

        def forward(self):
            for i in range(2):
                self.beside[i].wait_recv()
                self.on[i].start()

        def copies(self):
            return self.beside + self.core + self.on

    gS, gO = GroupGather(S), GroupGather(dO)
    small_beside.start()
    small_core.start()
    for k in ks:
        fan_o.out(k)
    gO.out(0)
    gO.out(1)
    for k in both(long_way):
        fan_p.forward(k)
    small_beside.wait_recv()
    small_on.start()
    fan_p.arrived()
    small_core.wait_recv()
    small_on.wait_recv()

    W, tmp3 = v["W"], v["tmp3"]
    WQ, WO, WK, WV = 0, D, 2 * D, 2 * D + KV * HD
    K4 = 4 * KS

    def unpack_first(gi, _):
        for i in range(4):
            at = pl.ds(pl.multiple_of((i * R + gi) * AR, 16), PH)
            rows = AW[at, :].astype(F32)
            tmp[i * DS : (i + 1) * DS, 0:D] = rows[0:DS]
            tmp3[i * KS : (i + 1) * KS, :] = rows[KO:VO]
            tmp3[K4 + i * KS : K4 + (i + 1) * KS, :] = rows[VO:OO]
        W[pl.ds(pl.multiple_of(WQ + gi * DP, 16), DP), 0:D] = tmp[0:DP, 0:D].astype(BF16)
        W[pl.ds(pl.multiple_of(WK + gi * K4, 16), K4), 0:D] = tmp3[0:K4, :].astype(BF16)
        W[pl.ds(pl.multiple_of(WV + gi * K4, 16), K4), 0:D] = tmp3[K4:, :].astype(BF16)
        return 0

    OB = OO // 16 * 16

    def unpack_output(gi, _):
        for i in range(4):
            at = pl.ds(pl.multiple_of((i * R + gi) * AR + OB, 16), AR - OB)
            tmp[i * DS : (i + 1) * DS, 0:D] = AW[at, :].astype(F32)[OO - OB : AR - OB]
        W[pl.ds(pl.multiple_of(WO + gi * DP, 16), DP), 0:D] = tmp[0:DP, 0:D].astype(BF16)
        return 0

    lax.fori_loop(0, R, unpack_first, 0)

    rows_n = 4 * R * 8
    ST = 64

    def owner_of(lanes, size):
        block = jnp.floor((lanes.astype(F32) + 0.5) * (1.0 / size)).astype(jnp.int32)
        return block, lanes - block * size

    def row_device(start):
        i = lax.div(iota((ST, 1), 0) + start, 8)
        return lax.rem(i, R) * 4 + lax.div(i, R)

    def spread(width, size, offset, stride):
        owner, inner = owner_of(iota((1, width), 1), size)
        pick = (iota((LANES, width), 0) == inner * stride + offset).astype(BF16)

        def tile(i, total):
            start = pl.multiple_of(i * ST, ST)
            full = nn(SM[pl.ds(start, ST), :].astype(BF16), pick)
            full = jnp.where(row_device(start) == owner, full, 0.0)
            return total + jnp.sum(full, axis=0, keepdims=True)

        return lax.fori_loop(0, rows_n // ST, tile, jnp.zeros((1, width), F32))

    vec = v["vec"]
    vec[0:1, :] = spread(D, DS, 0, 1)
    vec[1:2, :] = spread(D, DS, DS, 1)
    vec[2:3, :] = spread(D, DS, 2 * DS, 1)
    vec[3:4, 0:LANES] = spread(LANES, KS, 3 * DS, 2)
    vec[4:5, 0:LANES] = spread(LANES, KS, 3 * DS + 1, 2)

    cosine, sine = v["cos"], v["sin"]
    normed, Q, mixed = v["normed"], v["Q"], v["mixed"]
    KX, VX, res = v["KX"], v["VX"], v["res"]

    def swap_halves(block):
        lanes = iota(block.shape, 1)
        return jnp.where(
            lax.rem(lanes, HD) < HD // 2,
            pltpu.roll(block, LANES - HD // 2, 1),
            pltpu.roll(block, HD // 2, 1),
        )

    def rotate(block, rows):
        return block * cosine[rows, :] + swap_halves(block) * sine[rows, :]

    def rotate_back(block, rows):
        return block * cosine[rows, :] - swap_halves(block) * sine[rows, :]

    HB = T // 2

    def project(i, _):
        rows = pl.ds(pl.multiple_of(i * HB, HB), HB)
        xb = v["tok"][rows, :].astype(F32)
        nb = (xb * stats[rows, 126:127] * vec[0:1, :]).astype(BF16)
        normed[rows, :] = nb
        q = nt(nb, W[WQ : WQ + D, 0:D]) + vec[1:2, :]
        for p in range(PAIRS):
            lanes = slice(p * LANES, (p + 1) * LANES)
            Q[rows, lanes] = rotate(q[:, lanes], rows).astype(BF16)
        key = rotate(nt(nb, W[WK : WK + KV * HD, 0:D]) + vec[3:4, 0:LANES], rows)
        value = nt(nb, W[WV : WV + KV * HD, 0:D]) + vec[4:5, 0:LANES]
        low_half = iota((HB, LANES), 1) < HD
        for ref, full in ((KX, key), (VX, value)):
            other = pltpu.roll(full, HD, 1)
            ref[0, rows, :] = jnp.where(low_half, full, 0.0).astype(BF16)
            ref[1, rows, :] = jnp.where(low_half, 0.0, other).astype(BF16)
            ref[2, rows, :] = jnp.where(low_half, other, 0.0).astype(BF16)
            ref[3, rows, :] = jnp.where(low_half, 0.0, full).astype(BF16)
        return 0

    lax.fori_loop(0, 2, project, 0)
    serve_down(1)
    for k in ks:
        fan_o.forward(k)

    def head_index(p, odd):
        h = 2 * p + odd
        return h, lax.div(h, GROUP) * 2 + odd

    def scores(q_pair, idx, rb, cols):
        s = nt(q_pair, KX[idx, 0:cols, :])
        return s * SCALE + bias[rb * HB : (rb + 1) * HB, 0:cols].astype(F32)

    def attend(p, _):
        lanes = pl.ds(pl.multiple_of(p * LANES, LANES), LANES)
        for rb in range(2):
            rows, cols = slice(rb * HB, (rb + 1) * HB), (rb + 1) * HB
            q_pair = Q[rows, lanes]
            total = None
            for odd in range(2):
                h, idx = head_index(p, odd)
                s = scores(q_pair, idx, rb, cols)
                top = jnp.max(s, axis=1, keepdims=True)
                e = jnp.exp(s - top)
                norm = jnp.sum(e, axis=1, keepdims=True)
                low = (e * (1.0 / norm)).astype(BF16)
                part = nn(low, VX[idx, 0:cols, :])
                total = part if total is None else total + part
                lse = top + jnp.log(norm)
                stats[rows, :] = jnp.where(iota((HB, LANES), 1) == h, lse, stats[rows, :])
            mixed[rows, lanes] = total.astype(BF16)
        return 0

    lax.fori_loop(0, PAIRS // 2, attend, 0)
    serve_down(2)
    lax.fori_loop(PAIRS // 2, PAIRS, attend, 0)
    fan_o.arrived()
    lax.fori_loop(0, R, unpack_output, 0)
    net.sent(attn_copies)

    for i in range(2):
        rows = slice(i * HB, (i + 1) * HB)
        out = v["tok"][rows, :].astype(F32) + nt(mixed[rows, :], W[WO : WO + D, 0:D])
        res[rows, 0:D] = out
        r2 = lax.rsqrt(jnp.mean(out * out, axis=1, keepdims=True) + EPS)
        stats[rows, :] = jnp.where(iota((HB, LANES), 1) == 127, r2, stats[rows, :])
        S[rows, :] = (out * r2 * vec[2:3, :]).astype(BF16)
        gS.out(i)
    keep_w = net.local(W.at[:, pl.ds(0, D)], v["spill"])
    keep_w.start()
    serve_down(3)
    serve_units(1)
    gO.forward()
    serve_down(4)
    for d in range(5, long_way + 1):
        serve_down(d)
    keep_w.wait()
    for c in gO.core + gO.on + gS.core:
        c.wait_recv()

    hid, dg, du = v["hid"], v["dg"], v["du"]
    TT, CT = 512, 256

    def unit_tile(first, stride, i):
        return pl.ds(pl.multiple_of((first + stride * i) * CT, CT), CT)

    def phase_one(first, stride, count, lo, hi):
        down_n = (hi - lo) // TT

        def tile(i, _):
            rows = pl.ds(pl.multiple_of(lo + lax.rem(i, down_n) * TT, TT), TT)
            cols = unit_tile(first, stride, lax.div(i, down_n))
            s_rows, o_rows = S[rows, :], dO[rows, :]
            gate = nt(s_rows, Wg[cols, :])
            up = nt(s_rows, Wu[cols, :])
            dh = nn(o_rows, Wd[:, cols])
            sg = jax.nn.sigmoid(gate)
            gs = gate * sg
            hid[rows, cols] = (gs * up).astype(BF16)
            du[rows, cols] = (dh * gs).astype(BF16)
            dg[rows, cols] = (dh * up * (sg + gs * (1.0 - sg))).astype(BF16)
            return 0

        lax.fori_loop(0, count * down_n, tile, 0)

    rG, rU, rD = v["gG"], v["gU"], v["gD"]

    def unit_grads(first, stride, count):
        def tile(i, _):
            cols = unit_tile(first, stride, i)
            rG[cols, :] = tn(dg[:, cols], S[...]).astype(BF16)
            rU[cols, :] = tn(du[:, cols], S[...]).astype(BF16)
            return 0

        lax.fori_loop(0, count, tile, 0)

    def need(t):
        return max(abs(j + geo.OFF) for j in range(t * CT // FP, ((t + 1) * CT - 1) // FP + 1))

    tiles = sorted(range(U // CT), key=need)
    runs = []
    for t in tiles:
        if runs and runs[-1][3] == need(t):
            first, stride, count, step = runs[-1]
            if count == 1 or t - first == stride * count:
                runs[-1] = (first, t - first if count == 1 else stride, count + 1, step)
                continue
        runs.append((t, 1, 1, need(t)))
    early = [x for x in runs if x[3] < long_way - 1]
    middle = [x for x in runs if x[3] == long_way - 1]
    late = [x for x in runs if x[3] == long_way]
    step = 1
    for run in early:
        while step < run[3]:
            step += 1
            serve_units(step)
        phase_one(*run[:3], 0, 2 * T)
    gS.forward()
    for c in gS.on:
        c.wait_recv()
    for run in early:
        phase_one(*run[:3], 2 * T, 4 * T)
    while step < long_way - 1:
        step += 1
        serve_units(step)
    for run in early:
        unit_grads(*run[:3])
    serve_units(long_way)
    for run in late:
        phase_one(*run[:3], 0, 4 * T)
    for run in late:
        unit_grads(*run[:3])

    class Scatter:
        def __init__(self, cls, at, buf, add):
            self.nf, self.nb = classes[cls]
            self.at, self.buf, self.add = at, buf, add
            nf, nb = self.nf, self.nb
            self.f = [net.copy(at(nf - t + 1), buf.at[box(t, True)], right) for t in range(1, nf + 1)]
            self.b = [net.copy(at(-(nb - t + 1)), buf.at[box(t, False)], left) for t in range(1, nb + 1)]

        def begin_long(self):
            (self.f if self.nf > self.nb else self.b)[0].start()

        def begin_short(self):
            (self.b if self.nf > self.nb else self.f)[0].start()

        def begin(self):
            self.begin_long()
            self.begin_short()

        def serve(self, t):
            nf, nb = self.nf, self.nb
            if t <= nf:
                self.f[t - 1].wait_recv()
            if t <= nb:
                self.b[t - 1].wait_recv()
            if t < nf:
                self.add(nf - t, box(t, True), True)
            if t < nb:
                self.add(-(nb - t), box(t, False), False)
            if t < nf:
                self.f[t].start()
            if t < nb:
                self.b[t].start()

        def last(self, value):
            return value(box(self.nf, True), True) + value(box(self.nb, False), False)

    def unit_scatter(cls, grad, buf):
        def at(k):
            return grad.at[pl.ds(jslot(k) * FP, FP)]

        def add(k, slot, forward):
            rows = unit_rows(jslot(k))
            grad[rows, :] = (grad[rows, :].astype(F32) + buf[slot].astype(F32)).astype(BF16)

        return Scatter(cls, at, buf, add)

    def down_scatter(cls, grad, buf, lo, size):
        def add(k, slot, forward):
            rows = drow(k, lo, size)
            grad[rows, :] = (grad[rows, :].astype(F32) + turn(buf[slot], forward)).astype(BF16)

        return Scatter(cls, lambda k: grad.at[drow(k, lo, size)], buf, add)

    sG = unit_scatter("A", rG, v["bufG"])
    sU = unit_scatter("B", rU, v["bufU"])
    sDA = down_scatter("A", rD, v["bufA"], 0, DA)
    sDB = down_scatter("B", rD, v["bufB"], DA, DP - DA)
    scatter_steps = [(sG, 1), (sU, 1)]
    for t in range(2, long_way + 1):
        scatter_steps += [(sG, t), (sU, t), (sDA, t - 1), (sDB, t - 1)]
    scatter_steps += [(sDA, long_way), (sDB, long_way)]
    scatter_done = [0]

    def serve_scatter(upto):
        while scatter_done[0] < min(upto, len(scatter_steps)):
            x, t = scatter_steps[scatter_done[0]]
            x.serve(t)
            scatter_done[0] += 1

    sG.begin_long()
    sU.begin_long()
    for run in middle:
        phase_one(*run[:3], 0, 4 * T)
    for run in middle:
        unit_grads(*run[:3])
    sU.begin_short()
    sG.begin_short()

    def block(ref, i):
        return ref.at[pl.ds(i * T, T)]

    class GroupSum:
        def __init__(self, stages, inbox, part, out):
            self.stages, self.inbox, self.part, self.out = stages, inbox, part, out
            self.far = net.copy(stages[0], inbox[0], core)
            self.over = [
                net.copy(stages[1].at[pl.ds(i * HB, HB)], inbox[1].at[pl.ds(i * HB, HB)], beside)
                for i in range(2)
            ]
            self.near = net.copy(stages[2], inbox[2], core)
            self.over_open = [True, True]

        def fill(self, q, stage):
            for c in parts(0, D, 512):
                stage[:, c] = self.part(q, c).astype(BF16)

        def send_far(self):
            self.fill(3, self.stages[0])
            self.far.start()

        def send_over(self, before=None):
            stage, inbox = self.stages[1], self.inbox[0]
            self.fill(2, stage)
            self.far.wait_recv()
            for i in (1, 0):
                rows = slice(i * HB, (i + 1) * HB)
                stage[rows, :] = (stage[rows, :].astype(F32) + inbox[rows, :].astype(F32)).astype(BF16)
                if before is not None:
                    net.sent(before)
                    before = None
                self.over[i].start()

        def send_near(self):
            self.fill(1, self.stages[2])
            self.near.start()

        def keep(self, more=False):
            for c in parts(0, D, 512):
                value = self.part(0, c)
                self.out[:, c] = self.out[:, c] + value if more else value

        def await_over(self, i):
            if self.over_open[i]:
                self.over_open[i] = False
                self.over[i].wait_recv()

        def finish(self, i):
            rows = slice(i * HB, (i + 1) * HB)
            self.await_over(i)
            total = self.out[rows, :] + self.inbox[1][rows, :].astype(F32)
            self.out[rows, :] = total + self.inbox[2][rows, :].astype(F32)

        def sent(self):
            net.sent([c for c in net.open if any(c is x for x in [self.far, self.near] + self.over)])

    def ds_part(q, c):
        rows = slice(q * T, (q + 1) * T)
        return nn(dg[rows, :], Wg[:, c]) + nn(du[rows, :], Wu[:, c])

    def y_part(q, c):
        rows = slice(q * T, (q + 1) * T)
        return nt(hid[rows, :], Wd[c, :])

    y_out, ds_out = v["y"], v["x"]
    sum_ds = GroupSum(
        [block(AW, 3), v["stage"], block(S, 1)], [block(AW, i) for i in range(3)], ds_part, ds_out
    )
    sum_y = GroupSum(
        [block(dO, 3), block(dO, 2), block(dO, 1)],
        [dg.at[pl.ds(3 * T, T), pl.ds(0, D)], v["y_in"], dg.at[pl.ds(0, T), pl.ds(0, D)]],
        y_part,
        y_out,
    )
    sum_ds.send_far()
    sum_ds.send_over()
    serve_scatter(2)
    for part in (slice(0, 256), slice(256, 512), slice(512, D)):
        rD[part, :] = tn(dO[:, part], hid[...]).astype(BF16)
    sDA.begin()
    sDB.begin()
    net.sent(gS.copies() + gO.copies())
    sum_ds.send_near()
    sum_ds.keep()
    back_w = net.local(v["spill"], W.at[:, pl.ds(0, D)])
    back_w.start()
    sum_ds.near.wait_recv()
    sum_y.send_far()
    sum_y.send_over(sum_ds.over)
    y_out[...] = res[:, 0:D]
    kv_acc = res
    kv_acc[...] = jnp.zeros_like(kv_acc)

    dm_at, dq_at, low_at = 2 * T, 3 * T, 3 * T
    gains = v["gains"]
    gains[...] = jnp.zeros_like(gains)

    def open_back(i):
        rows = slice(i * HB, (i + 1) * HB)
        r2 = stats[rows, 127:128]
        resid, dsec = y_out[rows, :], ds_out[rows, :]
        gains[2:3, :] += jnp.sum(dsec * resid * r2, axis=0, keepdims=True)
        scaled = dsec * vec[2:3, :]
        inner = jnp.mean(scaled * resid, axis=1, keepdims=True)
        dres = dO[rows, :].astype(F32) + scaled * r2 - resid * (r2 * r2 * r2 * inner)
        ds_out[rows, :] = dres
        low = dres.astype(BF16)
        dg[low_at + i * HB : low_at + (i + 1) * HB, 0:D] = low
        hid[dm_at + i * HB : dm_at + (i + 1) * HB, 0:D] = nn(low, W[WO : WO + D, 0:D]).astype(BF16)

    def attend_back(rb):
        rows, cols = slice(rb * HB, (rb + 1) * HB), (rb + 1) * HB

        def pair(p, _):
            lanes = pl.ds(pl.multiple_of(p * LANES, LANES), LANES)
            q_pair, dm = Q[rows, lanes], hid[dm_at + rb * HB : dm_at + (rb + 1) * HB, lanes]
            total = None
            for odd in range(2):
                h, idx = head_index(p, odd)
                lse = jnp.sum(
                    jnp.where(iota((HB, LANES), 1) == h, stats[rows, :], 0.0), axis=1, keepdims=True
                )
                prob = jnp.exp(scores(q_pair, idx, rb, cols) - lse)
                dp = nt(dm, VX[idx, 0:cols, :])
                t = prob * dp
                delta = jnp.sum(t, axis=1, keepdims=True)
                ds = ((t - prob * delta) * SCALE).astype(BF16)
                k_lanes = pl.ds(pl.multiple_of(idx * LANES, LANES), LANES)
                v_lanes = pl.ds(pl.multiple_of((4 + idx) * LANES, LANES), LANES)
                kv_acc[0:cols, v_lanes] += tn(prob.astype(BF16), dm)
                kv_acc[0:cols, k_lanes] += tn(ds, q_pair)
                part = nn(ds, KX[idx, 0:cols, :])
                total = part if total is None else total + part
            hid[dq_at + rb * HB : dq_at + (rb + 1) * HB, lanes] = rotate_back(total, rows).astype(BF16)
            return 0

        return pair

    serve_scatter(4)
    sum_ds.finish(1)
    back_w.wait()
    open_back(1)
    lax.fori_loop(0, PAIRS // 2, attend_back(1), 0)
    serve_scatter(6)
    lax.fori_loop(PAIRS // 2, PAIRS, attend_back(1), 0)
    sum_ds.finish(0)
    sum_ds.sent()
    open_back(0)
    wgrad = S
    for c in parts(0, D, 256):
        wgrad[D : 2 * D, c] = tn(dg[low_at : low_at + T, 0:D], mixed[:, c]).astype(BF16)

    def pack_first(gi, _):
        q_rows = wgrad[pl.ds(pl.multiple_of(gi * DP, 16), DP), :].astype(F32)
        o_rows = wgrad[pl.ds(pl.multiple_of(D + gi * DP, 16), DP), :].astype(F32)
        k_rows = wgrad[pl.ds(pl.multiple_of(WK + gi * K4, 16), K4), :].astype(F32)
        v_rows = wgrad[pl.ds(pl.multiple_of(WV + gi * K4, 16), K4), :].astype(F32)
        for i in range(4):
            tmp[0:DS, 0:D] = q_rows[i * DS : (i + 1) * DS]
            tmp[KO:VO, 0:D] = k_rows[i * KS : (i + 1) * KS]
            tmp[VO:OO, 0:D] = v_rows[i * KS : (i + 1) * KS]
            tmp[OO:PH, 0:D] = o_rows[i * DS : i * DS + PH - OO]
            AW[pl.ds(pl.multiple_of((i * R + gi) * AR, 16), PH), :] = tmp[0:PH, 0:D].astype(BF16)
        return 0

    def pack_rest(gi, _):
        o_rows = wgrad[pl.ds(pl.multiple_of(D + gi * DP, 16), DP), :].astype(F32)
        for i in range(4):
            tmp[0 : AR - PH, 0:D] = o_rows[i * DS + PH - OO : (i + 1) * DS]
            AW[pl.ds(pl.multiple_of((i * R + gi) * AR + PH, 16), AR - PH), :] = tmp[
                0 : AR - PH, 0:D
            ].astype(BF16)
        return 0

    def inbox_rows(i, k, lo, size):
        at = pl.multiple_of(T + (i * R + place_group(k)) * AR + lo, 16)
        return pl.ds(at, size)

    order = [k for s in range(long_way, 0, -1) for k in both(s)] + [0]

    class AttentionSum:
        def __init__(self, cls, lo, size, ring):
            self.lo, self.size = lo, size

            def at(dev_m, k):
                return AW.at[arow(dev_m, k, lo, size)]

            def inbox(i, k):
                if i == 2:
                    return v["stage"].at[self.rows(k)]
                return dg.at[inbox_rows(i, k, lo, size), pl.ds(0, D)]

            self.far = {k: net.copy(at(m3, k), inbox(0, k), core) for k in order}
            self.near = {k: net.copy(at(m1, k), inbox(1, k), core) for k in order}
            self.over = {k: net.copy(at(m2, k), inbox(2, k), beside) for k in order}

            def add(k, slot, forward):
                rows = arow(m, k, lo, size)
                AW[rows, :] = (AW[rows, :].astype(F32) + ring[slot].astype(F32)).astype(BF16)

            self.ring = Scatter(cls, lambda k: at(m, k), ring, add)

        def rows(self, k):
            return pl.ds(pl.multiple_of(place_group(k) * AR + self.lo, 16), self.size)

        def begin(self):
            for k in order:
                self.far[k].start()
            for k in order:
                self.near[k].start()

        def send_over(self, k):
            self.far[k].wait_recv()
            rows = arow(m2, k, self.lo, self.size)
            got = dg[inbox_rows(0, k, self.lo, self.size), 0:D]
            AW[rows, :] = (AW[rows, :].astype(F32) + got.astype(F32)).astype(BF16)
            self.over[k].start()

        def settle(self, k):
            self.near[k].wait_recv()
            self.over[k].wait_recv()
            rows = arow(m, k, self.lo, self.size)
            total = AW[rows, :].astype(F32)
            total = total + dg[inbox_rows(1, k, self.lo, self.size), 0:D].astype(F32)
            total = total + v["stage"][self.rows(k), :].astype(F32)
            AW[rows, :] = total.astype(BF16)

    sum_p = AttentionSum("A", 0, PH, v["ringP"])
    sum_o = AttentionSum("B", PH, AR - PH, v["ringO"])
    lax.fori_loop(0, R, pack_rest, 0)
    sum_o.begin()
    serve_scatter(8)
    lax.fori_loop(0, PAIRS, attend_back(0), 0)
    for i in (1, 0):
        sum_y.await_over(i)
    for k in order:
        sum_o.send_over(k)
    serve_scatter(10)

    low_half = iota((T, LANES), 1) < HD

    def joined(part):
        return jnp.where(
            low_half, part(0) + pltpu.roll(part(1), HD, 1), pltpu.roll(part(2), HD, 1) + part(3)
        )

    dkv = v["dkv"]
    dkv[:, 0:LANES] = rotate_back(
        joined(lambda i: kv_acc[:, i * LANES : (i + 1) * LANES]), slice(0, T)
    ).astype(BF16)
    dkv[:, LANES : 2 * LANES] = joined(lambda i: kv_acc[:, (4 + i) * LANES : (5 + i) * LANES]).astype(BF16)
    for c in parts(0, D, 256):
        wgrad[0:D, c] = tn(hid[dq_at : dq_at + T, 0:D], normed[:, c]).astype(BF16)
        wgrad[2 * D :, c] = tn(dkv[...], normed[:, c]).astype(BF16)
    lax.fori_loop(0, R, pack_first, 0)
    sum_p.begin()
    for k in order:
        sum_p.send_over(k)
    serve_scatter(12)

    gains[1:2, :] = jnp.sum(hid[dq_at : dq_at + T, 0:D].astype(F32), axis=0, keepdims=True)
    gains[3:4, 0 : 2 * LANES] = jnp.sum(dkv[...].astype(F32), axis=0, keepdims=True)

    def close_back(i, _):
        rows = pl.ds(pl.multiple_of(i * HB, HB), HB)
        dn = nn(hid[pl.ds(pl.multiple_of(dq_at + i * HB, HB), HB), 0:D], W[WQ : WQ + D, 0:D])
        dn += nn(dkv[rows, :], W[WK : WK + 2 * KV * HD, 0:D])
        xb = v["tok"][rows, :].astype(F32)
        r1 = stats[rows, 126:127]
        gains[0:1, :] += jnp.sum(dn * xb * r1, axis=0, keepdims=True)
        scaled = dn * vec[0:1, :]
        inner = jnp.mean(scaled * xb, axis=1, keepdims=True)
        ds_out[rows, :] = ds_out[rows, :] + scaled * r1 - xb * (r1 * r1 * r1 * inner)
        return 0

    lax.fori_loop(0, 2, close_back, 0)
    keep_x = net.local(ds_out, v["x_out"])
    keep_x.start()
    sum_y.send_near()
    sum_y.keep(True)
    serve_scatter(13)
    sum_y.near.wait_recv()
    for i in (1, 0):
        sum_y.finish(i)
    sum_y.sent()
    y_out[...] = y_out[...] * stats[:, 125:126]
    keep_y = net.local(y_out, v["y_out"])
    keep_y.start()

    SG = v["SG"]

    def collect_tile(i, _):
        start = pl.multiple_of(i * ST, ST)
        first = lax.rem(iota((ST, 1), 0), 8) == 0
        total = None
        for row, width, size, offset, stride in (
            (gains[0:1, :], D, DS, 0, 1),
            (gains[1:2, :], D, DS, DS, 1),
            (gains[2:3, :], D, DS, 2 * DS, 1),
            (gains[3:4, 0:LANES], LANES, KS, 3 * DS, 2),
            (gains[3:4, LANES : 2 * LANES], LANES, KS, 3 * DS + 1, 2),
        ):
            owner, _ = owner_of(iota((1, width), 1), size)
            _, inner = owner_of(iota((width, LANES), 0), size)
            pick = (iota((width, LANES), 1) == inner * stride + offset).astype(BF16)
            full = jnp.where((row_device(start) == owner) & first, row, 0.0)
            high = full.astype(BF16)
            part = nn(high, pick) + nn((full - high.astype(F32)).astype(BF16), pick)
            total = part if total is None else total + part
        SG[pl.ds(start, ST), :] = total
        return 0

    lax.fori_loop(0, rows_n // ST, collect_tile, 0)

    def sg_rows(dev_m):
        return pl.ds(pl.multiple_of(dev_m * R * 8, 8), R * 8)

    sg_in = v["sg_in"]
    s_far = net.copy(SG.at[sg_rows(m3)], sg_in.at[0], core)
    s_near = net.copy(SG.at[sg_rows(m1)], sg_in.at[1], core)
    s_over = net.copy(SG.at[sg_rows(m2)], sg_in.at[2], beside)
    s_far.start()
    s_near.start()
    s_far.wait_recv()
    SG[sg_rows(m2), :] = SG[sg_rows(m2), :] + sg_in[0]
    s_over.start()

    def small_add(k, slot, forward):
        SG[srow(m, k), :] = SG[srow(m, k), :] + v["sring"][slot]

    ssm = Scatter("A", lambda k: SG.at[srow(m, k)], v["sring"], small_add)

    def settle(s):
        for k in both(s) if s else (0,):
            sum_p.settle(k)
            sum_o.settle(k)

    settle(long_way)
    settle(long_way - 1)
    sum_p.ring.begin()
    sum_o.ring.begin()
    s_near.wait_recv()
    s_over.wait_recv()
    SG[sg_rows(m), :] = SG[sg_rows(m), :] + sg_in[1] + sg_in[2]
    ssm.begin()
    for t in range(1, long_way + 1):
        if t < long_way:
            settle(long_way - t - 1)
        for x in (sum_p.ring, sum_o.ring, ssm):
            x.serve(t)
        if t < long_way:
            serve_scatter(12 + t)
    mine = arow(m, 0)
    low = AW[mine, :].astype(F32)
    res[0:PH, 0:D] = low[0:PH] + sum_p.ring.last(lambda i, f: v["ringP"][i].astype(F32))
    res[PH:AR, 0:D] = low[PH:AR] + sum_o.ring.last(lambda i, f: v["ringO"][i].astype(F32))
    v["small_out"][...] = SG[srow(m, 0), :] + ssm.last(lambda i, f: v["sring"][i])

    serve_scatter(len(scatter_steps))
    mine = unit_rows(own)
    res[AR : AR + FP, 0:D] = rG[mine, :].astype(F32) + sG.last(lambda i, f: v["bufG"][i].astype(F32))
    res[AR + FP : AR + 2 * FP, 0:D] = rU[mine, :].astype(F32) + sU.last(
        lambda i, f: v["bufU"][i].astype(F32)
    )
    keep_rows = net.local(res.at[pl.ds(0, AR + 2 * FP), pl.ds(0, D)], v["rows_out"])
    keep_rows.start()
    tmp[0:DA, :] = rD[drow(0, 0, DA), :].astype(F32) + sDA.last(lambda i, f: turn(v["bufA"][i], f))
    tmp[DA:DP, :] = rD[drow(0, DA, DP - DA), :].astype(F32) + sDB.last(
        lambda i, f: turn(v["bufB"][i], f)
    )
    down_in = down_p
    for i in range(4):
        dx[i, 0:DS, :] = tmp[i * DS : (i + 1) * DS, :].astype(BF16)
    home = [
        net.copy(dx.at[dst_m], down_in.at[m], dev)
        for dst_m, dev in ((m1, core), (m2, beside), (m3, across))
    ]
    for c in home:
        c.start()
    down_in[m] = dx[m]
    for c in home:
        c.wait_recv()
    for i in range(4):
        full = turn_by_seat(down_in[i].astype(F32), True)
        for place in range(R):
            v["down_out"][:, owned_units(place, i)] = full[0:DS, place * FP : place * FP + FS]
    net.sent(net.open)
    for c in (keep_y, keep_x, keep_rows):
        c.wait()


def layer(geo, ins):
    R, T, D, FP, U, DSP, DP, DA = geo.R, geo.T, geo.D, geo.FP, geo.U, geo.DSP, geo.DP, geo.DA
    AR = geo.AR
    outs = {
        "y_out": ((T, D), F32),
        "x_out": ((T, D), F32),
        "rows_out": ((AR + 2 * FP, D), F32),
        "down_out": ((geo.DS, R * 4 * geo.FS), F32),
        "small_out": ((8, LANES), F32),
        "spill": ((2 * D + 2 * KV * HD, D), BF16),
    }
    scratch = {
        "down_p": ((4, DSP, U), BF16),
        "y": ((T, D), F32),
        "x": ((T, D), F32),
        "dx": ((4, DSP, U), BF16),
        "AW": ((4 * R * AR, D), BF16),
        "SM": ((4 * R * 8, LANES), F32),
        "SG": ((4 * R * 8, LANES), F32),
        "sg_in": ((3, R * 8, LANES), F32),
        "sring": ((4, 8, LANES), F32),
        "ringP": ((4, geo.PH, D), BF16),
        "ringO": ((4, AR - geo.PH, D), BF16),
        "stage": ((T, D), BF16),
        "y_in": ((T, D), BF16),
        "S": ((4 * T, D), BF16),
        "dO": ((4 * T, D), BF16),
        "tmp": ((DP, U), F32),
        "tmp3": ((8 * geo.KS, D), F32),
        "Wg": ((U, D), BF16),
        "Wu": ((U, D), BF16),
        "Wd": ((D, U), BF16),
        "hid": ((4 * T, U), BF16),
        "dg": ((4 * T, U), BF16),
        "du": ((4 * T, U), BF16),
        "gG": ((U, D), BF16),
        "gU": ((U, D), BF16),
        "gD": ((D, U), BF16),
        "bufG": ((4, FP, D), BF16),
        "bufU": ((4, FP, D), BF16),
        "bufA": ((4, DA, U), BF16),
        "bufB": ((4, DP - DA, U), BF16),
        "stats": ((T, LANES), F32),
        "bias": ((T, T), BF16),
        "cos": ((T, LANES), F32),
        "sin": ((T, LANES), F32),
        "vec": ((8, D), F32),
        "gains": ((8, D), F32),
        "normed": ((T, D), BF16),
        "Q": ((T, D), BF16),
        "mixed": ((T, D), BF16),
        "KX": ((4, T, LANES), BF16),
        "VX": ((4, T, LANES), BF16),
        "res": ((T, D + LANES), F32),
        "dkv": ((T, 2 * LANES), BF16),
    }
    alias = {"W": "du"}
    names = list(ins) + list(outs) + list(scratch) + ["send_sems", "recv_sems", "local_sems"]
    vm = pl.BlockSpec(memory_space=pltpu.VMEM)
    hbm = pl.BlockSpec(memory_space=pl.ANY)

    def body(*refs):
        table = dict(zip(names, refs))
        for new, old in alias.items():
            table[new] = table[old]
        kernel_body(geo, list(table), *table.values())

    res = pl.pallas_call(
        body,
        out_shape=[jax.ShapeDtypeStruct(s, d) for s, d in outs.values()],
        in_specs=[hbm if n == "cot" else vm for n in ins],
        out_specs=[vm if n in ("small_out", "down_out") else hbm for n in outs],
        scratch_shapes=[pltpu.VMEM(s, d) for s, d in scratch.values()]
        + [pltpu.SemaphoreType.DMA((28 * R + 16,))] * 2
        + [pltpu.SemaphoreType.DMA((6,))],
        compiler_params=pltpu.CompilerParams(
            collective_id=0, has_side_effects=True, vmem_limit_bytes=64 * 2**20
        ),
    )(*ins.values())
    return dict(zip(outs, res))


D = 896
eps_norm = 1e-06
rope_base = 1000000.0
masked_value = -1e30


def apply_weight(left, weight):
    return lax.dot_general(
        left, weight, (((1,), (1,)), ((), ())), preferred_element_type=jnp.float32
    )


def apply_transpose(left, weight):
    return jnp.dot(left, weight, preferred_element_type=jnp.float32)


def weight_grad(grad_rows, input_rows):
    return lax.dot_general(
        grad_rows, input_rows, (((0,), (0,)), ((), ())), preferred_element_type=jnp.float32
    )


def rms_scale(field_rows):
    return lax.rsqrt(jnp.mean(field_rows * field_rows, axis=1, keepdims=True) + eps_norm)


def norm_backward(grad_rows, field_rows, scale_rows, gain_values):
    scaled = grad_rows * gain_values
    return scaled * scale_rows - field_rows * scale_rows**3 * jnp.mean(
        scaled * field_rows, axis=1, keepdims=True
    )


def rope_tables(block_segments):
    slot_index = jnp.arange(block_segments.shape[0])
    same_segment = block_segments[:, None] == block_segments[None, :]
    earlier = slot_index[None, :] < slot_index[:, None]
    positions = jnp.sum((same_segment & earlier).astype(jnp.float32), axis=1)
    frequency = jnp.exp(jnp.arange(HD // 2, dtype=jnp.float32) * (-2.0 * math.log(rope_base) / HD))
    angles = positions[:, None] * frequency[None, :]
    return (jnp.cos(angles)[:, None, :], jnp.sin(angles)[:, None, :])


def rotate(vectors, cosine_table, sine_table):
    first_half = vectors[..., : HD // 2]
    second_half = vectors[..., HD // 2 :]
    return jnp.concatenate(
        [
            first_half * cosine_table - second_half * sine_table,
            second_half * cosine_table + first_half * sine_table,
        ],
        axis=-1,
    )


def rotate_back(vectors, cosine_table, sine_table):
    first_half = vectors[..., : HD // 2]
    second_half = vectors[..., HD // 2 :]
    return jnp.concatenate(
        [
            first_half * cosine_table + second_half * sine_table,
            second_half * cosine_table - first_half * sine_table,
        ],
        axis=-1,
    )


def plain_local(
    tokens,
    segment_ids,
    live_counts,
    first_gain,
    query_weight,
    query_bias,
    key_weight,
    value_weight,
    key_value_bias,
    output_weight,
    second_gain,
    gate_weight,
    up_weight,
    down_weight,
    cotangent,
):
    attention_set = (
        lax.all_gather(first_gain, "dp", axis=0, tiled=True),
        lax.all_gather(query_weight, "dp", axis=0, tiled=True),
        lax.all_gather(query_bias, "dp", axis=0, tiled=True),
        lax.all_gather(key_weight, "dp", axis=0, tiled=True),
        lax.all_gather(value_weight, "dp", axis=0, tiled=True),
        lax.all_gather(key_value_bias, "dp", axis=0, tiled=True),
        lax.all_gather(output_weight, "dp", axis=0, tiled=True),
    )
    first_full, query_full, query_bias_full, key_full, value_full, pair_bias_full, output_full = (
        attention_set
    )
    slot_count = tokens.shape[0]
    group_size = HEADS // KV
    scale_factor = HD ** (-0.5)
    slot_index = jnp.arange(slot_count)
    live_rows = (slot_index < live_counts[0]).astype(jnp.float32)
    allowed = (segment_ids[:, None] == segment_ids[None, :]) & (
        slot_index[None, :] <= slot_index[:, None]
    ) & (live_rows[None, :] > 0.5) | (slot_index[None, :] == slot_index[:, None])
    cosine_table, sine_table = rope_tables(segment_ids)
    token_rows = tokens.astype(jnp.float32)
    first_scale = rms_scale(token_rows)
    normed = (token_rows * first_scale * first_full.astype(jnp.float32)).astype(jnp.bfloat16)
    pair_bias_values = pair_bias_full.astype(jnp.float32)
    query_pre = apply_weight(normed, query_full) + query_bias_full.astype(jnp.float32)
    key_pre = apply_weight(normed, key_full) + pair_bias_values[:, 0]
    values = (apply_weight(normed, value_full) + pair_bias_values[:, 1]).astype(jnp.bfloat16)
    values = values.reshape(slot_count, KV, HD)
    rotated_queries = rotate(query_pre.reshape(slot_count, HEADS, HD), cosine_table, sine_table)
    rotated_queries = rotated_queries.astype(jnp.bfloat16).reshape(slot_count, KV, group_size, HD)
    rotated_keys = rotate(key_pre.reshape(slot_count, KV, HD), cosine_table, sine_table).astype(
        jnp.bfloat16
    )

    def attention_logits():
        scores = jnp.einsum(
            "ikgd,jkd->kgij", rotated_queries, rotated_keys, preferred_element_type=jnp.float32
        )
        return jnp.where(allowed[None, None], scores * scale_factor, masked_value)

    logits = attention_logits()
    row_top = jnp.max(logits, axis=-1, keepdims=True)
    exponent = jnp.exp(logits - row_top)
    row_total = jnp.sum(exponent, axis=-1, keepdims=True)
    weights_low = (exponent / row_total).astype(jnp.bfloat16)
    mixed_heads = jnp.einsum(
        "kgij,jkd->ikgd", weights_low, values, preferred_element_type=jnp.float32
    )
    mixed_heads = mixed_heads.reshape(slot_count, D).astype(jnp.bfloat16)
    residual = token_rows + apply_weight(mixed_heads, output_full)
    feed_set = (
        lax.all_gather(second_gain, "dp", axis=0, tiled=True),
        lax.all_gather(gate_weight, "dp", axis=0, tiled=True),
        lax.all_gather(up_weight, "dp", axis=0, tiled=True),
        lax.all_gather(down_weight, "dp", axis=0, tiled=True),
    )
    second_full, gate_full, up_full, down_full = feed_set
    second_scale = rms_scale(residual)
    second = (residual * second_scale * second_full.astype(jnp.float32)).astype(jnp.bfloat16)
    gate_value = apply_weight(second, gate_full)
    up_value = apply_weight(second, up_full)
    hidden = (jax.nn.silu(gate_value) * up_value).astype(jnp.bfloat16)
    layer_out = (residual + apply_weight(hidden, down_full)) * live_rows[:, None]
    feed_back = (
        lax.all_gather(second_gain, "dp", axis=0, tiled=True),
        lax.all_gather(gate_weight, "dp", axis=0, tiled=True),
        lax.all_gather(up_weight, "dp", axis=0, tiled=True),
        lax.all_gather(down_weight, "dp", axis=0, tiled=True),
    )
    back_second, back_gate, back_up, back_down = feed_back
    out_grad = cotangent.astype(jnp.float32) * live_rows[:, None]
    out_grad_low = out_grad.astype(jnp.bfloat16)
    down_shard = lax.psum_scatter(
        weight_grad(out_grad_low, hidden), "dp", scatter_dimension=0, tiled=True
    )
    hidden_grad = apply_transpose(out_grad_low, back_down)
    sigmoid_gate = jax.nn.sigmoid(gate_value)
    up_grad_rows = (hidden_grad * (gate_value * sigmoid_gate)).astype(jnp.bfloat16)
    gate_grad_rows = (
        hidden_grad * up_value * sigmoid_gate * (1.0 + gate_value * (1.0 - sigmoid_gate))
    ).astype(jnp.bfloat16)
    gate_part = weight_grad(gate_grad_rows, second)
    up_part = weight_grad(up_grad_rows, second)
    gate_up_shard = lax.psum_scatter(
        jnp.concatenate([gate_part, up_part], axis=1), "dp", scatter_dimension=0, tiled=True
    )
    model_width = second.shape[1]
    gate_shard = gate_up_shard[:, :model_width]
    up_shard = gate_up_shard[:, model_width:]
    second_grad_rows = apply_transpose(gate_grad_rows, back_gate) + apply_transpose(
        up_grad_rows, back_up
    )
    second_gain_grad = jnp.sum(second_grad_rows * residual * second_scale, axis=0)
    residual_grad = out_grad + norm_backward(
        second_grad_rows, residual, second_scale, back_second.astype(jnp.float32)
    )
    attention_back = (
        lax.all_gather(first_gain, "dp", axis=0, tiled=True),
        lax.all_gather(query_weight, "dp", axis=0, tiled=True),
        lax.all_gather(query_bias, "dp", axis=0, tiled=True),
        lax.all_gather(key_weight, "dp", axis=0, tiled=True),
        lax.all_gather(value_weight, "dp", axis=0, tiled=True),
        lax.all_gather(key_value_bias, "dp", axis=0, tiled=True),
        lax.all_gather(output_weight, "dp", axis=0, tiled=True),
    )
    back_first = attention_back[0]
    back_query = attention_back[1]
    back_key = attention_back[3]
    back_value = attention_back[4]
    back_output = attention_back[6]
    branch_grad = residual_grad.astype(jnp.bfloat16)
    output_grad = weight_grad(branch_grad, mixed_heads)
    mixed_grad = apply_transpose(branch_grad, back_output).astype(jnp.bfloat16)
    mixed_grad = mixed_grad.reshape(slot_count, KV, group_size, HD)
    probs = jnp.exp(attention_logits() - row_top) / row_total
    probs_low = probs.astype(jnp.bfloat16)
    value_grad_rows = jnp.einsum(
        "kgij,ikgd->jkd", probs_low, mixed_grad, preferred_element_type=jnp.float32
    )
    prob_grad = jnp.einsum("ikgd,jkd->kgij", mixed_grad, values, preferred_element_type=jnp.float32)
    logit_grad = probs * (prob_grad - jnp.sum(probs * prob_grad, axis=-1, keepdims=True))
    score_grad = (logit_grad * scale_factor).astype(jnp.bfloat16)
    query_rot_grad = jnp.einsum(
        "kgij,jkd->ikgd", score_grad, rotated_keys, preferred_element_type=jnp.float32
    )
    key_rot_grad = jnp.einsum(
        "kgij,ikgd->jkd", score_grad, rotated_queries, preferred_element_type=jnp.float32
    )
    query_grad_rows = rotate_back(
        query_rot_grad.reshape(slot_count, HEADS, HD), cosine_table, sine_table
    )
    query_grad_rows = query_grad_rows.astype(jnp.bfloat16).reshape(slot_count, D)
    key_grad_rows = (
        rotate_back(key_rot_grad, cosine_table, sine_table)
        .astype(jnp.bfloat16)
        .reshape(slot_count, KV * HD)
    )
    value_grad_low = value_grad_rows.astype(jnp.bfloat16).reshape(slot_count, KV * HD)
    query_grad = weight_grad(query_grad_rows, normed)
    query_bias_grad = jnp.sum(query_grad_rows.astype(jnp.float32), axis=0)
    key_grad = weight_grad(key_grad_rows, normed)
    value_grad = weight_grad(value_grad_low, normed)
    pair_bias_grad = jnp.stack(
        [
            jnp.sum(key_grad_rows.astype(jnp.float32), axis=0),
            jnp.sum(value_grad_low.astype(jnp.float32), axis=0),
        ],
        axis=1,
    )
    first_grad_rows = (
        apply_transpose(query_grad_rows, back_query)
        + apply_transpose(key_grad_rows, back_key)
        + apply_transpose(value_grad_low, back_value)
    )
    first_gain_grad = jnp.sum(first_grad_rows * token_rows * first_scale, axis=0)
    input_grad = residual_grad + norm_backward(
        first_grad_rows, token_rows, first_scale, back_first.astype(jnp.float32)
    )
    attention_shards = (
        lax.psum_scatter(first_gain_grad, "dp", scatter_dimension=0, tiled=True),
        lax.psum_scatter(query_grad, "dp", scatter_dimension=0, tiled=True),
        lax.psum_scatter(query_bias_grad, "dp", scatter_dimension=0, tiled=True),
        lax.psum_scatter(key_grad, "dp", scatter_dimension=0, tiled=True),
        lax.psum_scatter(value_grad, "dp", scatter_dimension=0, tiled=True),
        lax.psum_scatter(pair_bias_grad, "dp", scatter_dimension=0, tiled=True),
        lax.psum_scatter(output_grad, "dp", scatter_dimension=0, tiled=True),
        lax.psum_scatter(second_gain_grad, "dp", scatter_dimension=0, tiled=True),
    )
    return (layer_out, input_grad) + tuple(attention_shards) + (gate_shard, up_shard, down_shard)


def fused_local(
    geo,
    tokens,
    segment_ids,
    live_counts,
    first_gain,
    query_weight,
    query_bias,
    key_weight,
    value_weight,
    key_value_bias,
    output_weight,
    second_gain,
    gate_weight,
    up_weight,
    down_weight,
    cotangent,
):
    T, DS, FS, FP, KS = geo.T, geo.DS, geo.FS, geo.FP, geo.KS
    live = (jnp.arange(T) < live_counts[0]).astype(F32)
    vectors = jnp.concatenate(
        [first_gain, query_bias, second_gain, key_value_bias.reshape(-1)]
    ).astype(F32)
    aux = jnp.stack(
        [segment_ids.astype(F32), live, jnp.pad(vectors, (0, T - vectors.shape[0]))]
    )
    aux = jnp.pad(aux, ((0, 5), (0, 0)))
    res = layer(
        geo,
        {
            "tok": tokens,
            "cot": cotangent,
            "wq": query_weight,
            "wo": output_weight,
            "wk": key_weight,
            "wv": value_weight,
            "gate": gate_weight,
            "up": up_weight,
            "down": down_weight,
            "aux": aux,
        },
    )
    rows, vec = res["rows_out"], res["small_out"][0]
    AR, OO = geo.AR, geo.DS + 2 * geo.KS
    return (
        res["y_out"],
        res["x_out"],
        vec[:DS],
        rows[:DS],
        vec[DS : 2 * DS],
        rows[DS : DS + KS],
        rows[DS + KS : OO],
        vec[3 * DS : 3 * DS + 2 * KS].reshape(KS, 2),
        rows[OO:AR],
        vec[2 * DS : 3 * DS],
        rows[AR : AR + FS],
        rows[AR + FP : AR + FP + FS],
        res["down_out"],
    )


def local(tokens, segment_ids, live_counts, first_gain, *rest):
    geo = Geometry(
        lax.axis_size("dp"), tokens.shape[0], tokens.shape[1], rest[9].shape[1]
    )
    layer_of = functools.partial(fused_local, geo) if geo.fits() else plain_local
    return layer_of(tokens, segment_ids, live_counts, first_gain, *rest)


def solution(mesh):
    in_specs = (
        P("dp", None),
        P("dp"),
        P("dp"),
        P("dp"),
        P("dp", None),
        P("dp"),
        P("dp", None),
        P("dp", None),
        P("dp", None),
        P("dp", None),
        P("dp"),
        P("dp", None),
        P("dp", None),
        P("dp", None),
        P("dp", None),
    )
    out_specs = (
        P("dp", None),
        P("dp", None),
        P("dp"),
        P("dp", None),
        P("dp"),
        P("dp", None),
        P("dp", None),
        P("dp", None),
        P("dp", None),
        P("dp"),
        P("dp", None),
        P("dp", None),
        P("dp", None),
    )
    return jax.shard_map(local, mesh=mesh, in_specs=in_specs, out_specs=out_specs, check_vma=False)
```

```python
import functools
import math

import jax
import jax.numpy as jnp
from jax import lax
from jax.experimental import pallas as pl
from jax.experimental.pallas import tpu as pltpu
from jax.sharding import PartitionSpec as P

MESH = pl.DeviceIdType.MESH
F32 = jnp.float32
BF16 = jnp.bfloat16

HEADS = 14
KV = 2
HD = 64
GROUP = HEADS // KV
PAIRS = HEADS // 2
LANES = 128
EPS = 1e-06
ROPE_BASE = 1000000.0
MASKED = -1e30
SCALE = HD ** (-0.5)


def up16(n):
    return -(-n // 16) * 16


def nn(a, b):
    return jnp.dot(a, b, preferred_element_type=F32)


def nt(a, b):
    return lax.dot_general(a, b, (((1,), (1,)), ((), ())), preferred_element_type=F32)


def tn(a, b):
    return lax.dot_general(a, b, (((0,), (0,)), ((), ())), preferred_element_type=F32)


class Geometry:
    def __init__(self, devices, slots, width, hidden):
        self.n = devices
        self.R = devices // 4
        self.T = slots
        self.D = width
        self.FS = hidden // devices
        self.FP = up16(self.FS)
        self.U = self.R * self.FP
        self.DS = width // devices
        self.DSP = up16(self.DS)
        self.DP = 4 * self.DS
        self.DA = up16(self.DP // 2)
        self.KS = KV * HD // devices
        self.AR = 2 * self.DS + 2 * self.KS
        self.PH = up16(self.DS + 2 * self.KS)
        self.OFF = 1 - self.R // 2

    def fits(self):
        return (
            self.n % 32 == 0
            and self.DP % 16 == 0
            and self.AR % 16 == 0
            and self.FP % 32 == 0 and self.FS % 8 == 0
            and self.PH < self.AR
            and (4 * self.KS) % 16 == 0
            and self.U % 256 == 0
            and self.R * self.AR == self.T
            and self.R & (self.R - 1) == 0
            and 2 * self.D + 2 * KV * HD == 4 * self.T
            and 3 * self.DS + 2 * self.KS <= LANES
            and 4 * self.T * self.U * 6 <= 16 * 2**20
        )


def ring_place(g, R):
    odd = lax.rem(g, 2)
    half = lax.div(g, 2)
    return (1 - odd) * half + odd * (R - 1 - half)


def ring_group(place, R):
    high = lax.div(place, R // 2)
    return (1 - high) * (2 * place) + high * (2 * (R - 1 - place) + 1)


class Net:
    def __init__(self, send_sems, recv_sems, local_sems):
        self.send_sems, self.recv_sems, self.local_sems = send_sems, recv_sems, local_sems
        self.count = 0
        self.local_count = 0
        self.open = []
        self.index = []
        self.free = []

    def copy(self, src, dst, device):
        if self.free:
            i = self.free.pop()
        else:
            i = self.count
            self.count += 1
        made = pltpu.make_async_remote_copy(
            src_ref=src,
            dst_ref=dst,
            send_sem=self.send_sems.at[i],
            recv_sem=self.recv_sems.at[i],
            device_id=(device,),
            device_id_type=MESH,
        )
        self.open.append(made)
        self.index.append((made, i))
        return made

    def release(self, copies):
        for c in copies:
            self.free += [i for made, i in self.index if made is c]

    def sent(self, copies):
        for c in copies:
            c.wait_send()
        self.open = [x for x in self.open if all(x is not c for c in copies)]

    def local(self, src, dst):
        i = self.local_count
        self.local_count += 1
        return pltpu.make_async_copy(src, dst, self.local_sems.at[i])


def parts(lo, hi, step):
    return [slice(at, min(at + step, hi)) for at in range(lo, hi, step)]


def iota(shape, axis):
    return lax.broadcasted_iota(jnp.int32, shape, axis)


def kernel_body(geo, names, *refs):
    v = dict(zip(names, refs))
    R, T, D, FP, FS, U = geo.R, geo.T, geo.D, geo.FP, geo.FS, geo.U
    DSP, DS, DP, DA, KS, AR, PH = geo.DSP, geo.DS, geo.DP, geo.DA, geo.KS, geo.AR, geo.PH
    me = lax.axis_index("dp")
    m, g = lax.rem(me, 4), lax.div(me, 4)
    r = ring_place(g, R)

    def place_group(k):
        return ring_group(lax.rem(r + k + 2 * R, R), R)

    right = place_group(1) * 4 + m
    left = place_group(-1) * 4 + m
    m1 = m + 1 - 2 * lax.rem(m, 2)
    m2 = m + 2 - 4 * lax.div(m, 2)
    m3 = m1 + 2 - 4 * lax.div(m1, 2)
    core, beside, across = g * 4 + m1, g * 4 + m2, g * 4 + m3
    net = Net(v["send_sems"], v["recv_sems"], v["local_sems"])

    barrier = pltpu.get_barrier_semaphore()
    for peer in (right, left, core, beside, across):
        pl.semaphore_signal(barrier, inc=1, device_id=(peer,), device_id_type=MESH)

    AW, SM, tmp, aux = v["AW"], v["SM"], v["tmp"], v["aux"]
    S, dO = v["S"], v["dO"]
    Wg, Wu, Wd = v["Wg"], v["Wu"], v["Wd"]
    stats, bias = v["stats"], v["bias"]

    bring_cot = net.local(v["cot"], dO.at[pl.ds(0, T)])
    bring_cot.start()

    KO, VO, OO = DS, DS + KS, DS + 2 * KS
    tmp[0:DS, 0:D] = v["wq"][...].astype(F32)
    tmp[KO:VO, 0:D] = v["wk"][...].astype(F32)
    tmp[VO:OO, 0:D] = v["wv"][...].astype(F32)
    tmp[OO:AR, 0:D] = v["wo"][...].astype(F32)

    def arow(dev_m, k, lo=0, size=AR):
        return pl.ds(pl.multiple_of((dev_m * R + place_group(k)) * AR + lo, 16), size)

    AW[arow(m, 0), :] = tmp[0:AR, 0:D].astype(BF16)

    def srow(dev_m, k):
        return pl.ds(pl.multiple_of((dev_m * R + place_group(k)) * 8, 8), 8)

    SM[srow(m, 0), :] = jnp.where(iota((8, LANES), 0) == 0, aux[2:3, 0:LANES], 0.0)

    def jslot(k):
        return (k - geo.OFF) % R

    def unit_rows(j):
        return slice(j * FP, (j + 1) * FP)

    own = jslot(0)
    for ref, mine in ((Wg, v["gate"]), (Wu, v["up"])):
        if FP > FS:
            ref[unit_rows(own), :] = jnp.zeros((FP, D), BF16)
        ref[own * FP : own * FP + FS, :] = mine[...]

    pl.semaphore_wait(barrier, 5)

    long_way, short_way = R // 2, R // 2 - 1
    classes = {"A": (long_way, short_way), "B": (short_way, long_way)}

    class Gather:
        def __init__(self, cls, src, dst, arrive=None):
            self.nf, self.nb = classes[cls]
            self.f = [net.copy(src(-(s - 1)), dst(-s, s), right) for s in range(1, self.nf + 1)]
            self.b = [net.copy(src(s - 1), dst(s, s), left) for s in range(1, self.nb + 1)]
            self.arrive = arrive

        def begin(self):
            self.f[0].start()
            self.b[0].start()

        def serve(self, s):
            if s <= self.nf:
                self.f[s - 1].wait_recv()
            if s <= self.nb:
                self.b[s - 1].wait_recv()
            if self.arrive and s <= self.nf:
                self.arrive(-s, s)
            if self.arrive and s <= self.nb:
                self.arrive(s, s)
            if s < self.nf:
                self.f[s].start()
            if s < self.nb:
                self.b[s].start()

    def nearer(k):
        return k + 1 if k < 0 else k - 1

    class Fan:
        def __init__(self, cls, lo, size):
            def at(dev_m, k):
                return AW.at[arow(dev_m, k, lo, size)]

            self.ring = Gather(cls, lambda k: at(m, k), lambda k, s: at(m, nearer(k)))
            self.beside = {k: net.copy(at(m, k), at(m, k), beside) for k in ks}
            self.core = {k: net.copy(at(m, k), at(m, k), core) for k in ks}
            self.on = {k: net.copy(at(m2, k), at(m2, k), core) for k in ks}

        def out(self, k):
            self.beside[k].start()
            self.core[k].start()

        def forward(self, k):
            self.beside[k].wait_recv()
            self.on[k].start()

        def arrived(self):
            for k in ks:
                self.core[k].wait_recv()
                self.on[k].wait_recv()

        def copies(self):
            within = [c for d in (self.beside, self.core, self.on) for c in d.values()]
            return self.ring.f + self.ring.b + within

    def both(s):
        return [-s, s] if s < long_way else [s]

    ks = [0] + [k for s in range(1, long_way + 1) for k in both(s)]
    fan_p, fan_o = Fan("A", 0, PH), Fan("B", PH, AR - PH)
    gsm = Gather("A", lambda k: SM.at[srow(m, k)], lambda k, s: SM.at[srow(m, nearer(k))])

    def small_rows(dev_m):
        return SM.at[pl.ds(pl.multiple_of(dev_m * R * 8, 8), R * 8)]

    small_beside = net.copy(small_rows(m), small_rows(m), beside)
    small_core = net.copy(small_rows(m), small_rows(m), core)
    small_on = net.copy(small_rows(m2), small_rows(m2), core)
    attn_copies = fan_p.copies() + fan_o.copies() + gsm.f + gsm.b
    attn_copies += [small_beside, small_core, small_on]

    def drow(k, lo=0, size=DP):
        return pl.ds(pl.multiple_of(place_group(k) * DP + lo, 16), size)

    def turn(block, forward):
        return pltpu.roll(block.astype(F32), U - FP if forward else FP, 1)

    def box(s, forward):
        return (s % 2) * 2 + (0 if forward else 1)

    def down_gather(cls, buf, lo, size):
        def arrive(k, s):
            Wd[drow(k, lo, size), :] = turn(buf[box(s, k < 0)], k < 0).astype(BF16)

        return Gather(
            cls, lambda k: Wd.at[drow(k, lo, size)], lambda k, s: buf.at[box(s, k < 0)], arrive
        )

    def unit_gather(cls, ref, lo):
        def at(k):
            return ref.at[pl.ds(jslot(k) * FP + lo, FP // 2)]

        return Gather(cls, at, lambda k, s: at(k))

    gDA = down_gather("A", v["bufA"], 0, DA)
    gDB = down_gather("B", v["bufB"], DA, DP - DA)
    unit_pieces = [
        unit_gather("A", Wg, 0),
        unit_gather("B", Wg, FP // 2),
        unit_gather("A", Wu, 0),
        unit_gather("B", Wu, FP // 2),
    ]

    def serve_units(s):
        for x in unit_pieces:
            x.serve(s)

    def serve_down(s):
        gDA.serve(s)
        gDB.serve(s)

    def serve_attention(s):
        fan_p.ring.serve(s)
        fan_o.ring.serve(s)
        gsm.serve(s)

    fan_p.ring.begin()
    fan_o.ring.begin()
    gsm.begin()
    fan_p.out(0)
    unit_pieces[0].begin()

    seat = lax.rem(r + geo.OFF + R, R)

    def turn_by_seat(block, back):
        b = 1
        while b < R:
            odd = lax.rem(lax.div(seat, b), 2) == 1
            block = jnp.where(odd, pltpu.roll(block, b * FP if back else U - b * FP, 1), block)
            b *= 2
        return block

    def owned_units(place, i):
        half = R // 2
        group = 2 * place if place < half else 2 * (R - 1 - place) + 1
        return slice((4 * group + i) * FS, (4 * group + i + 1) * FS)

    down_p, dx = v["down_p"], v["dx"]
    for i in range(4):
        for place in range(R):
            rows = slice(i * DS, (i + 1) * DS)
            if FP > FS:
                tmp[rows, place * FP + FS : (place + 1) * FP] = jnp.zeros((DS, FP - FS), F32)
            tmp[rows, place * FP : place * FP + FS] = v["down"][:, owned_units(place, i)].astype(F32)
    tmp[...] = turn_by_seat(tmp[...], False)
    for i in range(4):
        down_p[i, 0:DS, :] = tmp[i * DS : (i + 1) * DS, :].astype(BF16)
    down_copies = [
        net.copy(down_p.at[dst_m], dx.at[m], dev)
        for dst_m, dev in ((m1, core), (m2, beside), (m3, across))
    ]
    for c in down_copies:
        c.start()

    frequency = jnp.exp(
        lax.rem(iota((1, LANES), 1), HD // 2).astype(F32) * (-2.0 * math.log(ROPE_BASE) / HD)
    )
    PT = 128

    def prepare(i, _):
        start = pl.multiple_of(i * PT, PT)
        rows = pl.ds(start, PT)
        seg_row, live_row = aux[0:1, :], aux[1:2, :]
        ii, jj = iota((PT, T), 0) + start, iota((PT, T), 1)
        seg_col = jnp.sum(jnp.where(ii == jj, seg_row, 0.0), axis=1, keepdims=True)
        live_col = jnp.sum(jnp.where(ii == jj, live_row, 0.0), axis=1, keepdims=True)
        same = seg_col == seg_row
        position = jnp.sum(jnp.where(same & (jj < ii), 1.0, 0.0), axis=1, keepdims=True)
        allowed = (same & (jj <= ii) & (live_row > 0.5)) | (ii == jj)
        bias[rows, :] = jnp.where(allowed, 0.0, MASKED).astype(BF16)
        dO[rows, :] = (dO[rows, :].astype(F32) * live_col).astype(BF16)
        lane = iota((PT, LANES), 1)
        angles = position * frequency
        v["cos"][rows, :] = jnp.cos(angles)
        sine = jnp.sin(angles)
        v["sin"][rows, :] = jnp.where(lax.rem(lane, HD) < HD // 2, -sine, sine)
        x = v["tok"][rows, :].astype(F32)
        r1 = lax.rsqrt(jnp.mean(x * x, axis=1, keepdims=True) + EPS)
        stats[rows, :] = jnp.where(lane == 126, r1, jnp.where(lane == 125, live_col, 0.0))
        return 0

    bring_cot.wait()
    serve_attention(1)
    for k in both(1):
        fan_p.out(k)
    unit_pieces[1].begin()
    lax.fori_loop(0, T // PT // 2, prepare, 0)
    fan_p.forward(0)
    for s in range(2, long_way + 1):
        serve_attention(s)
        for k in both(s):
            fan_p.out(k)
        if s == 2:
            unit_pieces[2].begin()
            lax.fori_loop(T // PT // 2, T // PT, prepare, 0)
        if s == 3:
            unit_pieces[3].begin()
            dx[m] = down_p[m]
            for c in down_copies:
                c.wait_recv()
            for i in range(4):
                tmp[i * DS : (i + 1) * DS, :] = dx[i].astype(F32)[0:DS, :]
            Wd[drow(0), :] = tmp[0:DP, :].astype(BF16)
            net.sent(down_copies)
        for k in both(s - 1):
            fan_p.forward(k)
    gDA.begin()
    gDB.begin()

    PX = T // 2

    class GroupGather:
        def __init__(self, buf):
            def at(q, i):
                return buf.at[pl.ds(q * T + i * PX, PX)]

            self.beside = [net.copy(at(0, i), at(2, i), beside) for i in range(2)]
            self.core = [net.copy(at(0, i), at(1, i), core) for i in range(2)]
            self.on = [net.copy(at(2, i), at(3, i), core) for i in range(2)]

        def out(self, i):
            self.beside[i].start()
            self.core[i].start()

        def forward(self):
            for i in range(2):
                self.beside[i].wait_recv()
                self.on[i].start()

        def copies(self):
            return self.beside + self.core + self.on

    gS, gO = GroupGather(S), GroupGather(dO)
    small_beside.start()
    small_core.start()
    for k in ks:
        fan_o.out(k)
    gO.out(0)
    gO.out(1)
    for k in both(long_way):
        fan_p.forward(k)
    small_beside.wait_recv()
    small_on.start()
    fan_p.arrived()
    small_core.wait_recv()
    small_on.wait_recv()

    W, tmp3 = v["W"], v["tmp3"]
    WQ, WO, WK, WV = 0, D, 2 * D, 2 * D + KV * HD
    K4 = 4 * KS

    def unpack_first(gi, _):
        for i in range(4):
            at = pl.ds(pl.multiple_of((i * R + gi) * AR, 16), PH)
            rows = AW[at, :].astype(F32)
            tmp[i * DS : (i + 1) * DS, 0:D] = rows[0:DS]
            tmp3[i * KS : (i + 1) * KS, :] = rows[KO:VO]
            tmp3[K4 + i * KS : K4 + (i + 1) * KS, :] = rows[VO:OO]
        W[pl.ds(pl.multiple_of(WQ + gi * DP, 16), DP), 0:D] = tmp[0:DP, 0:D].astype(BF16)
        W[pl.ds(pl.multiple_of(WK + gi * K4, 16), K4), 0:D] = tmp3[0:K4, :].astype(BF16)
        W[pl.ds(pl.multiple_of(WV + gi * K4, 16), K4), 0:D] = tmp3[K4:, :].astype(BF16)
        return 0

    OB = OO // 16 * 16

    def unpack_output(gi, _):
        for i in range(4):
            at = pl.ds(pl.multiple_of((i * R + gi) * AR + OB, 16), AR - OB)
            tmp[i * DS : (i + 1) * DS, 0:D] = AW[at, :].astype(F32)[OO - OB : AR - OB]
        W[pl.ds(pl.multiple_of(WO + gi * DP, 16), DP), 0:D] = tmp[0:DP, 0:D].astype(BF16)
        return 0

    lax.fori_loop(0, R, unpack_first, 0)

    rows_n = 4 * R * 8
    ST = 64

    def owner_of(lanes, size):
        block = jnp.floor((lanes.astype(F32) + 0.5) * (1.0 / size)).astype(jnp.int32)
        return block, lanes - block * size

    def row_device(start):
        i = lax.div(iota((ST, 1), 0) + start, 8)
        return lax.rem(i, R) * 4 + lax.div(i, R)

    def spread(width, size, offset, stride):
        owner, inner = owner_of(iota((1, width), 1), size)
        pick = (iota((LANES, width), 0) == inner * stride + offset).astype(BF16)

        def tile(i, total):
            start = pl.multiple_of(i * ST, ST)
            full = nn(SM[pl.ds(start, ST), :].astype(BF16), pick)
            full = jnp.where(row_device(start) == owner, full, 0.0)
            return total + jnp.sum(full, axis=0, keepdims=True)

        return lax.fori_loop(0, rows_n // ST, tile, jnp.zeros((1, width), F32))

    vec = v["vec"]
    vec[0:1, :] = spread(D, DS, 0, 1)
    vec[1:2, :] = spread(D, DS, DS, 1)
    vec[2:3, :] = spread(D, DS, 2 * DS, 1)
    vec[3:4, 0:LANES] = spread(LANES, KS, 3 * DS, 2)
    vec[4:5, 0:LANES] = spread(LANES, KS, 3 * DS + 1, 2)

    cosine, sine = v["cos"], v["sin"]
    normed, Q, mixed = v["normed"], v["Q"], v["mixed"]
    KX, VX, res = v["KX"], v["VX"], v["res"]

    def swap_halves(block):
        lanes = iota(block.shape, 1)
        return jnp.where(
            lax.rem(lanes, HD) < HD // 2,
            pltpu.roll(block, LANES - HD // 2, 1),
            pltpu.roll(block, HD // 2, 1),
        )

    def rotate(block, rows):
        return block * cosine[rows, :] + swap_halves(block) * sine[rows, :]

    def rotate_back(block, rows):
        return block * cosine[rows, :] - swap_halves(block) * sine[rows, :]

    HB = T // 2

    def project(i, _):
        rows = pl.ds(pl.multiple_of(i * HB, HB), HB)
        xb = v["tok"][rows, :].astype(F32)
        nb = (xb * stats[rows, 126:127] * vec[0:1, :]).astype(BF16)
        normed[rows, :] = nb
        q = nt(nb, W[WQ : WQ + D, 0:D]) + vec[1:2, :]
        for p in range(PAIRS):
            lanes = slice(p * LANES, (p + 1) * LANES)
            Q[rows, lanes] = rotate(q[:, lanes], rows).astype(BF16)
        key = rotate(nt(nb, W[WK : WK + KV * HD, 0:D]) + vec[3:4, 0:LANES], rows)
        value = nt(nb, W[WV : WV + KV * HD, 0:D]) + vec[4:5, 0:LANES]
        low_half = iota((HB, LANES), 1) < HD
        for ref, full in ((KX, key), (VX, value)):
            other = pltpu.roll(full, HD, 1)
            ref[0, rows, :] = jnp.where(low_half, full, 0.0).astype(BF16)
            ref[1, rows, :] = jnp.where(low_half, 0.0, other).astype(BF16)
            ref[2, rows, :] = jnp.where(low_half, other, 0.0).astype(BF16)
            ref[3, rows, :] = jnp.where(low_half, 0.0, full).astype(BF16)
        return 0

    lax.fori_loop(0, 2, project, 0)
    serve_down(1)
    for k in ks:
        fan_o.forward(k)

    def head_index(p, odd):
        h = 2 * p + odd
        return h, lax.div(h, GROUP) * 2 + odd

    def scores(q_pair, idx, rb, cols):
        s = nt(q_pair, KX[idx, 0:cols, :])
        return s * SCALE + bias[rb * HB : (rb + 1) * HB, 0:cols].astype(F32)

    def attend(p, _):
        lanes = pl.ds(pl.multiple_of(p * LANES, LANES), LANES)
        for rb in range(2):
            rows, cols = slice(rb * HB, (rb + 1) * HB), (rb + 1) * HB
            q_pair = Q[rows, lanes]
            total = None
            for odd in range(2):
                h, idx = head_index(p, odd)
                s = scores(q_pair, idx, rb, cols)
                top = jnp.max(s, axis=1, keepdims=True)
                e = jnp.exp(s - top)
                norm = jnp.sum(e, axis=1, keepdims=True)
                low = (e * (1.0 / norm)).astype(BF16)
                part = nn(low, VX[idx, 0:cols, :])
                total = part if total is None else total + part
                lse = top + jnp.log(norm)
                stats[rows, :] = jnp.where(iota((HB, LANES), 1) == h, lse, stats[rows, :])
            mixed[rows, lanes] = total.astype(BF16)
        return 0

    lax.fori_loop(0, PAIRS // 2, attend, 0)
    serve_down(2)
    lax.fori_loop(PAIRS // 2, PAIRS, attend, 0)
    fan_o.arrived()
    lax.fori_loop(0, R, unpack_output, 0)
    net.sent(attn_copies)

    for i in range(2):
        rows = slice(i * HB, (i + 1) * HB)
        out = v["tok"][rows, :].astype(F32) + nt(mixed[rows, :], W[WO : WO + D, 0:D])
        res[rows, 0:D] = out
        r2 = lax.rsqrt(jnp.mean(out * out, axis=1, keepdims=True) + EPS)
        stats[rows, :] = jnp.where(iota((HB, LANES), 1) == 127, r2, stats[rows, :])
        S[rows, :] = (out * r2 * vec[2:3, :]).astype(BF16)
        gS.out(i)
    keep_w = net.local(W.at[:, pl.ds(0, D)], v["spill"])
    keep_w.start()
    serve_down(3)
    serve_units(1)
    gO.forward()
    serve_down(4)
    for d in range(5, long_way + 1):
        serve_down(d)
    keep_w.wait()
    for c in gO.core + gO.on + gS.core:
        c.wait_recv()

    hid, dg, du = v["hid"], v["dg"], v["du"]
    TT, CT = 512, 256

    def unit_tile(first, stride, i):
        return pl.ds(pl.multiple_of((first + stride * i) * CT, CT), CT)

    def phase_one(first, stride, count, lo, hi):
        down_n = (hi - lo) // TT

        def tile(i, _):
            rows = pl.ds(pl.multiple_of(lo + lax.rem(i, down_n) * TT, TT), TT)
            cols = unit_tile(first, stride, lax.div(i, down_n))
            s_rows, o_rows = S[rows, :], dO[rows, :]
            gate = nt(s_rows, Wg[cols, :])
            up = nt(s_rows, Wu[cols, :])
            dh = nn(o_rows, Wd[:, cols])
            sg = jax.nn.sigmoid(gate)
            gs = gate * sg
            hid[rows, cols] = (gs * up).astype(BF16)
            du[rows, cols] = (dh * gs).astype(BF16)
            dg[rows, cols] = (dh * up * (sg + gs * (1.0 - sg))).astype(BF16)
            return 0

        lax.fori_loop(0, count * down_n, tile, 0)

    rG, rU, rD = v["gG"], v["gU"], v["gD"]

    def unit_grads(first, stride, count):
        def tile(i, _):
            cols = unit_tile(first, stride, i)
            rG[cols, :] = tn(dg[:, cols], S[...]).astype(BF16)
            rU[cols, :] = tn(du[:, cols], S[...]).astype(BF16)
            return 0

        lax.fori_loop(0, count, tile, 0)

    def need(t):
        return max(abs(j + geo.OFF) for j in range(t * CT // FP, ((t + 1) * CT - 1) // FP + 1))

    tiles = sorted(range(U // CT), key=need)
    runs = []
    for t in tiles:
        if runs and runs[-1][3] == need(t):
            first, stride, count, step = runs[-1]
            if count == 1 or t - first == stride * count:
                runs[-1] = (first, t - first if count == 1 else stride, count + 1, step)
                continue
        runs.append((t, 1, 1, need(t)))
    early = [x for x in runs if x[3] < long_way - 1]
    middle = [x for x in runs if x[3] == long_way - 1]
    late = [x for x in runs if x[3] == long_way]
    step = 1
    for run in early:
        while step < run[3]:
            step += 1
            serve_units(step)
        phase_one(*run[:3], 0, 2 * T)
    gS.forward()
    for c in gS.on:
        c.wait_recv()
    for run in early:
        phase_one(*run[:3], 2 * T, 4 * T)
    while step < long_way - 1:
        step += 1
        serve_units(step)
    for run in early:
        unit_grads(*run[:3])
    serve_units(long_way)
    for run in late:
        phase_one(*run[:3], 0, 4 * T)
    for run in late:
        unit_grads(*run[:3])

    net.release(attn_copies)

    class Scatter:
        def __init__(self, cls, at, buf, add):
            self.nf, self.nb = classes[cls]
            self.at, self.buf, self.add = at, buf, add
            nf, nb = self.nf, self.nb
            self.f = [net.copy(at(nf - t + 1), buf.at[box(t, True)], right) for t in range(1, nf + 1)]
            self.b = [net.copy(at(-(nb - t + 1)), buf.at[box(t, False)], left) for t in range(1, nb + 1)]

        def begin_long(self):
            (self.f if self.nf > self.nb else self.b)[0].start()

        def begin_short(self):
            (self.b if self.nf > self.nb else self.f)[0].start()

        def begin(self):
            self.begin_long()
            self.begin_short()

        def serve(self, t):
            nf, nb = self.nf, self.nb
            if t <= nf:
                self.f[t - 1].wait_recv()
            if t <= nb:
                self.b[t - 1].wait_recv()
            if t < nf:
                self.add(nf - t, box(t, True), True)
            if t < nb:
                self.add(-(nb - t), box(t, False), False)
            if t < nf:
                self.f[t].start()
            if t < nb:
                self.b[t].start()

        def last(self, value):
            return value(box(self.nf, True), True) + value(box(self.nb, False), False)

    def unit_scatter(cls, grad, buf):
        def at(k):
            return grad.at[pl.ds(jslot(k) * FP, FP)]

        def add(k, slot, forward):
            rows = unit_rows(jslot(k))
            grad[rows, :] = (grad[rows, :].astype(F32) + buf[slot].astype(F32)).astype(BF16)

        return Scatter(cls, at, buf, add)

    def down_scatter(cls, grad, buf, lo, size):
        def add(k, slot, forward):
            rows = drow(k, lo, size)
            grad[rows, :] = (grad[rows, :].astype(F32) + turn(buf[slot], forward)).astype(BF16)

        return Scatter(cls, lambda k: grad.at[drow(k, lo, size)], buf, add)

    sG = unit_scatter("A", rG, v["bufG"])
    sU = unit_scatter("B", rU, v["bufU"])
    sDA = down_scatter("A", rD, v["bufA"], 0, DA)
    sDB = down_scatter("B", rD, v["bufB"], DA, DP - DA)
    scatter_steps = [(sG, 1), (sU, 1), (sG, 2), (sDA, 1), (sDB, 1), (sU, 2), (sDA, 2), (sDB, 2)]
    for t in range(3, long_way):
        scatter_steps += [(sG, t), (sU, t), (sDA, t), (sDB, t)]
    scatter_steps += [(sDA, long_way), (sDB, long_way), (sG, long_way), (sU, long_way)]
    scatter_done = [0]

    def serve_scatter(upto):
        while scatter_done[0] < min(upto, len(scatter_steps)):
            x, t = scatter_steps[scatter_done[0]]
            x.serve(t)
            scatter_done[0] += 1

    sG.begin_long()
    sU.begin_long()
    for run in middle:
        phase_one(*run[:3], 0, 4 * T)
    for run in middle:
        unit_grads(*run[:3])
    sU.begin_short()
    sG.begin_short()

    def block(ref, i):
        return ref.at[pl.ds(i * T, T)]

    class GroupSum:
        def __init__(self, stages, inbox, part, out):
            self.stages, self.inbox, self.part, self.out = stages, inbox, part, out
            self.far = net.copy(stages[0], inbox[0], core)
            self.over = [
                net.copy(stages[1].at[pl.ds(i * HB, HB)], inbox[1].at[pl.ds(i * HB, HB)], beside)
                for i in range(2)
            ]
            self.near = net.copy(stages[2], inbox[2], core)
            self.over_open = [True, True]

        def fill(self, q, stage):
            for c in parts(0, D, 512):
                stage[:, c] = self.part(q, c).astype(BF16)

        def send_far(self):
            self.fill(3, self.stages[0])
            self.far.start()

        def send_over(self, before=None):
            stage, inbox = self.stages[1], self.inbox[0]
            self.fill(2, stage)
            self.far.wait_recv()
            for i in (1, 0):
                rows = slice(i * HB, (i + 1) * HB)
                stage[rows, :] = (stage[rows, :].astype(F32) + inbox[rows, :].astype(F32)).astype(BF16)
                if before is not None:
                    net.sent(before)
                    before = None
                self.over[i].start()

        def send_near(self):
            self.fill(1, self.stages[2])
            self.near.start()

        def keep(self, more=False):
            for c in parts(0, D, 512):
                value = self.part(0, c)
                self.out[:, c] = self.out[:, c] + value if more else value

        def await_over(self, i):
            if self.over_open[i]:
                self.over_open[i] = False
                self.over[i].wait_recv()

        def finish(self, i):
            rows = slice(i * HB, (i + 1) * HB)
            self.await_over(i)
            total = self.out[rows, :] + self.inbox[1][rows, :].astype(F32)
            self.out[rows, :] = total + self.inbox[2][rows, :].astype(F32)

        def sent(self):
            net.sent([c for c in net.open if any(c is x for x in [self.far, self.near] + self.over)])

    def ds_part(q, c):
        rows = slice(q * T, (q + 1) * T)
        return nn(dg[rows, :], Wg[:, c]) + nn(du[rows, :], Wu[:, c])

    def y_part(q, c):
        rows = slice(q * T, (q + 1) * T)
        return nt(hid[rows, :], Wd[c, :])

    y_out, ds_out = v["y"], v["x"]
    sum_ds = GroupSum(
        [block(AW, 3), v["stage"], block(S, 1)], [block(AW, i) for i in range(3)], ds_part, ds_out
    )
    sum_y = GroupSum(
        [block(dO, 3), block(dO, 2), block(dO, 1)],
        [dg.at[pl.ds(3 * T, T), pl.ds(0, D)], v["y_in"], dg.at[pl.ds(0, T), pl.ds(0, D)]],
        y_part,
        y_out,
    )
    sum_ds.send_far()
    sum_ds.send_over()
    serve_scatter(2)
    for part in (slice(0, 256), slice(256, 512), slice(512, D)):
        rD[part, :] = tn(dO[:, part], hid[...]).astype(BF16)
    sDA.begin()
    sDB.begin()
    net.sent(gS.copies() + gO.copies())
    sum_ds.send_near()
    sum_ds.keep()
    back_w = net.local(v["spill"], W.at[:, pl.ds(0, D)])
    back_w.start()
    sum_ds.near.wait_recv()
    sum_y.send_far()
    sum_y.send_over(sum_ds.over)
    y_out[...] = res[:, 0:D]
    kv_acc = res
    kv_acc[...] = jnp.zeros_like(kv_acc)

    dm_at, dq_at, low_at = 2 * T, 3 * T, 3 * T
    gains = v["gains"]
    gains[...] = jnp.zeros_like(gains)

    def open_back(i):
        rows = slice(i * HB, (i + 1) * HB)
        r2 = stats[rows, 127:128]
        resid, dsec = y_out[rows, :], ds_out[rows, :]
        gains[2:3, :] += jnp.sum(dsec * resid * r2, axis=0, keepdims=True)
        scaled = dsec * vec[2:3, :]
        inner = jnp.mean(scaled * resid, axis=1, keepdims=True)
        dres = dO[rows, :].astype(F32) + scaled * r2 - resid * (r2 * r2 * r2 * inner)
        ds_out[rows, :] = dres
        low = dres.astype(BF16)
        dg[low_at + i * HB : low_at + (i + 1) * HB, 0:D] = low
        hid[dm_at + i * HB : dm_at + (i + 1) * HB, 0:D] = nn(low, W[WO : WO + D, 0:D]).astype(BF16)

    def attend_back(rb):
        rows, cols = slice(rb * HB, (rb + 1) * HB), (rb + 1) * HB

        def pair(p, _):
            lanes = pl.ds(pl.multiple_of(p * LANES, LANES), LANES)
            q_pair, dm = Q[rows, lanes], hid[dm_at + rb * HB : dm_at + (rb + 1) * HB, lanes]
            total = None
            for odd in range(2):
                h, idx = head_index(p, odd)
                lse = jnp.sum(
                    jnp.where(iota((HB, LANES), 1) == h, stats[rows, :], 0.0), axis=1, keepdims=True
                )
                prob = jnp.exp(scores(q_pair, idx, rb, cols) - lse)
                dp = nt(dm, VX[idx, 0:cols, :])
                t = prob * dp
                delta = jnp.sum(t, axis=1, keepdims=True)
                ds = ((t - prob * delta) * SCALE).astype(BF16)
                k_lanes = pl.ds(pl.multiple_of(idx * LANES, LANES), LANES)
                v_lanes = pl.ds(pl.multiple_of((4 + idx) * LANES, LANES), LANES)
                kv_acc[0:cols, v_lanes] += tn(prob.astype(BF16), dm)
                kv_acc[0:cols, k_lanes] += tn(ds, q_pair)
                part = nn(ds, KX[idx, 0:cols, :])
                total = part if total is None else total + part
            hid[dq_at + rb * HB : dq_at + (rb + 1) * HB, lanes] = rotate_back(total, rows).astype(BF16)
            return 0

        return pair

    serve_scatter(4)
    sum_ds.finish(1)
    back_w.wait()
    open_back(1)
    lax.fori_loop(0, PAIRS // 2, attend_back(1), 0)
    serve_scatter(6)
    lax.fori_loop(PAIRS // 2, PAIRS, attend_back(1), 0)
    sum_ds.finish(0)
    sum_ds.sent()
    open_back(0)
    wgrad = S
    for c in parts(0, D, 256):
        wgrad[D : 2 * D, c] = tn(dg[low_at : low_at + T, 0:D], mixed[:, c]).astype(BF16)

    def pack_first(gi, _):
        q_rows = wgrad[pl.ds(pl.multiple_of(gi * DP, 16), DP), :].astype(F32)
        o_rows = wgrad[pl.ds(pl.multiple_of(D + gi * DP, 16), DP), :].astype(F32)
        k_rows = wgrad[pl.ds(pl.multiple_of(WK + gi * K4, 16), K4), :].astype(F32)
        v_rows = wgrad[pl.ds(pl.multiple_of(WV + gi * K4, 16), K4), :].astype(F32)
        for i in range(4):
            tmp[0:DS, 0:D] = q_rows[i * DS : (i + 1) * DS]
            tmp[KO:VO, 0:D] = k_rows[i * KS : (i + 1) * KS]
            tmp[VO:OO, 0:D] = v_rows[i * KS : (i + 1) * KS]
            tmp[OO:PH, 0:D] = o_rows[i * DS : i * DS + PH - OO]
            AW[pl.ds(pl.multiple_of((i * R + gi) * AR, 16), PH), :] = tmp[0:PH, 0:D].astype(BF16)
        return 0

    def pack_rest(gi, _):
        o_rows = wgrad[pl.ds(pl.multiple_of(D + gi * DP, 16), DP), :].astype(F32)
        for i in range(4):
            tmp[0 : AR - PH, 0:D] = o_rows[i * DS + PH - OO : (i + 1) * DS]
            AW[pl.ds(pl.multiple_of((i * R + gi) * AR + PH, 16), AR - PH), :] = tmp[
                0 : AR - PH, 0:D
            ].astype(BF16)
        return 0

    def inbox_rows(i, k, lo, size):
        at = pl.multiple_of(T + (i * R + place_group(k)) * AR + lo, 16)
        return pl.ds(at, size)

    order = [k for s in range(long_way, 0, -1) for k in both(s)] + [0]

    class AttentionSum:
        def __init__(self, cls, lo, size, ring):
            self.lo, self.size = lo, size

            def at(dev_m, k):
                return AW.at[arow(dev_m, k, lo, size)]

            def inbox(i, k):
                if i == 2:
                    return v["stage"].at[self.rows(k)]
                return dg.at[inbox_rows(i, k, lo, size), pl.ds(0, D)]

            self.far = {k: net.copy(at(m3, k), inbox(0, k), core) for k in order}
            self.near = {k: net.copy(at(m1, k), inbox(1, k), core) for k in order}
            self.over = {k: net.copy(at(m2, k), inbox(2, k), beside) for k in order}

            def add(k, slot, forward):
                rows = arow(m, k, lo, size)
                AW[rows, :] = (AW[rows, :].astype(F32) + ring[slot].astype(F32)).astype(BF16)

            self.ring = Scatter(cls, lambda k: at(m, k), ring, add)

        def rows(self, k):
            return pl.ds(pl.multiple_of(place_group(k) * AR + self.lo, 16), self.size)

        def begin(self):
            for k in order:
                self.far[k].start()
            for k in order:
                self.near[k].start()

        def send_over(self, k):
            self.far[k].wait_recv()
            rows = arow(m2, k, self.lo, self.size)
            got = dg[inbox_rows(0, k, self.lo, self.size), 0:D]
            AW[rows, :] = (AW[rows, :].astype(F32) + got.astype(F32)).astype(BF16)
            self.over[k].start()

        def settle(self, k):
            self.near[k].wait_recv()
            self.over[k].wait_recv()
            rows = arow(m, k, self.lo, self.size)
            total = AW[rows, :].astype(F32)
            total = total + dg[inbox_rows(1, k, self.lo, self.size), 0:D].astype(F32)
            total = total + v["stage"][self.rows(k), :].astype(F32)
            AW[rows, :] = total.astype(BF16)

    sum_p = AttentionSum("A", 0, PH, v["ringP"])
    sum_o = AttentionSum("B", PH, AR - PH, v["ringO"])
    lax.fori_loop(0, R, pack_rest, 0)
    sum_o.begin()
    serve_scatter(8)
    lax.fori_loop(0, PAIRS, attend_back(0), 0)
    for i in (1, 0):
        sum_y.await_over(i)
    for k in order:
        sum_o.send_over(k)
    serve_scatter(10)

    low_half = iota((T, LANES), 1) < HD

    def joined(part):
        return jnp.where(
            low_half, part(0) + pltpu.roll(part(1), HD, 1), pltpu.roll(part(2), HD, 1) + part(3)
        )

    dkv = v["dkv"]
    dkv[:, 0:LANES] = rotate_back(
        joined(lambda i: kv_acc[:, i * LANES : (i + 1) * LANES]), slice(0, T)
    ).astype(BF16)
    dkv[:, LANES : 2 * LANES] = joined(lambda i: kv_acc[:, (4 + i) * LANES : (5 + i) * LANES]).astype(BF16)
    for c in parts(0, D, 256):
        wgrad[0:D, c] = tn(hid[dq_at : dq_at + T, 0:D], normed[:, c]).astype(BF16)
        wgrad[2 * D :, c] = tn(dkv[...], normed[:, c]).astype(BF16)
    lax.fori_loop(0, R, pack_first, 0)
    sum_p.begin()
    for k in order:
        sum_p.send_over(k)
    serve_scatter(11)

    gains[1:2, :] = jnp.sum(hid[dq_at : dq_at + T, 0:D].astype(F32), axis=0, keepdims=True)
    gains[3:4, 0 : 2 * LANES] = jnp.sum(dkv[...].astype(F32), axis=0, keepdims=True)

    def close_back(i, _):
        rows = pl.ds(pl.multiple_of(i * HB, HB), HB)
        dn = nn(hid[pl.ds(pl.multiple_of(dq_at + i * HB, HB), HB), 0:D], W[WQ : WQ + D, 0:D])
        dn += nn(dkv[rows, :], W[WK : WK + 2 * KV * HD, 0:D])
        xb = v["tok"][rows, :].astype(F32)
        r1 = stats[rows, 126:127]
        gains[0:1, :] += jnp.sum(dn * xb * r1, axis=0, keepdims=True)
        scaled = dn * vec[0:1, :]
        inner = jnp.mean(scaled * xb, axis=1, keepdims=True)
        ds_out[rows, :] = ds_out[rows, :] + scaled * r1 - xb * (r1 * r1 * r1 * inner)
        return 0

    lax.fori_loop(0, 2, close_back, 0)
    keep_x = net.local(ds_out, v["x_out"])
    keep_x.start()
    sum_y.send_near()
    sum_y.keep(True)
    serve_scatter(12)
    sum_y.near.wait_recv()
    for i in (1, 0):
        sum_y.finish(i)
    sum_y.sent()
    y_out[...] = y_out[...] * stats[:, 125:126]
    keep_y = net.local(y_out, v["y_out"])
    keep_y.start()

    SG = v["SG"]

    def collect_tile(i, _):
        start = pl.multiple_of(i * ST, ST)
        first = lax.rem(iota((ST, 1), 0), 8) == 0
        total = None
        for row, width, size, offset, stride in (
            (gains[0:1, :], D, DS, 0, 1),
            (gains[1:2, :], D, DS, DS, 1),
            (gains[2:3, :], D, DS, 2 * DS, 1),
            (gains[3:4, 0:LANES], LANES, KS, 3 * DS, 2),
            (gains[3:4, LANES : 2 * LANES], LANES, KS, 3 * DS + 1, 2),
        ):
            owner, _ = owner_of(iota((1, width), 1), size)
            _, inner = owner_of(iota((width, LANES), 0), size)
            pick = (iota((width, LANES), 1) == inner * stride + offset).astype(BF16)
            full = jnp.where((row_device(start) == owner) & first, row, 0.0)
            high = full.astype(BF16)
            part = nn(high, pick) + nn((full - high.astype(F32)).astype(BF16), pick)
            total = part if total is None else total + part
        SG[pl.ds(start, ST), :] = total
        return 0

    lax.fori_loop(0, rows_n // ST, collect_tile, 0)

    def sg_rows(dev_m):
        return pl.ds(pl.multiple_of(dev_m * R * 8, 8), R * 8)

    sg_in = v["sg_in"]
    s_far = net.copy(SG.at[sg_rows(m3)], sg_in.at[0], core)
    s_near = net.copy(SG.at[sg_rows(m1)], sg_in.at[1], core)
    s_over = net.copy(SG.at[sg_rows(m2)], sg_in.at[2], beside)
    s_far.start()
    s_near.start()
    s_far.wait_recv()
    SG[sg_rows(m2), :] = SG[sg_rows(m2), :] + sg_in[0]
    s_over.start()

    def down_send():
        tmp[0:DA, :] = rD[drow(0, 0, DA), :].astype(F32) + sDA.last(
            lambda i, f: turn(v["bufA"][i], f)
        )
        tmp[DA:DP, :] = rD[drow(0, DA, DP - DA), :].astype(F32) + sDB.last(
            lambda i, f: turn(v["bufB"][i], f)
        )
        for i in range(4):
            dx[i, 0:DS, :] = tmp[i * DS : (i + 1) * DS, :].astype(BF16)
        for c in home:
            c.start()
        down_p[m] = dx[m]

    def down_home():
        for c in home:
            c.wait_recv()
        for i in range(4):
            full = turn_by_seat(down_p[i].astype(F32), True)
            for place in range(R):
                v["down_out"][:, owned_units(place, i)] = full[0:DS, place * FP : place * FP + FS]

    home = [
        net.copy(dx.at[dst_m], down_p.at[m], dev)
        for dst_m, dev in ((m1, core), (m2, beside), (m3, across))
    ]

    def small_add(k, slot, forward):
        SG[srow(m, k), :] = SG[srow(m, k), :] + v["sring"][slot]

    ssm = Scatter("A", lambda k: SG.at[srow(m, k)], v["sring"], small_add)

    def settle(s):
        for k in both(s) if s else (0,):
            sum_p.settle(k)
            sum_o.settle(k)

    settle(long_way)
    settle(long_way - 1)
    sum_p.ring.begin()
    sum_o.ring.begin()
    s_near.wait_recv()
    s_over.wait_recv()
    SG[sg_rows(m), :] = SG[sg_rows(m), :] + sg_in[1] + sg_in[2]
    ssm.begin()
    for t in range(1, long_way + 1):
        if t < long_way:
            settle(long_way - t - 1)
        for x in (sum_p.ring, sum_o.ring, ssm):
            x.serve(t)
        if t == 2:
            serve_scatter(14)
            down_send()
    mine = arow(m, 0)
    low = AW[mine, :].astype(F32)
    first = low[0:PH] + sum_p.ring.last(lambda i, f: v["ringP"][i].astype(F32))
    rest = low[PH:AR] + sum_o.ring.last(lambda i, f: v["ringO"][i].astype(F32))
    v["small_out"][...] = SG[srow(m, 0), :] + ssm.last(lambda i, f: v["sring"][i])
    v["q_out"][...] = first[0:DS]
    v["k_out"][...] = first[KO:VO]
    v["v_out"][...] = first[VO:OO]
    v["o_out"][0 : PH - OO, :] = first[OO:PH]
    v["o_out"][PH - OO : DS, :] = rest

    serve_scatter(len(scatter_steps))
    mine = slice(own * FP, own * FP + FS)
    res[0:FS, 0:D] = rG[mine, :].astype(F32) + sG.last(
        lambda i, f: v["bufG"][i, 0:FS, :].astype(F32)
    )
    res[FS : 2 * FS, 0:D] = rU[mine, :].astype(F32) + sU.last(
        lambda i, f: v["bufU"][i, 0:FS, :].astype(F32)
    )
    keep_rows = net.local(res.at[pl.ds(0, 2 * FS), pl.ds(0, D)], v["rows_out"])
    keep_rows.start()
    down_home()
    net.sent(net.open)
    for c in (keep_y, keep_x, keep_rows):
        c.wait()


def layer(geo, ins):
    R, T, D, FP, U, DSP, DP, DA = geo.R, geo.T, geo.D, geo.FP, geo.U, geo.DSP, geo.DP, geo.DA
    AR = geo.AR
    outs = {
        "y_out": ((T, D), F32),
        "x_out": ((T, D), F32),
        "rows_out": ((2 * geo.FS, D), F32),
        "q_out": ((geo.DS, D), F32),
        "k_out": ((geo.KS, D), F32),
        "v_out": ((geo.KS, D), F32),
        "o_out": ((geo.DS, D), F32),
        "down_out": ((geo.DS, R * 4 * geo.FS), F32),
        "small_out": ((8, LANES), F32),
        "spill": ((2 * D + 2 * KV * HD, D), BF16),
    }
    scratch = {
        "down_p": ((4, DSP, U), BF16),
        "y": ((T, D), F32),
        "x": ((T, D), F32),
        "dx": ((4, DSP, U), BF16),
        "AW": ((4 * R * AR, D), BF16),
        "SM": ((4 * R * 8, LANES), F32),
        "SG": ((4 * R * 8, LANES), F32),
        "sg_in": ((3, R * 8, LANES), F32),
        "sring": ((4, 8, LANES), F32),
        "ringP": ((4, geo.PH, D), BF16),
        "ringO": ((4, AR - geo.PH, D), BF16),
        "stage": ((T, D), BF16),
        "y_in": ((T, D), BF16),
        "S": ((4 * T, D), BF16),
        "dO": ((4 * T, D), BF16),
        "tmp": ((DP, U), F32),
        "tmp3": ((8 * geo.KS, D), F32),
        "Wg": ((U, D), BF16),
        "Wu": ((U, D), BF16),
        "Wd": ((D, U), BF16),
        "hid": ((4 * T, U), BF16),
        "dg": ((4 * T, U), BF16),
        "du": ((4 * T, U), BF16),
        "gG": ((U, D), BF16),
        "gU": ((U, D), BF16),
        "gD": ((D, U), BF16),
        "bufG": ((4, FP, D), BF16),
        "bufU": ((4, FP, D), BF16),
        "bufA": ((4, DA, U), BF16),
        "bufB": ((4, DP - DA, U), BF16),
        "stats": ((T, LANES), F32),
        "bias": ((T, T), BF16),
        "cos": ((T, LANES), F32),
        "sin": ((T, LANES), F32),
        "vec": ((8, D), F32),
        "gains": ((8, D), F32),
        "normed": ((T, D), BF16),
        "Q": ((T, D), BF16),
        "mixed": ((T, D), BF16),
        "KX": ((4, T, LANES), BF16),
        "VX": ((4, T, LANES), BF16),
        "res": ((T, D + LANES), F32),
        "dkv": ((T, 2 * LANES), BF16),
    }
    alias = {"W": "du"}
    names = list(ins) + list(outs) + list(scratch) + ["send_sems", "recv_sems", "local_sems"]
    vm = pl.BlockSpec(memory_space=pltpu.VMEM)
    hbm = pl.BlockSpec(memory_space=pl.ANY)

    def body(*refs):
        table = dict(zip(names, refs))
        for new, old in alias.items():
            table[new] = table[old]
        kernel_body(geo, list(table), *table.values())

    res = pl.pallas_call(
        body,
        out_shape=[jax.ShapeDtypeStruct(s, d) for s, d in outs.values()],
        in_specs=[hbm if n == "cot" else vm for n in ins],
        out_specs=[hbm if n in ("y_out", "x_out", "rows_out", "spill") else vm for n in outs],
        scratch_shapes=[pltpu.VMEM(s, d) for s, d in scratch.values()]
        + [pltpu.SemaphoreType.DMA((28 * R + 16,))] * 2
        + [pltpu.SemaphoreType.DMA((6,))],
        compiler_params=pltpu.CompilerParams(
            collective_id=0, has_side_effects=True, vmem_limit_bytes=64 * 2**20
        ),
    )(*ins.values())
    return dict(zip(outs, res))


def hand_out(geo, res):
    whole = ["y_out", "x_out", "down_out", "q_out", "k_out", "v_out", "o_out"]
    rows = res["rows_out"].shape[0] // 2
    shapes = [res[n].shape for n in whole] + [(rows, geo.D)] * 2

    def body(*refs):
        count = len(shapes)
        sources, both = refs[: count - 2], refs[count - 2]
        results, held = refs[count - 1 : 2 * count - 1], refs[2 * count - 1 : 3 * count - 1]
        sems = refs[-1]
        sources += tuple(both.at[pl.ds(i * rows, rows)] for i in range(2))
        inward = [pltpu.make_async_copy(sources[i], held[i], sems.at[0, i]) for i in range(count)]
        outward = [pltpu.make_async_copy(held[i], results[i], sems.at[1, i]) for i in range(count)]
        for c in inward:
            c.start()
        for i in range(count):
            inward[i].wait()
            outward[i].start()
        for c in outward:
            c.wait()

    hbm = pl.BlockSpec(memory_space=pltpu.HBM)
    outs = pl.pallas_call(
        body,
        out_shape=[jax.ShapeDtypeStruct(s, F32) for s in shapes],
        in_specs=[hbm] * (len(shapes) - 1),
        out_specs=[hbm] * len(shapes),
        scratch_shapes=[pltpu.VMEM(s, F32) for s in shapes]
        + [pltpu.SemaphoreType.DMA((2, len(shapes)))],
        compiler_params=pltpu.CompilerParams(vmem_limit_bytes=64 * 2**20),
    )(*[res[n] for n in whole + ["rows_out"]])
    return dict(zip(["y", "x", "down", "q", "k", "v", "o", "gate", "up"], outs))


D = 896
eps_norm = 1e-06
rope_base = 1000000.0
masked_value = -1e30


def apply_weight(left, weight):
    return lax.dot_general(
        left, weight, (((1,), (1,)), ((), ())), preferred_element_type=jnp.float32
    )


def apply_transpose(left, weight):
    return jnp.dot(left, weight, preferred_element_type=jnp.float32)


def weight_grad(grad_rows, input_rows):
    return lax.dot_general(
        grad_rows, input_rows, (((0,), (0,)), ((), ())), preferred_element_type=jnp.float32
    )


def rms_scale(field_rows):
    return lax.rsqrt(jnp.mean(field_rows * field_rows, axis=1, keepdims=True) + eps_norm)


def norm_backward(grad_rows, field_rows, scale_rows, gain_values):
    scaled = grad_rows * gain_values
    return scaled * scale_rows - field_rows * scale_rows**3 * jnp.mean(
        scaled * field_rows, axis=1, keepdims=True
    )


def rope_tables(block_segments):
    slot_index = jnp.arange(block_segments.shape[0])
    same_segment = block_segments[:, None] == block_segments[None, :]
    earlier = slot_index[None, :] < slot_index[:, None]
    positions = jnp.sum((same_segment & earlier).astype(jnp.float32), axis=1)
    frequency = jnp.exp(jnp.arange(HD // 2, dtype=jnp.float32) * (-2.0 * math.log(rope_base) / HD))
    angles = positions[:, None] * frequency[None, :]
    return (jnp.cos(angles)[:, None, :], jnp.sin(angles)[:, None, :])


def rotate(vectors, cosine_table, sine_table):
    first_half = vectors[..., : HD // 2]
    second_half = vectors[..., HD // 2 :]
    return jnp.concatenate(
        [
            first_half * cosine_table - second_half * sine_table,
            second_half * cosine_table + first_half * sine_table,
        ],
        axis=-1,
    )


def rotate_back(vectors, cosine_table, sine_table):
    first_half = vectors[..., : HD // 2]
    second_half = vectors[..., HD // 2 :]
    return jnp.concatenate(
        [
            first_half * cosine_table + second_half * sine_table,
            second_half * cosine_table - first_half * sine_table,
        ],
        axis=-1,
    )


def plain_local(
    tokens,
    segment_ids,
    live_counts,
    first_gain,
    query_weight,
    query_bias,
    key_weight,
    value_weight,
    key_value_bias,
    output_weight,
    second_gain,
    gate_weight,
    up_weight,
    down_weight,
    cotangent,
):
    attention_set = (
        lax.all_gather(first_gain, "dp", axis=0, tiled=True),
        lax.all_gather(query_weight, "dp", axis=0, tiled=True),
        lax.all_gather(query_bias, "dp", axis=0, tiled=True),
        lax.all_gather(key_weight, "dp", axis=0, tiled=True),
        lax.all_gather(value_weight, "dp", axis=0, tiled=True),
        lax.all_gather(key_value_bias, "dp", axis=0, tiled=True),
        lax.all_gather(output_weight, "dp", axis=0, tiled=True),
    )
    first_full, query_full, query_bias_full, key_full, value_full, pair_bias_full, output_full = (
        attention_set
    )
    slot_count = tokens.shape[0]
    group_size = HEADS // KV
    scale_factor = HD ** (-0.5)
    slot_index = jnp.arange(slot_count)
    live_rows = (slot_index < live_counts[0]).astype(jnp.float32)
    allowed = (segment_ids[:, None] == segment_ids[None, :]) & (
        slot_index[None, :] <= slot_index[:, None]
    ) & (live_rows[None, :] > 0.5) | (slot_index[None, :] == slot_index[:, None])
    cosine_table, sine_table = rope_tables(segment_ids)
    token_rows = tokens.astype(jnp.float32)
    first_scale = rms_scale(token_rows)
    normed = (token_rows * first_scale * first_full.astype(jnp.float32)).astype(jnp.bfloat16)
    pair_bias_values = pair_bias_full.astype(jnp.float32)
    query_pre = apply_weight(normed, query_full) + query_bias_full.astype(jnp.float32)
    key_pre = apply_weight(normed, key_full) + pair_bias_values[:, 0]
    values = (apply_weight(normed, value_full) + pair_bias_values[:, 1]).astype(jnp.bfloat16)
    values = values.reshape(slot_count, KV, HD)
    rotated_queries = rotate(query_pre.reshape(slot_count, HEADS, HD), cosine_table, sine_table)
    rotated_queries = rotated_queries.astype(jnp.bfloat16).reshape(slot_count, KV, group_size, HD)
    rotated_keys = rotate(key_pre.reshape(slot_count, KV, HD), cosine_table, sine_table).astype(
        jnp.bfloat16
    )

    def attention_logits():
        scores = jnp.einsum(
            "ikgd,jkd->kgij", rotated_queries, rotated_keys, preferred_element_type=jnp.float32
        )
        return jnp.where(allowed[None, None], scores * scale_factor, masked_value)

    logits = attention_logits()
    row_top = jnp.max(logits, axis=-1, keepdims=True)
    exponent = jnp.exp(logits - row_top)
    row_total = jnp.sum(exponent, axis=-1, keepdims=True)
    weights_low = (exponent / row_total).astype(jnp.bfloat16)
    mixed_heads = jnp.einsum(
        "kgij,jkd->ikgd", weights_low, values, preferred_element_type=jnp.float32
    )
    mixed_heads = mixed_heads.reshape(slot_count, D).astype(jnp.bfloat16)
    residual = token_rows + apply_weight(mixed_heads, output_full)
    feed_set = (
        lax.all_gather(second_gain, "dp", axis=0, tiled=True),
        lax.all_gather(gate_weight, "dp", axis=0, tiled=True),
        lax.all_gather(up_weight, "dp", axis=0, tiled=True),
        lax.all_gather(down_weight, "dp", axis=0, tiled=True),
    )
    second_full, gate_full, up_full, down_full = feed_set
    second_scale = rms_scale(residual)
    second = (residual * second_scale * second_full.astype(jnp.float32)).astype(jnp.bfloat16)
    gate_value = apply_weight(second, gate_full)
    up_value = apply_weight(second, up_full)
    hidden = (jax.nn.silu(gate_value) * up_value).astype(jnp.bfloat16)
    layer_out = (residual + apply_weight(hidden, down_full)) * live_rows[:, None]
    feed_back = (
        lax.all_gather(second_gain, "dp", axis=0, tiled=True),
        lax.all_gather(gate_weight, "dp", axis=0, tiled=True),
        lax.all_gather(up_weight, "dp", axis=0, tiled=True),
        lax.all_gather(down_weight, "dp", axis=0, tiled=True),
    )
    back_second, back_gate, back_up, back_down = feed_back
    out_grad = cotangent.astype(jnp.float32) * live_rows[:, None]
    out_grad_low = out_grad.astype(jnp.bfloat16)
    down_shard = lax.psum_scatter(
        weight_grad(out_grad_low, hidden), "dp", scatter_dimension=0, tiled=True
    )
    hidden_grad = apply_transpose(out_grad_low, back_down)
    sigmoid_gate = jax.nn.sigmoid(gate_value)
    up_grad_rows = (hidden_grad * (gate_value * sigmoid_gate)).astype(jnp.bfloat16)
    gate_grad_rows = (
        hidden_grad * up_value * sigmoid_gate * (1.0 + gate_value * (1.0 - sigmoid_gate))
    ).astype(jnp.bfloat16)
    gate_part = weight_grad(gate_grad_rows, second)
    up_part = weight_grad(up_grad_rows, second)
    gate_up_shard = lax.psum_scatter(
        jnp.concatenate([gate_part, up_part], axis=1), "dp", scatter_dimension=0, tiled=True
    )
    model_width = second.shape[1]
    gate_shard = gate_up_shard[:, :model_width]
    up_shard = gate_up_shard[:, model_width:]
    second_grad_rows = apply_transpose(gate_grad_rows, back_gate) + apply_transpose(
        up_grad_rows, back_up
    )
    second_gain_grad = jnp.sum(second_grad_rows * residual * second_scale, axis=0)
    residual_grad = out_grad + norm_backward(
        second_grad_rows, residual, second_scale, back_second.astype(jnp.float32)
    )
    attention_back = (
        lax.all_gather(first_gain, "dp", axis=0, tiled=True),
        lax.all_gather(query_weight, "dp", axis=0, tiled=True),
        lax.all_gather(query_bias, "dp", axis=0, tiled=True),
        lax.all_gather(key_weight, "dp", axis=0, tiled=True),
        lax.all_gather(value_weight, "dp", axis=0, tiled=True),
        lax.all_gather(key_value_bias, "dp", axis=0, tiled=True),
        lax.all_gather(output_weight, "dp", axis=0, tiled=True),
    )
    back_first = attention_back[0]
    back_query = attention_back[1]
    back_key = attention_back[3]
    back_value = attention_back[4]
    back_output = attention_back[6]
    branch_grad = residual_grad.astype(jnp.bfloat16)
    output_grad = weight_grad(branch_grad, mixed_heads)
    mixed_grad = apply_transpose(branch_grad, back_output).astype(jnp.bfloat16)
    mixed_grad = mixed_grad.reshape(slot_count, KV, group_size, HD)
    probs = jnp.exp(attention_logits() - row_top) / row_total
    probs_low = probs.astype(jnp.bfloat16)
    value_grad_rows = jnp.einsum(
        "kgij,ikgd->jkd", probs_low, mixed_grad, preferred_element_type=jnp.float32
    )
    prob_grad = jnp.einsum("ikgd,jkd->kgij", mixed_grad, values, preferred_element_type=jnp.float32)
    logit_grad = probs * (prob_grad - jnp.sum(probs * prob_grad, axis=-1, keepdims=True))
    score_grad = (logit_grad * scale_factor).astype(jnp.bfloat16)
    query_rot_grad = jnp.einsum(
        "kgij,jkd->ikgd", score_grad, rotated_keys, preferred_element_type=jnp.float32
    )
    key_rot_grad = jnp.einsum(
        "kgij,ikgd->jkd", score_grad, rotated_queries, preferred_element_type=jnp.float32
    )
    query_grad_rows = rotate_back(
        query_rot_grad.reshape(slot_count, HEADS, HD), cosine_table, sine_table
    )
    query_grad_rows = query_grad_rows.astype(jnp.bfloat16).reshape(slot_count, D)
    key_grad_rows = (
        rotate_back(key_rot_grad, cosine_table, sine_table)
        .astype(jnp.bfloat16)
        .reshape(slot_count, KV * HD)
    )
    value_grad_low = value_grad_rows.astype(jnp.bfloat16).reshape(slot_count, KV * HD)
    query_grad = weight_grad(query_grad_rows, normed)
    query_bias_grad = jnp.sum(query_grad_rows.astype(jnp.float32), axis=0)
    key_grad = weight_grad(key_grad_rows, normed)
    value_grad = weight_grad(value_grad_low, normed)
    pair_bias_grad = jnp.stack(
        [
            jnp.sum(key_grad_rows.astype(jnp.float32), axis=0),
            jnp.sum(value_grad_low.astype(jnp.float32), axis=0),
        ],
        axis=1,
    )
    first_grad_rows = (
        apply_transpose(query_grad_rows, back_query)
        + apply_transpose(key_grad_rows, back_key)
        + apply_transpose(value_grad_low, back_value)
    )
    first_gain_grad = jnp.sum(first_grad_rows * token_rows * first_scale, axis=0)
    input_grad = residual_grad + norm_backward(
        first_grad_rows, token_rows, first_scale, back_first.astype(jnp.float32)
    )
    attention_shards = (
        lax.psum_scatter(first_gain_grad, "dp", scatter_dimension=0, tiled=True),
        lax.psum_scatter(query_grad, "dp", scatter_dimension=0, tiled=True),
        lax.psum_scatter(query_bias_grad, "dp", scatter_dimension=0, tiled=True),
        lax.psum_scatter(key_grad, "dp", scatter_dimension=0, tiled=True),
        lax.psum_scatter(value_grad, "dp", scatter_dimension=0, tiled=True),
        lax.psum_scatter(pair_bias_grad, "dp", scatter_dimension=0, tiled=True),
        lax.psum_scatter(output_grad, "dp", scatter_dimension=0, tiled=True),
        lax.psum_scatter(second_gain_grad, "dp", scatter_dimension=0, tiled=True),
    )
    return (layer_out, input_grad) + tuple(attention_shards) + (gate_shard, up_shard, down_shard)


def fused_local(
    geo,
    tokens,
    segment_ids,
    live_counts,
    first_gain,
    query_weight,
    query_bias,
    key_weight,
    value_weight,
    key_value_bias,
    output_weight,
    second_gain,
    gate_weight,
    up_weight,
    down_weight,
    cotangent,
):
    T, DS, KS = geo.T, geo.DS, geo.KS
    live = (jnp.arange(T) < live_counts[0]).astype(F32)
    vectors = jnp.concatenate(
        [first_gain, query_bias, second_gain, key_value_bias.reshape(-1)]
    ).astype(F32)
    aux = jnp.stack(
        [segment_ids.astype(F32), live, jnp.pad(vectors, (0, T - vectors.shape[0]))]
    )
    aux = jnp.pad(aux, ((0, 5), (0, 0)))
    res = layer(
        geo,
        {
            "tok": tokens,
            "cot": cotangent,
            "wq": query_weight,
            "wo": output_weight,
            "wk": key_weight,
            "wv": value_weight,
            "gate": gate_weight,
            "up": up_weight,
            "down": down_weight,
            "aux": aux,
        },
    )
    vec = res["small_out"][0]
    out = hand_out(geo, res)
    return (
        out["y"],
        out["x"],
        vec[:DS],
        out["q"],
        vec[DS : 2 * DS],
        out["k"],
        out["v"],
        vec[3 * DS : 3 * DS + 2 * KS].reshape(KS, 2),
        out["o"],
        vec[2 * DS : 3 * DS],
        out["gate"],
        out["up"],
        out["down"],
    )


def local(tokens, segment_ids, live_counts, first_gain, *rest):
    geo = Geometry(
        lax.axis_size("dp"), tokens.shape[0], tokens.shape[1], rest[9].shape[1]
    )
    layer_of = functools.partial(fused_local, geo) if geo.fits() else plain_local
    return layer_of(tokens, segment_ids, live_counts, first_gain, *rest)


def solution(mesh):
    in_specs = (
        P("dp", None),
        P("dp"),
        P("dp"),
        P("dp"),
        P("dp", None),
        P("dp"),
        P("dp", None),
        P("dp", None),
        P("dp", None),
        P("dp", None),
        P("dp"),
        P("dp", None),
        P("dp", None),
        P("dp", None),
        P("dp", None),
    )
    out_specs = (
        P("dp", None),
        P("dp", None),
        P("dp"),
        P("dp", None),
        P("dp"),
        P("dp", None),
        P("dp", None),
        P("dp", None),
        P("dp", None),
        P("dp"),
        P("dp", None),
        P("dp", None),
        P("dp", None),
    )
    return jax.shard_map(local, mesh=mesh, in_specs=in_specs, out_specs=out_specs, check_vma=False)
```

```python
import functools
import math

import jax
import jax.numpy as jnp
from jax import lax
from jax.experimental import pallas as pl
from jax.experimental.pallas import tpu as pltpu
from jax.sharding import PartitionSpec as P

MESH = pl.DeviceIdType.MESH
F32 = jnp.float32
BF16 = jnp.bfloat16

HEADS = 14
KV = 2
HD = 64
GROUP = HEADS // KV
PAIRS = HEADS // 2
LANES = 128
EPS = 1e-06
ROPE_BASE = 1000000.0
MASKED = -1e30
SCALE = HD ** (-0.5)


def up16(n):
    return -(-n // 16) * 16


def nn(a, b):
    return jnp.dot(a, b, preferred_element_type=F32)


def nt(a, b):
    return lax.dot_general(a, b, (((1,), (1,)), ((), ())), preferred_element_type=F32)


def tn(a, b):
    return lax.dot_general(a, b, (((0,), (0,)), ((), ())), preferred_element_type=F32)


class Geometry:
    def __init__(self, devices, slots, width, hidden):
        self.n = devices
        self.R = devices // 4
        self.T = slots
        self.D = width
        self.FS = hidden // devices
        self.FP = up16(self.FS)
        self.U = self.R * self.FP
        self.DS = width // devices
        self.DSP = up16(self.DS)
        self.DP = 4 * self.DS
        self.DA = up16(self.DP // 2)
        self.KS = KV * HD // devices
        self.AR = 2 * self.DS + 2 * self.KS
        self.PH = up16(self.DS + 2 * self.KS)
        self.OFF = 1 - self.R // 2

    def fits(self):
        return (
            self.n % 32 == 0
            and self.DP % 16 == 0
            and self.AR % 16 == 0
            and self.FP % 32 == 0 and self.FS % 8 == 0
            and self.PH < self.AR
            and (4 * self.KS) % 16 == 0
            and self.U % 256 == 0
            and self.R * self.AR == self.T
            and self.R & (self.R - 1) == 0
            and 2 * self.D + 2 * KV * HD == 4 * self.T
            and 3 * self.DS + 2 * self.KS <= LANES
            and 4 * self.T * self.U * 6 <= 16 * 2**20
        )


def ring_place(g, R):
    odd = lax.rem(g, 2)
    half = lax.div(g, 2)
    return (1 - odd) * half + odd * (R - 1 - half)


def ring_group(place, R):
    high = lax.div(place, R // 2)
    return (1 - high) * (2 * place) + high * (2 * (R - 1 - place) + 1)


class Net:
    def __init__(self, send_sems, recv_sems, local_sems):
        self.send_sems, self.recv_sems, self.local_sems = send_sems, recv_sems, local_sems
        self.count = 0
        self.local_count = 0
        self.open = []
        self.index = []
        self.free = []

    def copy(self, src, dst, device):
        if self.free:
            i = self.free.pop()
        else:
            i = self.count
            self.count += 1
        made = pltpu.make_async_remote_copy(
            src_ref=src,
            dst_ref=dst,
            send_sem=self.send_sems.at[i],
            recv_sem=self.recv_sems.at[i],
            device_id=(device,),
            device_id_type=MESH,
        )
        self.open.append(made)
        self.index.append((made, i))
        return made

    def release(self, copies):
        for c in copies:
            self.free += [i for made, i in self.index if made is c]

    def sent(self, copies):
        for c in copies:
            c.wait_send()
        self.open = [x for x in self.open if all(x is not c for c in copies)]

    def local(self, src, dst):
        i = self.local_count
        self.local_count += 1
        return pltpu.make_async_copy(src, dst, self.local_sems.at[i])


def parts(lo, hi, step):
    return [slice(at, min(at + step, hi)) for at in range(lo, hi, step)]


def iota(shape, axis):
    return lax.broadcasted_iota(jnp.int32, shape, axis)


def kernel_body(geo, names, *refs):
    v = dict(zip(names, refs))
    R, T, D, FP, FS, U = geo.R, geo.T, geo.D, geo.FP, geo.FS, geo.U
    DSP, DS, DP, DA, KS, AR, PH = geo.DSP, geo.DS, geo.DP, geo.DA, geo.KS, geo.AR, geo.PH
    me = lax.axis_index("dp")
    m, g = lax.rem(me, 4), lax.div(me, 4)
    r = ring_place(g, R)

    def place_group(k):
        return ring_group(lax.rem(r + k + 2 * R, R), R)

    right = place_group(1) * 4 + m
    left = place_group(-1) * 4 + m
    m1 = m + 1 - 2 * lax.rem(m, 2)
    m2 = m + 2 - 4 * lax.div(m, 2)
    m3 = m1 + 2 - 4 * lax.div(m1, 2)
    core, beside, across = g * 4 + m1, g * 4 + m2, g * 4 + m3
    net = Net(v["send_sems"], v["recv_sems"], v["local_sems"])

    barrier = pltpu.get_barrier_semaphore()
    for peer in (right, left, core, beside, across):
        pl.semaphore_signal(barrier, inc=1, device_id=(peer,), device_id_type=MESH)

    AW, SM, tmp, aux = v["AW"], v["SM"], v["tmp"], v["aux"]
    S, dO = v["S"], v["dO"]
    Wg, Wu, Wd = v["Wg"], v["Wu"], v["Wd"]
    stats, bias = v["stats"], v["bias"]

    bring_cot = net.local(v["cot"], dO.at[pl.ds(0, T)])
    bring_cot.start()

    KO, VO, OO = DS, DS + KS, DS + 2 * KS
    tmp[0:DS, 0:D] = v["wq"][...].astype(F32)
    tmp[KO:VO, 0:D] = v["wk"][...].astype(F32)
    tmp[VO:OO, 0:D] = v["wv"][...].astype(F32)
    tmp[OO:AR, 0:D] = v["wo"][...].astype(F32)

    def arow(dev_m, k, lo=0, size=AR):
        return pl.ds(pl.multiple_of((dev_m * R + place_group(k)) * AR + lo, 16), size)

    AW[arow(m, 0), :] = tmp[0:AR, 0:D].astype(BF16)

    def srow(dev_m, k):
        return pl.ds(pl.multiple_of((dev_m * R + place_group(k)) * 8, 8), 8)

    SM[srow(m, 0), :] = jnp.where(iota((8, LANES), 0) == 0, aux[2:3, 0:LANES], 0.0)

    def jslot(k):
        return (k - geo.OFF) % R

    def unit_rows(j):
        return slice(j * FP, (j + 1) * FP)

    own = jslot(0)
    for ref, mine in ((Wg, v["gate"]), (Wu, v["up"])):
        if FP > FS:
            ref[unit_rows(own), :] = jnp.zeros((FP, D), BF16)
        ref[own * FP : own * FP + FS, :] = mine[...]

    pl.semaphore_wait(barrier, 5)

    long_way, short_way = R // 2, R // 2 - 1
    classes = {"A": (long_way, short_way), "B": (short_way, long_way)}

    class Gather:
        def __init__(self, cls, src, dst, arrive=None):
            self.nf, self.nb = classes[cls]
            self.f = [net.copy(src(-(s - 1)), dst(-s, s), right) for s in range(1, self.nf + 1)]
            self.b = [net.copy(src(s - 1), dst(s, s), left) for s in range(1, self.nb + 1)]
            self.arrive = arrive

        def begin(self):
            self.f[0].start()
            self.b[0].start()

        def serve(self, s):
            if s <= self.nf:
                self.f[s - 1].wait_recv()
            if s <= self.nb:
                self.b[s - 1].wait_recv()
            if self.arrive and s <= self.nf:
                self.arrive(-s, s)
            if self.arrive and s <= self.nb:
                self.arrive(s, s)
            if s < self.nf:
                self.f[s].start()
            if s < self.nb:
                self.b[s].start()

    def nearer(k):
        return k + 1 if k < 0 else k - 1

    class Fan:
        def __init__(self, cls, lo, size):
            def at(dev_m, k):
                return AW.at[arow(dev_m, k, lo, size)]

            self.ring = Gather(cls, lambda k: at(m, k), lambda k, s: at(m, nearer(k)))
            self.beside = {k: net.copy(at(m, k), at(m, k), beside) for k in ks}
            self.core = {k: net.copy(at(m, k), at(m, k), core) for k in ks}
            self.on = {k: net.copy(at(m2, k), at(m2, k), core) for k in ks}

        def out(self, k):
            self.beside[k].start()
            self.core[k].start()

        def forward(self, k):
            self.beside[k].wait_recv()
            self.on[k].start()

        def arrived(self):
            for k in ks:
                self.core[k].wait_recv()
                self.on[k].wait_recv()

        def copies(self):
            within = [c for d in (self.beside, self.core, self.on) for c in d.values()]
            return self.ring.f + self.ring.b + within

    def both(s):
        return [-s, s] if s < long_way else [s]

    ks = [0] + [k for s in range(1, long_way + 1) for k in both(s)]
    fan_p, fan_o = Fan("A", 0, PH), Fan("B", PH, AR - PH)
    gsm = Gather("A", lambda k: SM.at[srow(m, k)], lambda k, s: SM.at[srow(m, nearer(k))])

    def small_rows(dev_m):
        return SM.at[pl.ds(pl.multiple_of(dev_m * R * 8, 8), R * 8)]

    small_beside = net.copy(small_rows(m), small_rows(m), beside)
    small_core = net.copy(small_rows(m), small_rows(m), core)
    small_on = net.copy(small_rows(m2), small_rows(m2), core)
    attn_copies = fan_p.copies() + fan_o.copies() + gsm.f + gsm.b
    attn_copies += [small_beside, small_core, small_on]

    def drow(k, lo=0, size=DP):
        return pl.ds(pl.multiple_of(place_group(k) * DP + lo, 16), size)

    def turn(block, forward):
        return pltpu.roll(block.astype(F32), U - FP if forward else FP, 1)

    def box(s, forward):
        return (s % 2) * 2 + (0 if forward else 1)

    def down_gather(cls, buf, lo, size):
        def arrive(k, s):
            Wd[drow(k, lo, size), :] = turn(buf[box(s, k < 0)], k < 0).astype(BF16)

        return Gather(
            cls, lambda k: Wd.at[drow(k, lo, size)], lambda k, s: buf.at[box(s, k < 0)], arrive
        )

    def unit_gather(cls, ref, lo):
        def at(k):
            return ref.at[pl.ds(jslot(k) * FP + lo, FP // 2)]

        return Gather(cls, at, lambda k, s: at(k))

    gDA = down_gather("A", v["bufA"], 0, DA)
    gDB = down_gather("B", v["bufB"], DA, DP - DA)
    unit_pieces = [
        unit_gather("A", Wg, 0),
        unit_gather("B", Wg, FP // 2),
        unit_gather("A", Wu, 0),
        unit_gather("B", Wu, FP // 2),
    ]

    def serve_units(s):
        for x in unit_pieces:
            x.serve(s)

    def serve_down(s):
        gDA.serve(s)
        gDB.serve(s)

    def serve_attention(s):
        fan_p.ring.serve(s)
        fan_o.ring.serve(s)
        gsm.serve(s)

    fan_p.ring.begin()
    fan_o.ring.begin()
    gsm.begin()
    fan_p.out(0)
    unit_pieces[0].begin()

    seat = lax.rem(r + geo.OFF + R, R)

    def turn_by_seat(block, back):
        b = 1
        while b < R:
            odd = lax.rem(lax.div(seat, b), 2) == 1
            block = jnp.where(odd, pltpu.roll(block, b * FP if back else U - b * FP, 1), block)
            b *= 2
        return block

    def owned_units(place, i):
        half = R // 2
        group = 2 * place if place < half else 2 * (R - 1 - place) + 1
        return slice((4 * group + i) * FS, (4 * group + i + 1) * FS)

    down_p, dx = v["down_p"], v["dx"]
    for i in range(4):
        for place in range(R):
            rows = slice(i * DS, (i + 1) * DS)
            if FP > FS:
                tmp[rows, place * FP + FS : (place + 1) * FP] = jnp.zeros((DS, FP - FS), F32)
            tmp[rows, place * FP : place * FP + FS] = v["down"][:, owned_units(place, i)].astype(F32)
    tmp[...] = turn_by_seat(tmp[...], False)
    for i in range(4):
        down_p[i, 0:DS, :] = tmp[i * DS : (i + 1) * DS, :].astype(BF16)
    down_copies = [
        net.copy(down_p.at[dst_m], dx.at[m], dev)
        for dst_m, dev in ((m1, core), (m2, beside), (m3, across))
    ]
    for c in down_copies:
        c.start()

    frequency = jnp.exp(
        lax.rem(iota((1, LANES), 1), HD // 2).astype(F32) * (-2.0 * math.log(ROPE_BASE) / HD)
    )
    PT = 128

    def prepare(i, _):
        start = pl.multiple_of(i * PT, PT)
        rows = pl.ds(start, PT)
        seg_row, live_row = aux[0:1, :], aux[1:2, :]
        ii, jj = iota((PT, T), 0) + start, iota((PT, T), 1)
        seg_col = jnp.sum(jnp.where(ii == jj, seg_row, 0.0), axis=1, keepdims=True)
        live_col = jnp.sum(jnp.where(ii == jj, live_row, 0.0), axis=1, keepdims=True)
        same = seg_col == seg_row
        position = jnp.sum(jnp.where(same & (jj < ii), 1.0, 0.0), axis=1, keepdims=True)
        allowed = (same & (jj <= ii) & (live_row > 0.5)) | (ii == jj)
        bias[rows, :] = jnp.where(allowed, 0.0, MASKED).astype(BF16)
        dO[rows, :] = (dO[rows, :].astype(F32) * live_col).astype(BF16)
        lane = iota((PT, LANES), 1)
        angles = position * frequency
        v["cos"][rows, :] = jnp.cos(angles)
        sine = jnp.sin(angles)
        v["sin"][rows, :] = jnp.where(lax.rem(lane, HD) < HD // 2, -sine, sine)
        x = v["tok"][rows, :].astype(F32)
        r1 = lax.rsqrt(jnp.mean(x * x, axis=1, keepdims=True) + EPS)
        stats[rows, :] = jnp.where(lane == 126, r1, jnp.where(lane == 125, live_col, 0.0))
        return 0

    bring_cot.wait()
    serve_attention(1)
    for k in both(1):
        fan_p.out(k)
    unit_pieces[1].begin()
    lax.fori_loop(0, T // PT // 2, prepare, 0)
    fan_p.forward(0)
    fan_o.out(0)
    for s in range(2, long_way + 1):
        serve_attention(s)
        for k in both(s):
            fan_p.out(k)
        for k in both(s - 1):
            fan_o.out(k)
        if s == 2:
            unit_pieces[2].begin()
            lax.fori_loop(T // PT // 2, T // PT, prepare, 0)
        if s == 3:
            unit_pieces[3].begin()
            dx[m] = down_p[m]
            for c in down_copies:
                c.wait_recv()
            for i in range(4):
                tmp[i * DS : (i + 1) * DS, :] = dx[i].astype(F32)[0:DS, :]
            Wd[drow(0), :] = tmp[0:DP, :].astype(BF16)
            net.sent(down_copies)
        for k in both(s - 1):
            fan_p.forward(k)
    gDA.begin()
    gDB.begin()

    PX = T // 2

    class GroupGather:
        def __init__(self, buf):
            def at(q, i):
                return buf.at[pl.ds(q * T + i * PX, PX)]

            self.beside = [net.copy(at(0, i), at(2, i), beside) for i in range(2)]
            self.core = [net.copy(at(0, i), at(1, i), core) for i in range(2)]
            self.on = [net.copy(at(2, i), at(3, i), core) for i in range(2)]

        def out(self, i):
            self.beside[i].start()
            self.core[i].start()

        def forward(self):
            for i in range(2):
                self.beside[i].wait_recv()
                self.on[i].start()

        def copies(self):
            return self.beside + self.core + self.on

    gS, gO = GroupGather(S), GroupGather(dO)
    small_beside.start()
    small_core.start()
    for k in both(long_way):
        fan_o.out(k)
    gO.out(0)
    gO.out(1)
    for k in both(long_way):
        fan_p.forward(k)
    small_beside.wait_recv()
    small_on.start()
    fan_p.arrived()
    small_core.wait_recv()
    small_on.wait_recv()

    serve_down(1)

    W, tmp3 = v["W"], v["tmp3"]
    WQ, WO, WK, WV = 0, D, 2 * D, 2 * D + KV * HD
    K4 = 4 * KS

    def unpack_first(gi, _):
        for i in range(4):
            at = pl.ds(pl.multiple_of((i * R + gi) * AR, 16), PH)
            rows = AW[at, :].astype(F32)
            tmp[i * DS : (i + 1) * DS, 0:D] = rows[0:DS]
            tmp3[i * KS : (i + 1) * KS, :] = rows[KO:VO]
            tmp3[K4 + i * KS : K4 + (i + 1) * KS, :] = rows[VO:OO]
        W[pl.ds(pl.multiple_of(WQ + gi * DP, 16), DP), 0:D] = tmp[0:DP, 0:D].astype(BF16)
        W[pl.ds(pl.multiple_of(WK + gi * K4, 16), K4), 0:D] = tmp3[0:K4, :].astype(BF16)
        W[pl.ds(pl.multiple_of(WV + gi * K4, 16), K4), 0:D] = tmp3[K4:, :].astype(BF16)
        return 0

    OB = OO // 16 * 16

    def unpack_output(gi, _):
        for i in range(4):
            at = pl.ds(pl.multiple_of((i * R + gi) * AR + OB, 16), AR - OB)
            tmp[i * DS : (i + 1) * DS, 0:D] = AW[at, :].astype(F32)[OO - OB : AR - OB]
        W[pl.ds(pl.multiple_of(WO + gi * DP, 16), DP), 0:D] = tmp[0:DP, 0:D].astype(BF16)
        return 0

    lax.fori_loop(0, R, unpack_first, 0)

    rows_n = 4 * R * 8
    ST = 64

    def owner_of(lanes, size):
        block = jnp.floor((lanes.astype(F32) + 0.5) * (1.0 / size)).astype(jnp.int32)
        return block, lanes - block * size

    def row_device(start):
        i = lax.div(iota((ST, 1), 0) + start, 8)
        return lax.rem(i, R) * 4 + lax.div(i, R)

    def spread(width, size, offset, stride):
        owner, inner = owner_of(iota((1, width), 1), size)
        pick = (iota((LANES, width), 0) == inner * stride + offset).astype(BF16)

        def tile(i, total):
            start = pl.multiple_of(i * ST, ST)
            full = nn(SM[pl.ds(start, ST), :].astype(BF16), pick)
            full = jnp.where(row_device(start) == owner, full, 0.0)
            return total + jnp.sum(full, axis=0, keepdims=True)

        return lax.fori_loop(0, rows_n // ST, tile, jnp.zeros((1, width), F32))

    vec = v["vec"]
    vec[0:1, :] = spread(D, DS, 0, 1)
    vec[1:2, :] = spread(D, DS, DS, 1)
    vec[2:3, :] = spread(D, DS, 2 * DS, 1)
    vec[3:4, 0:LANES] = spread(LANES, KS, 3 * DS, 2)
    vec[4:5, 0:LANES] = spread(LANES, KS, 3 * DS + 1, 2)

    cosine, sine = v["cos"], v["sin"]
    normed, Q, mixed = v["normed"], v["Q"], v["mixed"]
    KX, VX, res = v["KX"], v["VX"], v["res"]

    def swap_halves(block):
        lanes = iota(block.shape, 1)
        return jnp.where(
            lax.rem(lanes, HD) < HD // 2,
            pltpu.roll(block, LANES - HD // 2, 1),
            pltpu.roll(block, HD // 2, 1),
        )

    def rotate(block, rows):
        return block * cosine[rows, :] + swap_halves(block) * sine[rows, :]

    def rotate_back(block, rows):
        return block * cosine[rows, :] - swap_halves(block) * sine[rows, :]

    HB = T // 2

    def project(i, _):
        rows = pl.ds(pl.multiple_of(i * HB, HB), HB)
        xb = v["tok"][rows, :].astype(F32)
        nb = (xb * stats[rows, 126:127] * vec[0:1, :]).astype(BF16)
        normed[rows, :] = nb
        q = nt(nb, W[WQ : WQ + D, 0:D]) + vec[1:2, :]
        for p in range(PAIRS):
            lanes = slice(p * LANES, (p + 1) * LANES)
            Q[rows, lanes] = rotate(q[:, lanes], rows).astype(BF16)
        key = rotate(nt(nb, W[WK : WK + KV * HD, 0:D]) + vec[3:4, 0:LANES], rows)
        value = nt(nb, W[WV : WV + KV * HD, 0:D]) + vec[4:5, 0:LANES]
        low_half = iota((HB, LANES), 1) < HD
        for ref, full in ((KX, key), (VX, value)):
            other = pltpu.roll(full, HD, 1)
            ref[0, rows, :] = jnp.where(low_half, full, 0.0).astype(BF16)
            ref[1, rows, :] = jnp.where(low_half, 0.0, other).astype(BF16)
            ref[2, rows, :] = jnp.where(low_half, other, 0.0).astype(BF16)
            ref[3, rows, :] = jnp.where(low_half, 0.0, full).astype(BF16)
        return 0

    lax.fori_loop(0, 2, project, 0)
    unit_pieces[0].serve(1)
    for k in ks:
        fan_o.forward(k)

    def head_index(p, odd):
        h = 2 * p + odd
        return h, lax.div(h, GROUP) * 2 + odd

    def scores(q_pair, idx, rb, cols):
        s = nt(q_pair, KX[idx, 0:cols, :])
        return s * SCALE + bias[rb * HB : (rb + 1) * HB, 0:cols].astype(F32)

    def attend(p, _):
        lanes = pl.ds(pl.multiple_of(p * LANES, LANES), LANES)
        for rb in range(2):
            rows, cols = slice(rb * HB, (rb + 1) * HB), (rb + 1) * HB
            q_pair = Q[rows, lanes]
            total = None
            for odd in range(2):
                h, idx = head_index(p, odd)
                s = scores(q_pair, idx, rb, cols)
                top = jnp.max(s, axis=1, keepdims=True)
                e = jnp.exp(s - top)
                norm = jnp.sum(e, axis=1, keepdims=True)
                low = (e * (1.0 / norm)).astype(BF16)
                part = nn(low, VX[idx, 0:cols, :])
                total = part if total is None else total + part
                lse = top + jnp.log(norm)
                stats[rows, :] = jnp.where(iota((HB, LANES), 1) == h, lse, stats[rows, :])
            mixed[rows, lanes] = total.astype(BF16)
        return 0

    lax.fori_loop(0, PAIRS // 2, attend, 0)
    serve_down(2)
    lax.fori_loop(PAIRS // 2, PAIRS, attend, 0)
    unit_pieces[1].serve(1)
    fan_o.arrived()
    lax.fori_loop(0, R, unpack_output, 0)
    net.sent(attn_copies)

    for i in range(2):
        rows = slice(i * HB, (i + 1) * HB)
        out = v["tok"][rows, :].astype(F32) + nt(mixed[rows, :], W[WO : WO + D, 0:D])
        res[rows, 0:D] = out
        r2 = lax.rsqrt(jnp.mean(out * out, axis=1, keepdims=True) + EPS)
        stats[rows, :] = jnp.where(iota((HB, LANES), 1) == 127, r2, stats[rows, :])
        S[rows, :] = (out * r2 * vec[2:3, :]).astype(BF16)
        gS.out(i)
    keep_w = net.local(W.at[:, pl.ds(0, D)], v["spill"])
    keep_w.start()
    serve_down(3)
    for x in unit_pieces[2:]:
        x.serve(1)
    gO.forward()
    serve_down(4)
    for d in range(5, long_way + 1):
        serve_down(d)
    keep_w.wait()
    for c in gO.core + gO.on + gS.core:
        c.wait_recv()

    hid, dg, du = v["hid"], v["dg"], v["du"]
    TT, CT = 512, 256

    def unit_tile(first, stride, i):
        return pl.ds(pl.multiple_of((first + stride * i) * CT, CT), CT)

    def phase_one(first, stride, count, lo, hi):
        down_n = (hi - lo) // TT

        def tile(i, _):
            rows = pl.ds(pl.multiple_of(lo + lax.rem(i, down_n) * TT, TT), TT)
            cols = unit_tile(first, stride, lax.div(i, down_n))
            s_rows, o_rows = S[rows, :], dO[rows, :]
            gate = nt(s_rows, Wg[cols, :])
            up = nt(s_rows, Wu[cols, :])
            dh = nn(o_rows, Wd[:, cols])
            sg = jax.nn.sigmoid(gate)
            gs = gate * sg
            hid[rows, cols] = (gs * up).astype(BF16)
            du[rows, cols] = (dh * gs).astype(BF16)
            dg[rows, cols] = (dh * up * (sg + gs * (1.0 - sg))).astype(BF16)
            return 0

        lax.fori_loop(0, count * down_n, tile, 0)

    rG, rU, rD = v["gG"], v["gU"], v["gD"]

    def unit_grads(first, stride, count, lo=0, hi=4 * T, add=False, targets="GU"):
        def tile(i, _):
            cols = unit_tile(first, stride, i)
            for name, ref, left in (("G", rG, dg), ("U", rU, du)):
                if name in targets:
                    value = tn(left[lo:hi, cols], S[lo:hi, :])
                    if add:
                        value = value + ref[cols, :].astype(F32)
                    ref[cols, :] = value.astype(BF16)
            return 0

        lax.fori_loop(0, count, tile, 0)

    def need(t):
        return max(abs(j + geo.OFF) for j in range(t * CT // FP, ((t + 1) * CT - 1) // FP + 1))

    tiles = sorted(range(U // CT), key=need)
    runs = []
    for t in tiles:
        if runs and runs[-1][3] == need(t):
            first, stride, count, step = runs[-1]
            if count == 1 or t - first == stride * count:
                runs[-1] = (first, t - first if count == 1 else stride, count + 1, step)
                continue
        runs.append((t, 1, 1, need(t)))
    early = [x for x in runs if x[3] < long_way - 1]
    middle = [x for x in runs if x[3] == long_way - 1]
    late = [x for x in runs if x[3] == long_way]
    for x in unit_pieces[:2]:
        x.serve(2)
    for run in early[:-1]:
        phase_one(*run[:3], 0, 2 * T)
    for x in unit_pieces[2:]:
        x.serve(2)
    for step in range(3, long_way - 1):
        serve_units(step)
    phase_one(*early[-1][:3], 0, 2 * T)
    for run in early:
        unit_grads(*run[:3], 0, 2 * T)
    for x in unit_pieces[:2]:
        x.serve(long_way - 1)
    gS.forward()
    for c in gS.on:
        c.wait_recv()
    for run in early:
        phase_one(*run[:3], 2 * T, 4 * T)
    for x in unit_pieces[2:]:
        x.serve(long_way - 1)
    for run in middle:
        phase_one(*run[:3], 0, 2 * T)
    serve_units(long_way)
    for run in late:
        phase_one(*run[:3], 0, 4 * T)
    for run in late:
        unit_grads(*run[:3])

    net.release(attn_copies)

    class Scatter:
        def __init__(self, cls, at, buf, add):
            self.nf, self.nb = classes[cls]
            self.at, self.buf, self.add = at, buf, add
            nf, nb = self.nf, self.nb
            self.f = [net.copy(at(nf - t + 1), buf.at[box(t, True)], right) for t in range(1, nf + 1)]
            self.b = [net.copy(at(-(nb - t + 1)), buf.at[box(t, False)], left) for t in range(1, nb + 1)]

        def begin_long(self):
            (self.f if self.nf > self.nb else self.b)[0].start()

        def begin_short(self):
            (self.b if self.nf > self.nb else self.f)[0].start()

        def begin(self):
            self.begin_long()
            self.begin_short()

        def serve(self, t):
            nf, nb = self.nf, self.nb
            if t <= nf:
                self.f[t - 1].wait_recv()
            if t <= nb:
                self.b[t - 1].wait_recv()
            if t < nf:
                self.add(nf - t, box(t, True), True)
            if t < nb:
                self.add(-(nb - t), box(t, False), False)
            if t < nf:
                self.f[t].start()
            if t < nb:
                self.b[t].start()

        def last(self, value):
            return value(box(self.nf, True), True) + value(box(self.nb, False), False)

    def unit_scatter(cls, grad, buf):
        def at(k):
            return grad.at[pl.ds(jslot(k) * FP, FP)]

        def add(k, slot, forward):
            rows = unit_rows(jslot(k))
            grad[rows, :] = (grad[rows, :].astype(F32) + buf[slot].astype(F32)).astype(BF16)

        return Scatter(cls, at, buf, add)

    def down_scatter(cls, grad, buf, lo, size):
        def add(k, slot, forward):
            rows = drow(k, lo, size)
            grad[rows, :] = (grad[rows, :].astype(F32) + turn(buf[slot], forward)).astype(BF16)

        return Scatter(cls, lambda k: grad.at[drow(k, lo, size)], buf, add)

    sG = unit_scatter("A", rG, v["bufG"])
    sU = unit_scatter("B", rU, v["bufU"])
    sDA = down_scatter("A", rD, v["bufA"], 0, DA)
    sDB = down_scatter("B", rD, v["bufB"], DA, DP - DA)
    scatter_steps = [(sG, 1), (sU, 1), (sG, 2), (sDA, 1), (sDB, 1), (sU, 2), (sDA, 2), (sDB, 2)]
    for t in range(3, long_way):
        scatter_steps += [(sG, t), (sU, t), (sDA, t), (sDB, t)]
    scatter_steps += [(sDA, long_way), (sDB, long_way), (sG, long_way), (sU, long_way)]
    scatter_done = [0]

    def serve_scatter(upto):
        while scatter_done[0] < min(upto, len(scatter_steps)):
            x, t = scatter_steps[scatter_done[0]]
            x.serve(t)
            scatter_done[0] += 1

    sG.begin_long()
    sU.begin_long()
    mid = [first + stride * i for first, stride, count, _ in middle for i in range(count)]
    phase_one(mid[0], 1, 1, 2 * T, 4 * T)
    unit_grads(mid[0], 1, 1, targets="G")
    sG.begin_short()
    for t in mid[1:]:
        phase_one(t, 1, 1, 2 * T, 4 * T)
        unit_grads(t, 1, 1, targets="U")
    sU.begin_short()

    def block(ref, i):
        return ref.at[pl.ds(i * T, T)]

    class GroupSum:
        def __init__(self, stages, inbox, part, out):
            self.stages, self.inbox, self.part, self.out = stages, inbox, part, out
            self.far = net.copy(stages[0], inbox[0], core)
            self.over = [
                net.copy(stages[1].at[pl.ds(i * HB, HB)], inbox[1].at[pl.ds(i * HB, HB)], beside)
                for i in range(2)
            ]
            self.near = net.copy(stages[2], inbox[2], core)
            self.over_open = [True, True]

        def fill(self, q, stage):
            for c in parts(0, D, 512):
                stage[:, c] = self.part(q, c).astype(BF16)

        def send_far(self):
            self.fill(3, self.stages[0])
            self.far.start()

        def send_over(self, before=None):
            stage, inbox = self.stages[1], self.inbox[0]
            self.fill(2, stage)
            self.far.wait_recv()
            for i in (1, 0):
                rows = slice(i * HB, (i + 1) * HB)
                stage[rows, :] = (stage[rows, :].astype(F32) + inbox[rows, :].astype(F32)).astype(BF16)
                if before is not None:
                    net.sent(before)
                    before = None
                self.over[i].start()

        def send_near(self):
            self.fill(1, self.stages[2])
            self.near.start()

        def keep(self, more=False):
            for c in parts(0, D, 512):
                value = self.part(0, c)
                self.out[:, c] = self.out[:, c] + value if more else value

        def await_over(self, i):
            if self.over_open[i]:
                self.over_open[i] = False
                self.over[i].wait_recv()

        def finish(self, i):
            rows = slice(i * HB, (i + 1) * HB)
            self.await_over(i)
            total = self.out[rows, :] + self.inbox[1][rows, :].astype(F32)
            self.out[rows, :] = total + self.inbox[2][rows, :].astype(F32)

        def sent(self):
            net.sent([c for c in net.open if any(c is x for x in [self.far, self.near] + self.over)])

    def ds_part(q, c):
        rows = slice(q * T, (q + 1) * T)
        return nn(dg[rows, :], Wg[:, c]) + nn(du[rows, :], Wu[:, c])

    def y_part(q, c):
        rows = slice(q * T, (q + 1) * T)
        return nt(hid[rows, :], Wd[c, :])

    y_out, ds_out = v["y"], v["x"]
    sum_ds = GroupSum(
        [block(AW, 3), v["stage"], block(S, 1)], [block(AW, i) for i in range(3)], ds_part, ds_out
    )
    sum_y = GroupSum(
        [block(dO, 3), block(dO, 2), block(dO, 1)],
        [dg.at[pl.ds(3 * T, T), pl.ds(0, D)], v["y_in"], dg.at[pl.ds(0, T), pl.ds(0, D)]],
        y_part,
        y_out,
    )
    sum_ds.send_far()
    sum_ds.send_over()
    for run in early:
        unit_grads(*run[:3], 2 * T, 4 * T, add=True)
    unit_grads(mid[0], 1, 1, targets="U")
    for t in mid[1:]:
        unit_grads(t, 1, 1, targets="G")
    serve_scatter(2)
    for part in (slice(0, 256), slice(256, 512), slice(512, D)):
        rD[part, :] = tn(dO[:, part], hid[...]).astype(BF16)
    sDA.begin()
    sDB.begin()
    net.sent(gS.copies() + gO.copies())
    sum_ds.send_near()
    sum_ds.keep()
    back_w = net.local(v["spill"], W.at[:, pl.ds(0, D)])
    back_w.start()
    sum_ds.near.wait_recv()
    sum_y.send_far()
    sum_y.send_over(sum_ds.over)
    y_out[...] = res[:, 0:D]
    kv_acc = res
    kv_acc[...] = jnp.zeros_like(kv_acc)

    dm_at, dq_at, low_at = 2 * T, 3 * T, 3 * T
    gains = v["gains"]
    gains[...] = jnp.zeros_like(gains)

    def open_back(i):
        rows = slice(i * HB, (i + 1) * HB)
        r2 = stats[rows, 127:128]
        resid, dsec = y_out[rows, :], ds_out[rows, :]
        gains[2:3, :] += jnp.sum(dsec * resid * r2, axis=0, keepdims=True)
        scaled = dsec * vec[2:3, :]
        inner = jnp.mean(scaled * resid, axis=1, keepdims=True)
        dres = dO[rows, :].astype(F32) + scaled * r2 - resid * (r2 * r2 * r2 * inner)
        ds_out[rows, :] = dres
        low = dres.astype(BF16)
        dg[low_at + i * HB : low_at + (i + 1) * HB, 0:D] = low
        hid[dm_at + i * HB : dm_at + (i + 1) * HB, 0:D] = nn(low, W[WO : WO + D, 0:D]).astype(BF16)

    def attend_back(rb):
        rows, cols = slice(rb * HB, (rb + 1) * HB), (rb + 1) * HB

        def pair(p, _):
            lanes = pl.ds(pl.multiple_of(p * LANES, LANES), LANES)
            q_pair, dm = Q[rows, lanes], hid[dm_at + rb * HB : dm_at + (rb + 1) * HB, lanes]
            total = None
            for odd in range(2):
                h, idx = head_index(p, odd)
                lse = jnp.sum(
                    jnp.where(iota((HB, LANES), 1) == h, stats[rows, :], 0.0), axis=1, keepdims=True
                )
                prob = jnp.exp(scores(q_pair, idx, rb, cols) - lse)
                dp = nt(dm, VX[idx, 0:cols, :])
                t = prob * dp
                delta = jnp.sum(t, axis=1, keepdims=True)
                ds = ((t - prob * delta) * SCALE).astype(BF16)
                k_lanes = pl.ds(pl.multiple_of(idx * LANES, LANES), LANES)
                v_lanes = pl.ds(pl.multiple_of((4 + idx) * LANES, LANES), LANES)
                kv_acc[0:cols, v_lanes] += tn(prob.astype(BF16), dm)
                kv_acc[0:cols, k_lanes] += tn(ds, q_pair)
                part = nn(ds, KX[idx, 0:cols, :])
                total = part if total is None else total + part
            hid[dq_at + rb * HB : dq_at + (rb + 1) * HB, lanes] = rotate_back(total, rows).astype(BF16)
            return 0

        return pair

    serve_scatter(4)
    sum_ds.finish(1)
    back_w.wait()
    open_back(1)
    lax.fori_loop(0, PAIRS // 2, attend_back(1), 0)
    serve_scatter(6)
    lax.fori_loop(PAIRS // 2, PAIRS, attend_back(1), 0)
    sum_ds.finish(0)
    sum_ds.sent()
    open_back(0)
    wgrad = S
    for c in parts(0, D, 256):
        wgrad[D : 2 * D, c] = tn(dg[low_at : low_at + T, 0:D], mixed[:, c]).astype(BF16)

    def pack_first(gi, _):
        q_rows = wgrad[pl.ds(pl.multiple_of(gi * DP, 16), DP), :].astype(F32)
        o_rows = wgrad[pl.ds(pl.multiple_of(D + gi * DP, 16), DP), :].astype(F32)
        k_rows = wgrad[pl.ds(pl.multiple_of(WK + gi * K4, 16), K4), :].astype(F32)
        v_rows = wgrad[pl.ds(pl.multiple_of(WV + gi * K4, 16), K4), :].astype(F32)
        for i in range(4):
            tmp[0:DS, 0:D] = q_rows[i * DS : (i + 1) * DS]
            tmp[KO:VO, 0:D] = k_rows[i * KS : (i + 1) * KS]
            tmp[VO:OO, 0:D] = v_rows[i * KS : (i + 1) * KS]
            tmp[OO:PH, 0:D] = o_rows[i * DS : i * DS + PH - OO]
            AW[pl.ds(pl.multiple_of((i * R + gi) * AR, 16), PH), :] = tmp[0:PH, 0:D].astype(BF16)
        return 0

    def pack_rest(gi, _):
        o_rows = wgrad[pl.ds(pl.multiple_of(D + gi * DP, 16), DP), :].astype(F32)
        for i in range(4):
            tmp[0 : AR - PH, 0:D] = o_rows[i * DS + PH - OO : (i + 1) * DS]
            AW[pl.ds(pl.multiple_of((i * R + gi) * AR + PH, 16), AR - PH), :] = tmp[
                0 : AR - PH, 0:D
            ].astype(BF16)
        return 0

    def inbox_rows(i, k, lo, size):
        at = pl.multiple_of(T + (i * R + place_group(k)) * AR + lo, 16)
        return pl.ds(at, size)

    order = [k for s in range(long_way, 0, -1) for k in both(s)] + [0]

    class AttentionSum:
        def __init__(self, cls, lo, size, ring):
            self.lo, self.size = lo, size

            def at(dev_m, k):
                return AW.at[arow(dev_m, k, lo, size)]

            def inbox(i, k):
                if i == 2:
                    return v["stage"].at[self.rows(k)]
                return dg.at[inbox_rows(i, k, lo, size), pl.ds(0, D)]

            self.far = {k: net.copy(at(m3, k), inbox(0, k), core) for k in order}
            self.near = {k: net.copy(at(m1, k), inbox(1, k), core) for k in order}
            self.over = {k: net.copy(at(m2, k), inbox(2, k), beside) for k in order}

            def add(k, slot, forward):
                rows = arow(m, k, lo, size)
                AW[rows, :] = (AW[rows, :].astype(F32) + ring[slot].astype(F32)).astype(BF16)

            self.ring = Scatter(cls, lambda k: at(m, k), ring, add)

        def rows(self, k):
            return pl.ds(pl.multiple_of(place_group(k) * AR + self.lo, 16), self.size)

        def begin(self):
            for k in order:
                self.far[k].start()
            for k in order:
                self.near[k].start()

        def send_over(self, k):
            self.far[k].wait_recv()
            rows = arow(m2, k, self.lo, self.size)
            got = dg[inbox_rows(0, k, self.lo, self.size), 0:D]
            AW[rows, :] = (AW[rows, :].astype(F32) + got.astype(F32)).astype(BF16)
            self.over[k].start()

        def settle(self, k):
            self.near[k].wait_recv()
            self.over[k].wait_recv()
            rows = arow(m, k, self.lo, self.size)
            total = AW[rows, :].astype(F32)
            total = total + dg[inbox_rows(1, k, self.lo, self.size), 0:D].astype(F32)
            total = total + v["stage"][self.rows(k), :].astype(F32)
            AW[rows, :] = total.astype(BF16)

    sum_p = AttentionSum("A", 0, PH, v["ringP"])
    sum_o = AttentionSum("B", PH, AR - PH, v["ringO"])
    lax.fori_loop(0, R, pack_rest, 0)
    sum_o.begin()
    serve_scatter(8)
    lax.fori_loop(0, PAIRS, attend_back(0), 0)
    for i in (1, 0):
        sum_y.await_over(i)
    for k in order:
        sum_o.send_over(k)
    serve_scatter(10)

    low_half = iota((T, LANES), 1) < HD

    def joined(part):
        return jnp.where(
            low_half, part(0) + pltpu.roll(part(1), HD, 1), pltpu.roll(part(2), HD, 1) + part(3)
        )

    dkv = v["dkv"]
    dkv[:, 0:LANES] = rotate_back(
        joined(lambda i: kv_acc[:, i * LANES : (i + 1) * LANES]), slice(0, T)
    ).astype(BF16)
    dkv[:, LANES : 2 * LANES] = joined(lambda i: kv_acc[:, (4 + i) * LANES : (5 + i) * LANES]).astype(BF16)
    for c in parts(0, D, 256):
        wgrad[0:D, c] = tn(hid[dq_at : dq_at + T, 0:D], normed[:, c]).astype(BF16)
        wgrad[2 * D :, c] = tn(dkv[...], normed[:, c]).astype(BF16)
    lax.fori_loop(0, R, pack_first, 0)
    sum_p.begin()
    for k in order[:3]:
        sum_p.send_over(k)

    gains[1:2, :] = jnp.sum(hid[dq_at : dq_at + T, 0:D].astype(F32), axis=0, keepdims=True)
    gains[3:4, 0 : 2 * LANES] = jnp.sum(dkv[...].astype(F32), axis=0, keepdims=True)

    def close_back(i, _):
        rows = pl.ds(pl.multiple_of(i * HB, HB), HB)
        dn = nn(hid[pl.ds(pl.multiple_of(dq_at + i * HB, HB), HB), 0:D], W[WQ : WQ + D, 0:D])
        dn += nn(dkv[rows, :], W[WK : WK + 2 * KV * HD, 0:D])
        xb = v["tok"][rows, :].astype(F32)
        r1 = stats[rows, 126:127]
        gains[0:1, :] += jnp.sum(dn * xb * r1, axis=0, keepdims=True)
        scaled = dn * vec[0:1, :]
        inner = jnp.mean(scaled * xb, axis=1, keepdims=True)
        ds_out[rows, :] = ds_out[rows, :] + scaled * r1 - xb * (r1 * r1 * r1 * inner)
        return 0

    lax.fori_loop(0, 2, close_back, 0)
    keep_x = net.local(ds_out, v["x_out"])
    keep_x.start()

    SG = v["SG"]

    def collect_tile(i, _):
        start = pl.multiple_of(i * ST, ST)
        first = lax.rem(iota((ST, 1), 0), 8) == 0
        total = None
        for row, width, size, offset, stride in (
            (gains[0:1, :], D, DS, 0, 1),
            (gains[1:2, :], D, DS, DS, 1),
            (gains[2:3, :], D, DS, 2 * DS, 1),
            (gains[3:4, 0:LANES], LANES, KS, 3 * DS, 2),
            (gains[3:4, LANES : 2 * LANES], LANES, KS, 3 * DS + 1, 2),
        ):
            owner, _ = owner_of(iota((1, width), 1), size)
            _, inner = owner_of(iota((width, LANES), 0), size)
            pick = (iota((width, LANES), 1) == inner * stride + offset).astype(BF16)
            full = jnp.where((row_device(start) == owner) & first, row, 0.0)
            high = full.astype(BF16)
            part = nn(high, pick) + nn((full - high.astype(F32)).astype(BF16), pick)
            total = part if total is None else total + part
        SG[pl.ds(start, ST), :] = total
        return 0

    lax.fori_loop(0, rows_n // ST, collect_tile, 0)

    def sg_rows(dev_m):
        return pl.ds(pl.multiple_of(dev_m * R * 8, 8), R * 8)

    sg_in = v["sg_in"]
    s_far = net.copy(SG.at[sg_rows(m3)], sg_in.at[0], core)
    s_near = net.copy(SG.at[sg_rows(m1)], sg_in.at[1], core)
    s_over = net.copy(SG.at[sg_rows(m2)], sg_in.at[2], beside)
    s_far.start()
    s_near.start()
    s_far.wait_recv()
    SG[sg_rows(m2), :] = SG[sg_rows(m2), :] + sg_in[0]
    s_over.start()
    for k in order[3:]:
        sum_p.send_over(k)
    serve_scatter(11)

    def down_send():
        tmp[0:DA, :] = rD[drow(0, 0, DA), :].astype(F32) + sDA.last(
            lambda i, f: turn(v["bufA"][i], f)
        )
        tmp[DA:DP, :] = rD[drow(0, DA, DP - DA), :].astype(F32) + sDB.last(
            lambda i, f: turn(v["bufB"][i], f)
        )
        for i in range(4):
            dx[i, 0:DS, :] = tmp[i * DS : (i + 1) * DS, :].astype(BF16)
        for c in home:
            c.start()
        down_p[m] = dx[m]

    def down_home():
        for c in home:
            c.wait_recv()
        for i in range(4):
            full = turn_by_seat(down_p[i].astype(F32), True)
            for place in range(R):
                v["down_out"][:, owned_units(place, i)] = full[0:DS, place * FP : place * FP + FS]

    home = [
        net.copy(dx.at[dst_m], down_p.at[m], dev)
        for dst_m, dev in ((m1, core), (m2, beside), (m3, across))
    ]

    def small_add(k, slot, forward):
        SG[srow(m, k), :] = SG[srow(m, k), :] + v["sring"][slot]

    ssm = Scatter("A", lambda k: SG.at[srow(m, k)], v["sring"], small_add)

    def settle(s):
        for k in both(s) if s else (0,):
            sum_p.settle(k)
            sum_o.settle(k)

    def close_y(i):
        sum_y.finish(i)
        rows = slice(i * HB, (i + 1) * HB)
        y_out[rows, :] = y_out[rows, :] * stats[rows, 125:126]

    settle(long_way)
    settle(long_way - 1)
    sum_p.ring.begin()
    sum_o.ring.begin()
    sum_y.send_near()
    s_near.wait_recv()
    s_over.wait_recv()
    SG[sg_rows(m), :] = SG[sg_rows(m), :] + sg_in[1] + sg_in[2]
    ssm.begin()
    sum_y.keep(True)
    for t in range(1, long_way + 1):
        if t < long_way:
            settle(long_way - t - 1)
        for x in (sum_p.ring, sum_o.ring, ssm):
            x.serve(t)
        if t == 1:
            sum_y.near.wait_recv()
            close_y(1)
            close_y(0)
            sum_y.sent()
            keep_y = net.local(y_out, v["y_out"])
            keep_y.start()
            serve_scatter(12)
        if t == 2:
            serve_scatter(14)
            down_send()
    mine = arow(m, 0)
    low = AW[mine, :].astype(F32)
    first = low[0:PH] + sum_p.ring.last(lambda i, f: v["ringP"][i].astype(F32))
    rest = low[PH:AR] + sum_o.ring.last(lambda i, f: v["ringO"][i].astype(F32))
    v["small_out"][...] = SG[srow(m, 0), :] + ssm.last(lambda i, f: v["sring"][i])
    v["q_out"][...] = first[0:DS]
    v["k_out"][...] = first[KO:VO]
    v["v_out"][...] = first[VO:OO]
    v["o_out"][0 : PH - OO, :] = first[OO:PH]
    v["o_out"][PH - OO : DS, :] = rest

    serve_scatter(len(scatter_steps))
    mine = slice(own * FP, own * FP + FS)
    res[0:FS, 0:D] = rG[mine, :].astype(F32) + sG.last(
        lambda i, f: v["bufG"][i, 0:FS, :].astype(F32)
    )
    res[FS : 2 * FS, 0:D] = rU[mine, :].astype(F32) + sU.last(
        lambda i, f: v["bufU"][i, 0:FS, :].astype(F32)
    )
    keep_rows = net.local(res.at[pl.ds(0, 2 * FS), pl.ds(0, D)], v["rows_out"])
    keep_rows.start()
    down_home()
    net.sent(net.open)
    for c in (keep_y, keep_x, keep_rows):
        c.wait()


def layer(geo, ins):
    R, T, D, FP, U, DSP, DP, DA = geo.R, geo.T, geo.D, geo.FP, geo.U, geo.DSP, geo.DP, geo.DA
    AR = geo.AR
    outs = {
        "y_out": ((T, D), F32),
        "x_out": ((T, D), F32),
        "rows_out": ((2 * geo.FS, D), F32),
        "q_out": ((geo.DS, D), F32),
        "k_out": ((geo.KS, D), F32),
        "v_out": ((geo.KS, D), F32),
        "o_out": ((geo.DS, D), F32),
        "down_out": ((geo.DS, R * 4 * geo.FS), F32),
        "small_out": ((8, LANES), F32),
        "spill": ((2 * D + 2 * KV * HD, D), BF16),
    }
    scratch = {
        "down_p": ((4, DSP, U), BF16),
        "y": ((T, D), F32),
        "x": ((T, D), F32),
        "dx": ((4, DSP, U), BF16),
        "AW": ((4 * R * AR, D), BF16),
        "SM": ((4 * R * 8, LANES), F32),
        "SG": ((4 * R * 8, LANES), F32),
        "sg_in": ((3, R * 8, LANES), F32),
        "sring": ((4, 8, LANES), F32),
        "ringP": ((4, geo.PH, D), BF16),
        "ringO": ((4, AR - geo.PH, D), BF16),
        "stage": ((T, D), BF16),
        "y_in": ((T, D), BF16),
        "S": ((4 * T, D), BF16),
        "dO": ((4 * T, D), BF16),
        "tmp": ((DP, U), F32),
        "tmp3": ((8 * geo.KS, D), F32),
        "Wg": ((U, D), BF16),
        "Wu": ((U, D), BF16),
        "Wd": ((D, U), BF16),
        "hid": ((4 * T, U), BF16),
        "dg": ((4 * T, U), BF16),
        "du": ((4 * T, U), BF16),
        "gG": ((U, D), BF16),
        "gU": ((U, D), BF16),
        "gD": ((D, U), BF16),
        "bufG": ((4, FP, D), BF16),
        "bufU": ((4, FP, D), BF16),
        "bufA": ((4, DA, U), BF16),
        "bufB": ((4, DP - DA, U), BF16),
        "stats": ((T, LANES), F32),
        "bias": ((T, T), BF16),
        "cos": ((T, LANES), F32),
        "sin": ((T, LANES), F32),
        "vec": ((8, D), F32),
        "gains": ((8, D), F32),
        "normed": ((T, D), BF16),
        "Q": ((T, D), BF16),
        "mixed": ((T, D), BF16),
        "KX": ((4, T, LANES), BF16),
        "VX": ((4, T, LANES), BF16),
        "res": ((T, D + LANES), F32),
        "dkv": ((T, 2 * LANES), BF16),
    }
    alias = {"W": "du"}
    names = list(ins) + list(outs) + list(scratch) + ["send_sems", "recv_sems", "local_sems"]
    vm = pl.BlockSpec(memory_space=pltpu.VMEM)
    hbm = pl.BlockSpec(memory_space=pl.ANY)

    def body(*refs):
        table = dict(zip(names, refs))
        for new, old in alias.items():
            table[new] = table[old]
        kernel_body(geo, list(table), *table.values())

    res = pl.pallas_call(
        body,
        out_shape=[jax.ShapeDtypeStruct(s, d) for s, d in outs.values()],
        in_specs=[hbm if n == "cot" else vm for n in ins],
        out_specs=[hbm if n in ("y_out", "x_out", "rows_out", "spill") else vm for n in outs],
        scratch_shapes=[pltpu.VMEM(s, d) for s, d in scratch.values()]
        + [pltpu.SemaphoreType.DMA((28 * R + 16,))] * 2
        + [pltpu.SemaphoreType.DMA((6,))],
        compiler_params=pltpu.CompilerParams(
            collective_id=0, has_side_effects=True, vmem_limit_bytes=64 * 2**20
        ),
    )(*ins.values())
    return dict(zip(outs, res))


def hand_out(geo, res):
    whole = ["y_out", "x_out", "down_out", "q_out", "k_out", "v_out", "o_out"]
    rows = res["rows_out"].shape[0] // 2
    shapes = [res[n].shape for n in whole] + [(rows, geo.D)] * 2

    def body(*refs):
        count = len(shapes)
        sources, both = refs[: count - 2], refs[count - 2]
        results, held = refs[count - 1 : 2 * count - 1], refs[2 * count - 1 : 3 * count - 1]
        sems = refs[-1]
        sources += tuple(both.at[pl.ds(i * rows, rows)] for i in range(2))
        inward = [pltpu.make_async_copy(sources[i], held[i], sems.at[0, i]) for i in range(count)]
        outward = [pltpu.make_async_copy(held[i], results[i], sems.at[1, i]) for i in range(count)]
        for c in inward:
            c.start()
        for i in range(count):
            inward[i].wait()
            outward[i].start()
        for c in outward:
            c.wait()

    hbm = pl.BlockSpec(memory_space=pltpu.HBM)
    outs = pl.pallas_call(
        body,
        out_shape=[jax.ShapeDtypeStruct(s, F32) for s in shapes],
        in_specs=[hbm] * (len(shapes) - 1),
        out_specs=[hbm] * len(shapes),
        scratch_shapes=[pltpu.VMEM(s, F32) for s in shapes]
        + [pltpu.SemaphoreType.DMA((2, len(shapes)))],
        compiler_params=pltpu.CompilerParams(vmem_limit_bytes=64 * 2**20),
    )(*[res[n] for n in whole + ["rows_out"]])
    return dict(zip(["y", "x", "down", "q", "k", "v", "o", "gate", "up"], outs))


D = 896
eps_norm = 1e-06
rope_base = 1000000.0
masked_value = -1e30


def apply_weight(left, weight):
    return lax.dot_general(
        left, weight, (((1,), (1,)), ((), ())), preferred_element_type=jnp.float32
    )


def apply_transpose(left, weight):
    return jnp.dot(left, weight, preferred_element_type=jnp.float32)


def weight_grad(grad_rows, input_rows):
    return lax.dot_general(
        grad_rows, input_rows, (((0,), (0,)), ((), ())), preferred_element_type=jnp.float32
    )


def rms_scale(field_rows):
    return lax.rsqrt(jnp.mean(field_rows * field_rows, axis=1, keepdims=True) + eps_norm)


def norm_backward(grad_rows, field_rows, scale_rows, gain_values):
    scaled = grad_rows * gain_values
    return scaled * scale_rows - field_rows * scale_rows**3 * jnp.mean(
        scaled * field_rows, axis=1, keepdims=True
    )


def rope_tables(block_segments):
    slot_index = jnp.arange(block_segments.shape[0])
    same_segment = block_segments[:, None] == block_segments[None, :]
    earlier = slot_index[None, :] < slot_index[:, None]
    positions = jnp.sum((same_segment & earlier).astype(jnp.float32), axis=1)
    frequency = jnp.exp(jnp.arange(HD // 2, dtype=jnp.float32) * (-2.0 * math.log(rope_base) / HD))
    angles = positions[:, None] * frequency[None, :]
    return (jnp.cos(angles)[:, None, :], jnp.sin(angles)[:, None, :])


def rotate(vectors, cosine_table, sine_table):
    first_half = vectors[..., : HD // 2]
    second_half = vectors[..., HD // 2 :]
    return jnp.concatenate(
        [
            first_half * cosine_table - second_half * sine_table,
            second_half * cosine_table + first_half * sine_table,
        ],
        axis=-1,
    )


def rotate_back(vectors, cosine_table, sine_table):
    first_half = vectors[..., : HD // 2]
    second_half = vectors[..., HD // 2 :]
    return jnp.concatenate(
        [
            first_half * cosine_table + second_half * sine_table,
            second_half * cosine_table - first_half * sine_table,
        ],
        axis=-1,
    )


def plain_local(
    tokens,
    segment_ids,
    live_counts,
    first_gain,
    query_weight,
    query_bias,
    key_weight,
    value_weight,
    key_value_bias,
    output_weight,
    second_gain,
    gate_weight,
    up_weight,
    down_weight,
    cotangent,
):
    attention_set = (
        lax.all_gather(first_gain, "dp", axis=0, tiled=True),
        lax.all_gather(query_weight, "dp", axis=0, tiled=True),
        lax.all_gather(query_bias, "dp", axis=0, tiled=True),
        lax.all_gather(key_weight, "dp", axis=0, tiled=True),
        lax.all_gather(value_weight, "dp", axis=0, tiled=True),
        lax.all_gather(key_value_bias, "dp", axis=0, tiled=True),
        lax.all_gather(output_weight, "dp", axis=0, tiled=True),
    )
    first_full, query_full, query_bias_full, key_full, value_full, pair_bias_full, output_full = (
        attention_set
    )
    slot_count = tokens.shape[0]
    group_size = HEADS // KV
    scale_factor = HD ** (-0.5)
    slot_index = jnp.arange(slot_count)
    live_rows = (slot_index < live_counts[0]).astype(jnp.float32)
    allowed = (segment_ids[:, None] == segment_ids[None, :]) & (
        slot_index[None, :] <= slot_index[:, None]
    ) & (live_rows[None, :] > 0.5) | (slot_index[None, :] == slot_index[:, None])
    cosine_table, sine_table = rope_tables(segment_ids)
    token_rows = tokens.astype(jnp.float32)
    first_scale = rms_scale(token_rows)
    normed = (token_rows * first_scale * first_full.astype(jnp.float32)).astype(jnp.bfloat16)
    pair_bias_values = pair_bias_full.astype(jnp.float32)
    query_pre = apply_weight(normed, query_full) + query_bias_full.astype(jnp.float32)
    key_pre = apply_weight(normed, key_full) + pair_bias_values[:, 0]
    values = (apply_weight(normed, value_full) + pair_bias_values[:, 1]).astype(jnp.bfloat16)
    values = values.reshape(slot_count, KV, HD)
    rotated_queries = rotate(query_pre.reshape(slot_count, HEADS, HD), cosine_table, sine_table)
    rotated_queries = rotated_queries.astype(jnp.bfloat16).reshape(slot_count, KV, group_size, HD)
    rotated_keys = rotate(key_pre.reshape(slot_count, KV, HD), cosine_table, sine_table).astype(
        jnp.bfloat16
    )

    def attention_logits():
        scores = jnp.einsum(
            "ikgd,jkd->kgij", rotated_queries, rotated_keys, preferred_element_type=jnp.float32
        )
        return jnp.where(allowed[None, None], scores * scale_factor, masked_value)

    logits = attention_logits()
    row_top = jnp.max(logits, axis=-1, keepdims=True)
    exponent = jnp.exp(logits - row_top)
    row_total = jnp.sum(exponent, axis=-1, keepdims=True)
    weights_low = (exponent / row_total).astype(jnp.bfloat16)
    mixed_heads = jnp.einsum(
        "kgij,jkd->ikgd", weights_low, values, preferred_element_type=jnp.float32
    )
    mixed_heads = mixed_heads.reshape(slot_count, D).astype(jnp.bfloat16)
    residual = token_rows + apply_weight(mixed_heads, output_full)
    feed_set = (
        lax.all_gather(second_gain, "dp", axis=0, tiled=True),
        lax.all_gather(gate_weight, "dp", axis=0, tiled=True),
        lax.all_gather(up_weight, "dp", axis=0, tiled=True),
        lax.all_gather(down_weight, "dp", axis=0, tiled=True),
    )
    second_full, gate_full, up_full, down_full = feed_set
    second_scale = rms_scale(residual)
    second = (residual * second_scale * second_full.astype(jnp.float32)).astype(jnp.bfloat16)
    gate_value = apply_weight(second, gate_full)
    up_value = apply_weight(second, up_full)
    hidden = (jax.nn.silu(gate_value) * up_value).astype(jnp.bfloat16)
    layer_out = (residual + apply_weight(hidden, down_full)) * live_rows[:, None]
    feed_back = (
        lax.all_gather(second_gain, "dp", axis=0, tiled=True),
        lax.all_gather(gate_weight, "dp", axis=0, tiled=True),
        lax.all_gather(up_weight, "dp", axis=0, tiled=True),
        lax.all_gather(down_weight, "dp", axis=0, tiled=True),
    )
    back_second, back_gate, back_up, back_down = feed_back
    out_grad = cotangent.astype(jnp.float32) * live_rows[:, None]
    out_grad_low = out_grad.astype(jnp.bfloat16)
    down_shard = lax.psum_scatter(
        weight_grad(out_grad_low, hidden), "dp", scatter_dimension=0, tiled=True
    )
    hidden_grad = apply_transpose(out_grad_low, back_down)
    sigmoid_gate = jax.nn.sigmoid(gate_value)
    up_grad_rows = (hidden_grad * (gate_value * sigmoid_gate)).astype(jnp.bfloat16)
    gate_grad_rows = (
        hidden_grad * up_value * sigmoid_gate * (1.0 + gate_value * (1.0 - sigmoid_gate))
    ).astype(jnp.bfloat16)
    gate_part = weight_grad(gate_grad_rows, second)
    up_part = weight_grad(up_grad_rows, second)
    gate_up_shard = lax.psum_scatter(
        jnp.concatenate([gate_part, up_part], axis=1), "dp", scatter_dimension=0, tiled=True
    )
    model_width = second.shape[1]
    gate_shard = gate_up_shard[:, :model_width]
    up_shard = gate_up_shard[:, model_width:]
    second_grad_rows = apply_transpose(gate_grad_rows, back_gate) + apply_transpose(
        up_grad_rows, back_up
    )
    second_gain_grad = jnp.sum(second_grad_rows * residual * second_scale, axis=0)
    residual_grad = out_grad + norm_backward(
        second_grad_rows, residual, second_scale, back_second.astype(jnp.float32)
    )
    attention_back = (
        lax.all_gather(first_gain, "dp", axis=0, tiled=True),
        lax.all_gather(query_weight, "dp", axis=0, tiled=True),
        lax.all_gather(query_bias, "dp", axis=0, tiled=True),
        lax.all_gather(key_weight, "dp", axis=0, tiled=True),
        lax.all_gather(value_weight, "dp", axis=0, tiled=True),
        lax.all_gather(key_value_bias, "dp", axis=0, tiled=True),
        lax.all_gather(output_weight, "dp", axis=0, tiled=True),
    )
    back_first = attention_back[0]
    back_query = attention_back[1]
    back_key = attention_back[3]
    back_value = attention_back[4]
    back_output = attention_back[6]
    branch_grad = residual_grad.astype(jnp.bfloat16)
    output_grad = weight_grad(branch_grad, mixed_heads)
    mixed_grad = apply_transpose(branch_grad, back_output).astype(jnp.bfloat16)
    mixed_grad = mixed_grad.reshape(slot_count, KV, group_size, HD)
    probs = jnp.exp(attention_logits() - row_top) / row_total
    probs_low = probs.astype(jnp.bfloat16)
    value_grad_rows = jnp.einsum(
        "kgij,ikgd->jkd", probs_low, mixed_grad, preferred_element_type=jnp.float32
    )
    prob_grad = jnp.einsum("ikgd,jkd->kgij", mixed_grad, values, preferred_element_type=jnp.float32)
    logit_grad = probs * (prob_grad - jnp.sum(probs * prob_grad, axis=-1, keepdims=True))
    score_grad = (logit_grad * scale_factor).astype(jnp.bfloat16)
    query_rot_grad = jnp.einsum(
        "kgij,jkd->ikgd", score_grad, rotated_keys, preferred_element_type=jnp.float32
    )
    key_rot_grad = jnp.einsum(
        "kgij,ikgd->jkd", score_grad, rotated_queries, preferred_element_type=jnp.float32
    )
    query_grad_rows = rotate_back(
        query_rot_grad.reshape(slot_count, HEADS, HD), cosine_table, sine_table
    )
    query_grad_rows = query_grad_rows.astype(jnp.bfloat16).reshape(slot_count, D)
    key_grad_rows = (
        rotate_back(key_rot_grad, cosine_table, sine_table)
        .astype(jnp.bfloat16)
        .reshape(slot_count, KV * HD)
    )
    value_grad_low = value_grad_rows.astype(jnp.bfloat16).reshape(slot_count, KV * HD)
    query_grad = weight_grad(query_grad_rows, normed)
    query_bias_grad = jnp.sum(query_grad_rows.astype(jnp.float32), axis=0)
    key_grad = weight_grad(key_grad_rows, normed)
    value_grad = weight_grad(value_grad_low, normed)
    pair_bias_grad = jnp.stack(
        [
            jnp.sum(key_grad_rows.astype(jnp.float32), axis=0),
            jnp.sum(value_grad_low.astype(jnp.float32), axis=0),
        ],
        axis=1,
    )
    first_grad_rows = (
        apply_transpose(query_grad_rows, back_query)
        + apply_transpose(key_grad_rows, back_key)
        + apply_transpose(value_grad_low, back_value)
    )
    first_gain_grad = jnp.sum(first_grad_rows * token_rows * first_scale, axis=0)
    input_grad = residual_grad + norm_backward(
        first_grad_rows, token_rows, first_scale, back_first.astype(jnp.float32)
    )
    attention_shards = (
        lax.psum_scatter(first_gain_grad, "dp", scatter_dimension=0, tiled=True),
        lax.psum_scatter(query_grad, "dp", scatter_dimension=0, tiled=True),
        lax.psum_scatter(query_bias_grad, "dp", scatter_dimension=0, tiled=True),
        lax.psum_scatter(key_grad, "dp", scatter_dimension=0, tiled=True),
        lax.psum_scatter(value_grad, "dp", scatter_dimension=0, tiled=True),
        lax.psum_scatter(pair_bias_grad, "dp", scatter_dimension=0, tiled=True),
        lax.psum_scatter(output_grad, "dp", scatter_dimension=0, tiled=True),
        lax.psum_scatter(second_gain_grad, "dp", scatter_dimension=0, tiled=True),
    )
    return (layer_out, input_grad) + tuple(attention_shards) + (gate_shard, up_shard, down_shard)


def fused_local(
    geo,
    tokens,
    segment_ids,
    live_counts,
    first_gain,
    query_weight,
    query_bias,
    key_weight,
    value_weight,
    key_value_bias,
    output_weight,
    second_gain,
    gate_weight,
    up_weight,
    down_weight,
    cotangent,
):
    T, DS, KS = geo.T, geo.DS, geo.KS
    live = (jnp.arange(T) < live_counts[0]).astype(F32)
    vectors = jnp.concatenate(
        [first_gain, query_bias, second_gain, key_value_bias.reshape(-1)]
    ).astype(F32)
    aux = jnp.stack(
        [segment_ids.astype(F32), live, jnp.pad(vectors, (0, T - vectors.shape[0]))]
    )
    aux = jnp.pad(aux, ((0, 5), (0, 0)))
    res = layer(
        geo,
        {
            "tok": tokens,
            "cot": cotangent,
            "wq": query_weight,
            "wo": output_weight,
            "wk": key_weight,
            "wv": value_weight,
            "gate": gate_weight,
            "up": up_weight,
            "down": down_weight,
            "aux": aux,
        },
    )
    vec = res["small_out"][0]
    out = hand_out(geo, res)
    return (
        out["y"],
        out["x"],
        vec[:DS],
        out["q"],
        vec[DS : 2 * DS],
        out["k"],
        out["v"],
        vec[3 * DS : 3 * DS + 2 * KS].reshape(KS, 2),
        out["o"],
        vec[2 * DS : 3 * DS],
        out["gate"],
        out["up"],
        out["down"],
    )


def local(tokens, segment_ids, live_counts, first_gain, *rest):
    geo = Geometry(
        lax.axis_size("dp"), tokens.shape[0], tokens.shape[1], rest[9].shape[1]
    )
    layer_of = functools.partial(fused_local, geo) if geo.fits() else plain_local
    return layer_of(tokens, segment_ids, live_counts, first_gain, *rest)


def solution(mesh):
    in_specs = (
        P("dp", None),
        P("dp"),
        P("dp"),
        P("dp"),
        P("dp", None),
        P("dp"),
        P("dp", None),
        P("dp", None),
        P("dp", None),
        P("dp", None),
        P("dp"),
        P("dp", None),
        P("dp", None),
        P("dp", None),
        P("dp", None),
    )
    out_specs = (
        P("dp", None),
        P("dp", None),
        P("dp"),
        P("dp", None),
        P("dp"),
        P("dp", None),
        P("dp", None),
        P("dp", None),
        P("dp", None),
        P("dp"),
        P("dp", None),
        P("dp", None),
        P("dp", None),
    )
    return jax.shard_map(local, mesh=mesh, in_specs=in_specs, out_specs=out_specs, check_vma=False)
```

```python
import functools
import math

import jax
import jax.numpy as jnp
from jax import lax
from jax.experimental import pallas as pl
from jax.experimental.pallas import tpu as pltpu
from jax.sharding import PartitionSpec as P

MESH = pl.DeviceIdType.MESH
F32 = jnp.float32
BF16 = jnp.bfloat16

HEADS = 14
KV = 2
HD = 64
GROUP = HEADS // KV
PAIRS = HEADS // 2
LANES = 128
EPS = 1e-06
ROPE_BASE = 1000000.0
MASKED = -1e30
SCALE = HD ** (-0.5)


def up16(n):
    return -(-n // 16) * 16


def nn(a, b):
    return jnp.dot(a, b, preferred_element_type=F32)


def nt(a, b):
    return lax.dot_general(a, b, (((1,), (1,)), ((), ())), preferred_element_type=F32)


def tn(a, b):
    return lax.dot_general(a, b, (((0,), (0,)), ((), ())), preferred_element_type=F32)


class Geometry:
    def __init__(self, devices, slots, width, hidden):
        self.n = devices
        self.R = devices // 4
        self.T = slots
        self.D = width
        self.FS = hidden // devices
        self.FP = up16(self.FS)
        self.U = self.R * self.FP
        self.DS = width // devices
        self.DSP = up16(self.DS)
        self.DP = 4 * self.DS
        self.DA = up16(self.DP // 2)
        self.KS = KV * HD // devices
        self.AR = 2 * self.DS + 2 * self.KS
        self.PH = up16(self.DS + 2 * self.KS)
        self.OFF = 1 - self.R // 2

    def fits(self):
        return (
            self.n % 32 == 0
            and self.DP % 16 == 0
            and self.AR % 16 == 0
            and self.FP % 32 == 0 and self.FS % 8 == 0
            and self.PH < self.AR
            and (4 * self.KS) % 16 == 0
            and self.U % 256 == 0
            and self.R * self.AR == self.T
            and self.R & (self.R - 1) == 0
            and 2 * self.D + 2 * KV * HD == 4 * self.T
            and 3 * self.DS + 2 * self.KS <= LANES
            and 4 * self.T * self.U * 6 <= 16 * 2**20
        )


def ring_place(g, R):
    odd = lax.rem(g, 2)
    half = lax.div(g, 2)
    return (1 - odd) * half + odd * (R - 1 - half)


def ring_group(place, R):
    high = lax.div(place, R // 2)
    return (1 - high) * (2 * place) + high * (2 * (R - 1 - place) + 1)


class Net:
    def __init__(self, send_sems, recv_sems, local_sems):
        self.send_sems, self.recv_sems, self.local_sems = send_sems, recv_sems, local_sems
        self.count = 0
        self.local_count = 0
        self.open = []
        self.index = []
        self.free = []

    def copy(self, src, dst, device):
        if self.free:
            i = self.free.pop()
        else:
            i = self.count
            self.count += 1
        made = pltpu.make_async_remote_copy(
            src_ref=src,
            dst_ref=dst,
            send_sem=self.send_sems.at[i],
            recv_sem=self.recv_sems.at[i],
            device_id=(device,),
            device_id_type=MESH,
        )
        self.open.append(made)
        self.index.append((made, i))
        return made

    def release(self, copies):
        for c in copies:
            self.free += [i for made, i in self.index if made is c]

    def sent(self, copies):
        for c in copies:
            c.wait_send()
        self.open = [x for x in self.open if all(x is not c for c in copies)]

    def local(self, src, dst):
        i = self.local_count
        self.local_count += 1
        return pltpu.make_async_copy(src, dst, self.local_sems.at[i])


def parts(lo, hi, step):
    return [slice(at, min(at + step, hi)) for at in range(lo, hi, step)]


def iota(shape, axis):
    return lax.broadcasted_iota(jnp.int32, shape, axis)


def kernel_body(geo, names, *refs):
    v = dict(zip(names, refs))
    R, T, D, FP, FS, U = geo.R, geo.T, geo.D, geo.FP, geo.FS, geo.U
    DSP, DS, DP, DA, KS, AR, PH = geo.DSP, geo.DS, geo.DP, geo.DA, geo.KS, geo.AR, geo.PH
    me = lax.axis_index("dp")
    m, g = lax.rem(me, 4), lax.div(me, 4)
    r = ring_place(g, R)

    def place_group(k):
        return ring_group(lax.rem(r + k + 2 * R, R), R)

    right = place_group(1) * 4 + m
    left = place_group(-1) * 4 + m
    m1 = m + 1 - 2 * lax.rem(m, 2)
    m2 = m + 2 - 4 * lax.div(m, 2)
    m3 = m1 + 2 - 4 * lax.div(m1, 2)
    core, beside, across = g * 4 + m1, g * 4 + m2, g * 4 + m3
    net = Net(v["send_sems"], v["recv_sems"], v["local_sems"])

    barrier = pltpu.get_barrier_semaphore()
    for peer in (right, left, core, beside, across):
        pl.semaphore_signal(barrier, inc=1, device_id=(peer,), device_id_type=MESH)

    AW, SM, tmp, aux = v["AW"], v["SM"], v["tmp"], v["aux"]
    S, dO = v["S"], v["dO"]
    Wg, Wu, Wd = v["Wg"], v["Wu"], v["Wd"]
    stats, bias = v["stats"], v["bias"]

    bring_cot = net.local(v["cot"], dO.at[pl.ds(0, T)])
    bring_cot.start()

    KO, VO, OO = DS, DS + KS, DS + 2 * KS
    tmp[0:DS, 0:D] = v["wq"][...].astype(F32)
    tmp[KO:VO, 0:D] = v["wk"][...].astype(F32)
    tmp[VO:OO, 0:D] = v["wv"][...].astype(F32)
    tmp[OO:AR, 0:D] = v["wo"][...].astype(F32)

    def arow(dev_m, k, lo=0, size=AR):
        return pl.ds(pl.multiple_of((dev_m * R + place_group(k)) * AR + lo, 16), size)

    AW[arow(m, 0), :] = tmp[0:AR, 0:D].astype(BF16)

    def srow(dev_m, k):
        return pl.ds(pl.multiple_of((dev_m * R + place_group(k)) * 8, 8), 8)

    SM[srow(m, 0), :] = jnp.where(iota((8, LANES), 0) == 0, aux[2:3, 0:LANES], 0.0)

    def jslot(k):
        return (k - geo.OFF) % R

    def unit_rows(j):
        return slice(j * FP, (j + 1) * FP)

    own = jslot(0)
    for ref, mine in ((Wg, v["gate"]), (Wu, v["up"])):
        if FP > FS:
            ref[unit_rows(own), :] = jnp.zeros((FP, D), BF16)
        ref[own * FP : own * FP + FS, :] = mine[...]

    pl.semaphore_wait(barrier, 5)

    long_way, short_way = R // 2, R // 2 - 1
    classes = {"A": (long_way, short_way), "B": (short_way, long_way)}

    class Gather:
        def __init__(self, cls, src, dst, arrive=None):
            self.nf, self.nb = classes[cls]
            self.f = [net.copy(src(-(s - 1)), dst(-s, s), right) for s in range(1, self.nf + 1)]
            self.b = [net.copy(src(s - 1), dst(s, s), left) for s in range(1, self.nb + 1)]
            self.arrive = arrive

        def begin(self):
            self.f[0].start()
            self.b[0].start()

        def serve(self, s):
            if s <= self.nf:
                self.f[s - 1].wait_recv()
            if s <= self.nb:
                self.b[s - 1].wait_recv()
            if self.arrive and s <= self.nf:
                self.arrive(-s, s)
            if self.arrive and s <= self.nb:
                self.arrive(s, s)
            if s < self.nf:
                self.f[s].start()
            if s < self.nb:
                self.b[s].start()

    def nearer(k):
        return k + 1 if k < 0 else k - 1

    class Fan:
        def __init__(self, cls, lo, size):
            def at(dev_m, k):
                return AW.at[arow(dev_m, k, lo, size)]

            self.ring = Gather(cls, lambda k: at(m, k), lambda k, s: at(m, nearer(k)))
            self.beside = {k: net.copy(at(m, k), at(m, k), beside) for k in ks}
            self.core = {k: net.copy(at(m, k), at(m, k), core) for k in ks}
            self.on = {k: net.copy(at(m2, k), at(m2, k), core) for k in ks}

        def out(self, k):
            self.beside[k].start()
            self.core[k].start()

        def forward(self, k):
            self.beside[k].wait_recv()
            self.on[k].start()

        def arrived(self):
            for k in ks:
                self.core[k].wait_recv()
                self.on[k].wait_recv()

        def copies(self):
            within = [c for d in (self.beside, self.core, self.on) for c in d.values()]
            return self.ring.f + self.ring.b + within

    def both(s):
        return [-s, s] if s < long_way else [s]

    ks = [0] + [k for s in range(1, long_way + 1) for k in both(s)]
    fan_p, fan_o = Fan("A", 0, PH), Fan("B", PH, AR - PH)
    gsm = Gather("A", lambda k: SM.at[srow(m, k)], lambda k, s: SM.at[srow(m, nearer(k))])

    def small_rows(dev_m):
        return SM.at[pl.ds(pl.multiple_of(dev_m * R * 8, 8), R * 8)]

    small_beside = net.copy(small_rows(m), small_rows(m), beside)
    small_core = net.copy(small_rows(m), small_rows(m), core)
    small_on = net.copy(small_rows(m2), small_rows(m2), core)
    attn_copies = fan_p.copies() + fan_o.copies() + gsm.f + gsm.b
    attn_copies += [small_beside, small_core, small_on]

    def drow(k, lo=0, size=DP):
        return pl.ds(pl.multiple_of(place_group(k) * DP + lo, 16), size)

    def turn(block, forward):
        return pltpu.roll(block.astype(F32), U - FP if forward else FP, 1)

    def box(s, forward):
        return (s % 2) * 2 + (0 if forward else 1)

    def down_gather(cls, buf, lo, size):
        def arrive(k, s):
            Wd[drow(k, lo, size), :] = turn(buf[box(s, k < 0)], k < 0).astype(BF16)

        return Gather(
            cls, lambda k: Wd.at[drow(k, lo, size)], lambda k, s: buf.at[box(s, k < 0)], arrive
        )

    def unit_gather(cls, ref, lo):
        def at(k):
            return ref.at[pl.ds(jslot(k) * FP + lo, FP // 2)]

        return Gather(cls, at, lambda k, s: at(k))

    gDA = down_gather("A", v["bufA"], 0, DA)
    gDB = down_gather("B", v["bufB"], DA, DP - DA)
    unit_pieces = [
        unit_gather("A", Wg, 0),
        unit_gather("B", Wg, FP // 2),
        unit_gather("A", Wu, 0),
        unit_gather("B", Wu, FP // 2),
    ]

    def serve_units(s):
        for x in unit_pieces:
            x.serve(s)

    def serve_down(s):
        gDA.serve(s)
        gDB.serve(s)

    def serve_attention(s):
        fan_p.ring.serve(s)
        fan_o.ring.serve(s)
        gsm.serve(s)

    fan_p.ring.begin()
    fan_o.ring.begin()
    gsm.begin()
    fan_p.out(0)
    unit_pieces[0].begin()

    seat = lax.rem(r + geo.OFF + R, R)

    def turn_by_seat(block, back):
        b = 1
        while b < R:
            odd = lax.rem(lax.div(seat, b), 2) == 1
            block = jnp.where(odd, pltpu.roll(block, b * FP if back else U - b * FP, 1), block)
            b *= 2
        return block

    def owned_units(place, i):
        half = R // 2
        group = 2 * place if place < half else 2 * (R - 1 - place) + 1
        return slice((4 * group + i) * FS, (4 * group + i + 1) * FS)

    down_p, dx = v["down_p"], v["dx"]
    for i in range(4):
        for place in range(R):
            rows = slice(i * DS, (i + 1) * DS)
            if FP > FS:
                tmp[rows, place * FP + FS : (place + 1) * FP] = jnp.zeros((DS, FP - FS), F32)
            tmp[rows, place * FP : place * FP + FS] = v["down"][:, owned_units(place, i)].astype(F32)
    tmp[...] = turn_by_seat(tmp[...], False)
    for i in range(4):
        down_p[i, 0:DS, :] = tmp[i * DS : (i + 1) * DS, :].astype(BF16)
    down_copies = [
        net.copy(down_p.at[dst_m], dx.at[m], dev)
        for dst_m, dev in ((m1, core), (m2, beside), (m3, across))
    ]
    for c in down_copies:
        c.start()

    frequency = jnp.exp(
        lax.rem(iota((1, LANES), 1), HD // 2).astype(F32) * (-2.0 * math.log(ROPE_BASE) / HD)
    )
    PT = 128

    def prepare(i, _):
        start = pl.multiple_of(i * PT, PT)
        rows = pl.ds(start, PT)
        seg_row, live_row = aux[0:1, :], aux[1:2, :]
        ii, jj = iota((PT, T), 0) + start, iota((PT, T), 1)
        seg_col = jnp.sum(jnp.where(ii == jj, seg_row, 0.0), axis=1, keepdims=True)
        live_col = jnp.sum(jnp.where(ii == jj, live_row, 0.0), axis=1, keepdims=True)
        same = seg_col == seg_row
        position = jnp.sum(jnp.where(same & (jj < ii), 1.0, 0.0), axis=1, keepdims=True)
        allowed = (same & (jj <= ii) & (live_row > 0.5)) | (ii == jj)
        bias[rows, :] = jnp.where(allowed, 0.0, MASKED).astype(BF16)
        dO[rows, :] = (dO[rows, :].astype(F32) * live_col).astype(BF16)
        lane = iota((PT, LANES), 1)
        angles = position * frequency
        v["cos"][rows, :] = jnp.cos(angles)
        sine = jnp.sin(angles)
        v["sin"][rows, :] = jnp.where(lax.rem(lane, HD) < HD // 2, -sine, sine)
        x = v["tok"][rows, :].astype(F32)
        r1 = lax.rsqrt(jnp.mean(x * x, axis=1, keepdims=True) + EPS)
        stats[rows, :] = jnp.where(lane == 126, r1, jnp.where(lane == 125, live_col, 0.0))
        return 0

    bring_cot.wait()
    serve_attention(1)
    for k in both(1):
        fan_p.out(k)
    unit_pieces[1].begin()
    lax.fori_loop(0, T // PT // 2, prepare, 0)
    fan_p.forward(0)
    fan_o.out(0)
    for s in range(2, long_way + 1):
        serve_attention(s)
        for k in both(s):
            fan_p.out(k)
        for k in both(s - 1):
            fan_o.out(k)
        if s == 2:
            unit_pieces[2].begin()
            lax.fori_loop(T // PT // 2, T // PT, prepare, 0)
        if s == 3:
            unit_pieces[3].begin()
            dx[m] = down_p[m]
            for c in down_copies:
                c.wait_recv()
            for i in range(4):
                tmp[i * DS : (i + 1) * DS, :] = dx[i].astype(F32)[0:DS, :]
            Wd[drow(0), :] = tmp[0:DP, :].astype(BF16)
            net.sent(down_copies)
        for k in both(s - 1):
            fan_p.forward(k)
    gDA.begin()
    gDB.begin()

    PX = T // 2

    class GroupGather:
        def __init__(self, buf):
            def at(q, i):
                return buf.at[pl.ds(q * T + i * PX, PX)]

            self.beside = [net.copy(at(0, i), at(2, i), beside) for i in range(2)]
            self.core = [net.copy(at(0, i), at(1, i), core) for i in range(2)]
            self.on = [net.copy(at(2, i), at(3, i), core) for i in range(2)]

        def out(self, i):
            self.beside[i].start()
            self.core[i].start()

        def forward(self):
            for i in range(2):
                self.beside[i].wait_recv()
                self.on[i].start()

        def copies(self):
            return self.beside + self.core + self.on

    gS, gO = GroupGather(S), GroupGather(dO)
    small_beside.start()
    small_core.start()
    for k in both(long_way):
        fan_o.out(k)
    gO.out(0)
    gO.out(1)
    for k in both(long_way):
        fan_p.forward(k)
    small_beside.wait_recv()
    small_on.start()
    fan_p.arrived()
    small_core.wait_recv()
    small_on.wait_recv()

    serve_down(1)

    W, tmp3 = v["W"], v["tmp3"]
    WQ, WO, WK, WV = 0, D, 2 * D, 2 * D + KV * HD
    K4 = 4 * KS

    def unpack_first(gi, _):
        for i in range(4):
            at = pl.ds(pl.multiple_of((i * R + gi) * AR, 16), PH)
            rows = AW[at, :].astype(F32)
            tmp[i * DS : (i + 1) * DS, 0:D] = rows[0:DS]
            tmp3[i * KS : (i + 1) * KS, :] = rows[KO:VO]
            tmp3[K4 + i * KS : K4 + (i + 1) * KS, :] = rows[VO:OO]
        W[pl.ds(pl.multiple_of(WQ + gi * DP, 16), DP), 0:D] = tmp[0:DP, 0:D].astype(BF16)
        W[pl.ds(pl.multiple_of(WK + gi * K4, 16), K4), 0:D] = tmp3[0:K4, :].astype(BF16)
        W[pl.ds(pl.multiple_of(WV + gi * K4, 16), K4), 0:D] = tmp3[K4:, :].astype(BF16)
        return 0

    OB = OO // 16 * 16

    def unpack_output(gi, _):
        for i in range(4):
            at = pl.ds(pl.multiple_of((i * R + gi) * AR + OB, 16), AR - OB)
            tmp[i * DS : (i + 1) * DS, 0:D] = AW[at, :].astype(F32)[OO - OB : AR - OB]
        W[pl.ds(pl.multiple_of(WO + gi * DP, 16), DP), 0:D] = tmp[0:DP, 0:D].astype(BF16)
        return 0

    lax.fori_loop(0, R, unpack_first, 0)

    rows_n = 4 * R * 8
    ST = 64

    def owner_of(lanes, size):
        block = jnp.floor((lanes.astype(F32) + 0.5) * (1.0 / size)).astype(jnp.int32)
        return block, lanes - block * size

    def row_device(start):
        i = lax.div(iota((ST, 1), 0) + start, 8)
        return lax.rem(i, R) * 4 + lax.div(i, R)

    def spread(width, size, offset, stride):
        owner, inner = owner_of(iota((1, width), 1), size)
        pick = (iota((LANES, width), 0) == inner * stride + offset).astype(BF16)

        def tile(i, total):
            start = pl.multiple_of(i * ST, ST)
            full = nn(SM[pl.ds(start, ST), :].astype(BF16), pick)
            full = jnp.where(row_device(start) == owner, full, 0.0)
            return total + jnp.sum(full, axis=0, keepdims=True)

        return lax.fori_loop(0, rows_n // ST, tile, jnp.zeros((1, width), F32))

    vec = v["vec"]
    vec[0:1, :] = spread(D, DS, 0, 1)
    vec[1:2, :] = spread(D, DS, DS, 1)
    vec[2:3, :] = spread(D, DS, 2 * DS, 1)
    vec[3:4, 0:LANES] = spread(LANES, KS, 3 * DS, 2)
    vec[4:5, 0:LANES] = spread(LANES, KS, 3 * DS + 1, 2)

    cosine, sine = v["cos"], v["sin"]
    normed, Q, mixed = v["normed"], v["Q"], v["mixed"]
    KX, VX, res = v["KX"], v["VX"], v["res"]

    def swap_halves(block):
        lanes = iota(block.shape, 1)
        return jnp.where(
            lax.rem(lanes, HD) < HD // 2,
            pltpu.roll(block, LANES - HD // 2, 1),
            pltpu.roll(block, HD // 2, 1),
        )

    def rotate(block, rows):
        return block * cosine[rows, :] + swap_halves(block) * sine[rows, :]

    def rotate_back(block, rows):
        return block * cosine[rows, :] - swap_halves(block) * sine[rows, :]

    HB = T // 2

    def project(i, _):
        rows = pl.ds(pl.multiple_of(i * HB, HB), HB)
        xb = v["tok"][rows, :].astype(F32)
        nb = (xb * stats[rows, 126:127] * vec[0:1, :]).astype(BF16)
        normed[rows, :] = nb
        q = nt(nb, W[WQ : WQ + D, 0:D]) + vec[1:2, :]
        for p in range(PAIRS):
            lanes = slice(p * LANES, (p + 1) * LANES)
            Q[rows, lanes] = rotate(q[:, lanes], rows).astype(BF16)
        key = rotate(nt(nb, W[WK : WK + KV * HD, 0:D]) + vec[3:4, 0:LANES], rows)
        value = nt(nb, W[WV : WV + KV * HD, 0:D]) + vec[4:5, 0:LANES]
        low_half = iota((HB, LANES), 1) < HD
        for ref, full in ((KX, key), (VX, value)):
            other = pltpu.roll(full, HD, 1)
            ref[0, rows, :] = jnp.where(low_half, full, 0.0).astype(BF16)
            ref[1, rows, :] = jnp.where(low_half, 0.0, other).astype(BF16)
            ref[2, rows, :] = jnp.where(low_half, other, 0.0).astype(BF16)
            ref[3, rows, :] = jnp.where(low_half, 0.0, full).astype(BF16)
        return 0

    lax.fori_loop(0, 2, project, 0)
    unit_pieces[0].serve(1)
    for k in ks:
        fan_o.forward(k)

    def head_index(p, odd):
        h = 2 * p + odd
        return h, lax.div(h, GROUP) * 2 + odd

    def scores(q_pair, idx, rb, cols):
        s = nt(q_pair, KX[idx, 0:cols, :])
        return s * SCALE + bias[rb * HB : (rb + 1) * HB, 0:cols].astype(F32)

    def attend(p, _):
        lanes = pl.ds(pl.multiple_of(p * LANES, LANES), LANES)
        for rb in range(2):
            rows, cols = slice(rb * HB, (rb + 1) * HB), (rb + 1) * HB
            q_pair = Q[rows, lanes]
            total = None
            for odd in range(2):
                h, idx = head_index(p, odd)
                s = scores(q_pair, idx, rb, cols)
                top = jnp.max(s, axis=1, keepdims=True)
                e = jnp.exp(s - top)
                norm = jnp.sum(e, axis=1, keepdims=True)
                low = (e * (1.0 / norm)).astype(BF16)
                part = nn(low, VX[idx, 0:cols, :])
                total = part if total is None else total + part
                lse = top + jnp.log(norm)
                stats[rows, :] = jnp.where(iota((HB, LANES), 1) == h, lse, stats[rows, :])
            mixed[rows, lanes] = total.astype(BF16)
        return 0

    lax.fori_loop(0, PAIRS // 2, attend, 0)
    serve_down(2)
    lax.fori_loop(PAIRS // 2, PAIRS, attend, 0)
    unit_pieces[1].serve(1)
    fan_o.arrived()
    lax.fori_loop(0, R, unpack_output, 0)
    net.sent(attn_copies)

    for i in range(2):
        rows = slice(i * HB, (i + 1) * HB)
        out = v["tok"][rows, :].astype(F32) + nt(mixed[rows, :], W[WO : WO + D, 0:D])
        res[rows, 0:D] = out
        r2 = lax.rsqrt(jnp.mean(out * out, axis=1, keepdims=True) + EPS)
        stats[rows, :] = jnp.where(iota((HB, LANES), 1) == 127, r2, stats[rows, :])
        S[rows, :] = (out * r2 * vec[2:3, :]).astype(BF16)
        gS.out(i)
    keep_w = net.local(W.at[:, pl.ds(0, D)], v["spill"])
    keep_w.start()
    serve_down(3)
    for x in unit_pieces[2:]:
        x.serve(1)
    gO.forward()
    serve_down(4)
    for d in range(5, long_way + 1):
        serve_down(d)
    keep_w.wait()
    for c in gO.core + gO.on + gS.core:
        c.wait_recv()

    hid, dg, du = v["hid"], v["dg"], v["du"]
    TT, CT = 512, 256

    def unit_tile(first, stride, i):
        return pl.ds(pl.multiple_of((first + stride * i) * CT, CT), CT)

    def phase_one(first, stride, count, lo, hi):
        down_n = (hi - lo) // TT

        def tile(i, _):
            rows = pl.ds(pl.multiple_of(lo + lax.rem(i, down_n) * TT, TT), TT)
            cols = unit_tile(first, stride, lax.div(i, down_n))
            s_rows, o_rows = S[rows, :], dO[rows, :]
            gate = nt(s_rows, Wg[cols, :])
            up = nt(s_rows, Wu[cols, :])
            dh = nn(o_rows, Wd[:, cols])
            sg = jax.nn.sigmoid(gate)
            gs = gate * sg
            hid[rows, cols] = (gs * up).astype(BF16)
            du[rows, cols] = (dh * gs).astype(BF16)
            dg[rows, cols] = (dh * up * (sg + gs * (1.0 - sg))).astype(BF16)
            return 0

        lax.fori_loop(0, count * down_n, tile, 0)

    rG, rU, rD = v["gG"], v["gU"], v["gD"]

    def unit_grads(first, stride, count, lo=0, hi=4 * T, add=False, targets="GU"):
        def tile(i, _):
            cols = unit_tile(first, stride, i)
            for name, ref, left in (("G", rG, dg), ("U", rU, du)):
                if name in targets:
                    value = tn(left[lo:hi, cols], S[lo:hi, :])
                    if add:
                        value = value + ref[cols, :].astype(F32)
                    ref[cols, :] = value.astype(BF16)
            return 0

        lax.fori_loop(0, count, tile, 0)

    def need(t):
        return max(abs(j + geo.OFF) for j in range(t * CT // FP, ((t + 1) * CT - 1) // FP + 1))

    tiles = sorted(range(U // CT), key=need)
    runs = []
    for t in tiles:
        if runs and runs[-1][3] == need(t):
            first, stride, count, step = runs[-1]
            if count == 1 or t - first == stride * count:
                runs[-1] = (first, t - first if count == 1 else stride, count + 1, step)
                continue
        runs.append((t, 1, 1, need(t)))
    early = [x for x in runs if x[3] < long_way - 1]
    middle = [x for x in runs if x[3] == long_way - 1]
    late = [x for x in runs if x[3] == long_way]
    for x in unit_pieces[:2]:
        x.serve(2)
    for run in early[:-1]:
        phase_one(*run[:3], 0, 2 * T)
    for x in unit_pieces[2:]:
        x.serve(2)
    for step in range(3, long_way - 1):
        serve_units(step)
    phase_one(*early[-1][:3], 0, 2 * T)
    for run in early:
        unit_grads(*run[:3], 0, 2 * T)
    for x in unit_pieces[:2]:
        x.serve(long_way - 1)
    gS.forward()
    for c in gS.on:
        c.wait_recv()
    for run in early:
        phase_one(*run[:3], 2 * T, 4 * T)
    for x in unit_pieces[2:]:
        x.serve(long_way - 1)
    for run in middle:
        phase_one(*run[:3], 0, 2 * T)
    serve_units(long_way)
    for run in late:
        phase_one(*run[:3], 0, 4 * T)
    for run in late:
        unit_grads(*run[:3])

    net.release(attn_copies)

    class Scatter:
        def __init__(self, cls, at, buf, add):
            self.nf, self.nb = classes[cls]
            self.at, self.buf, self.add = at, buf, add
            nf, nb = self.nf, self.nb
            self.f = [net.copy(at(nf - t + 1), buf.at[box(t, True)], right) for t in range(1, nf + 1)]
            self.b = [net.copy(at(-(nb - t + 1)), buf.at[box(t, False)], left) for t in range(1, nb + 1)]

        def begin_long(self):
            (self.f if self.nf > self.nb else self.b)[0].start()

        def begin_short(self):
            (self.b if self.nf > self.nb else self.f)[0].start()

        def begin(self):
            self.begin_long()
            self.begin_short()

        def serve(self, t):
            nf, nb = self.nf, self.nb
            if t <= nf:
                self.f[t - 1].wait_recv()
            if t <= nb:
                self.b[t - 1].wait_recv()
            if t < nf:
                self.add(nf - t, box(t, True), True)
            if t < nb:
                self.add(-(nb - t), box(t, False), False)
            if t < nf:
                self.f[t].start()
            if t < nb:
                self.b[t].start()

        def last(self, value):
            return value(box(self.nf, True), True) + value(box(self.nb, False), False)

    def unit_scatter(cls, grad, buf):
        def at(k):
            return grad.at[pl.ds(jslot(k) * FP, FP)]

        def add(k, slot, forward):
            rows = unit_rows(jslot(k))
            grad[rows, :] = (grad[rows, :].astype(F32) + buf[slot].astype(F32)).astype(BF16)

        return Scatter(cls, at, buf, add)

    def down_scatter(cls, grad, buf, lo, size):
        def add(k, slot, forward):
            rows = drow(k, lo, size)
            grad[rows, :] = (grad[rows, :].astype(F32) + turn(buf[slot], forward)).astype(BF16)

        return Scatter(cls, lambda k: grad.at[drow(k, lo, size)], buf, add)

    sG = unit_scatter("A", rG, v["bufG"])
    sU = unit_scatter("B", rU, v["bufU"])
    sDA = down_scatter("A", rD, v["bufA"], 0, DA)
    sDB = down_scatter("B", rD, v["bufB"], DA, DP - DA)
    scatter_steps = [(sG, 1), (sU, 1), (sG, 2), (sDA, 1), (sDB, 1), (sU, 2), (sDA, 2), (sDB, 2)]
    for t in range(3, long_way):
        scatter_steps += [(sG, t), (sU, t), (sDA, t), (sDB, t)]
    scatter_steps += [(sDA, long_way), (sDB, long_way), (sG, long_way), (sU, long_way)]
    scatter_done = [0]

    def serve_scatter(upto):
        while scatter_done[0] < min(upto, len(scatter_steps)):
            x, t = scatter_steps[scatter_done[0]]
            x.serve(t)
            scatter_done[0] += 1

    sG.begin_long()
    sU.begin_long()
    mid = [first + stride * i for first, stride, count, _ in middle for i in range(count)]
    phase_one(mid[0], 1, 1, 2 * T, 4 * T)
    unit_grads(mid[0], 1, 1, targets="G")
    sG.begin_short()
    for t in mid[1:]:
        phase_one(t, 1, 1, 2 * T, 4 * T)
        unit_grads(t, 1, 1, targets="U")
    sU.begin_short()

    def block(ref, i):
        return ref.at[pl.ds(i * T, T)]

    class GroupSum:
        def __init__(self, stages, inbox, part, out):
            self.stages, self.inbox, self.part, self.out = stages, inbox, part, out
            self.far = net.copy(stages[0], inbox[0], core)
            self.over = [
                net.copy(stages[1].at[pl.ds(i * HB, HB)], inbox[1].at[pl.ds(i * HB, HB)], beside)
                for i in range(2)
            ]
            self.near = net.copy(stages[2], inbox[2], core)
            self.over_open = [True, True]

        def fill(self, q, stage):
            for c in parts(0, D, 512):
                stage[:, c] = self.part(q, c).astype(BF16)

        def send_far(self):
            self.fill(3, self.stages[0])
            self.far.start()

        def send_over(self, before=None):
            stage, inbox = self.stages[1], self.inbox[0]
            self.fill(2, stage)
            self.far.wait_recv()
            for i in (1, 0):
                rows = slice(i * HB, (i + 1) * HB)
                stage[rows, :] = (stage[rows, :].astype(F32) + inbox[rows, :].astype(F32)).astype(BF16)
                if before is not None:
                    net.sent(before)
                    before = None
                self.over[i].start()

        def send_near(self):
            self.fill(1, self.stages[2])
            self.near.start()

        def keep(self, more=False):
            for c in parts(0, D, 512):
                value = self.part(0, c)
                self.out[:, c] = self.out[:, c] + value if more else value

        def await_over(self, i):
            if self.over_open[i]:
                self.over_open[i] = False
                self.over[i].wait_recv()

        def finish(self, i):
            rows = slice(i * HB, (i + 1) * HB)
            self.await_over(i)
            total = self.out[rows, :] + self.inbox[1][rows, :].astype(F32)
            self.out[rows, :] = total + self.inbox[2][rows, :].astype(F32)

        def sent(self):
            net.sent([c for c in net.open if any(c is x for x in [self.far, self.near] + self.over)])

    def ds_part(q, c):
        rows = slice(q * T, (q + 1) * T)
        return nn(dg[rows, :], Wg[:, c]) + nn(du[rows, :], Wu[:, c])

    def y_part(q, c):
        rows = slice(q * T, (q + 1) * T)
        return nt(hid[rows, :], Wd[c, :])

    y_out, ds_out = v["y"], v["x"]
    sum_ds = GroupSum(
        [block(AW, 3), v["stage"], block(S, 1)], [block(AW, i) for i in range(3)], ds_part, ds_out
    )
    sum_y = GroupSum(
        [block(dO, 3), block(dO, 2), block(dO, 1)],
        [dg.at[pl.ds(3 * T, T), pl.ds(0, D)], v["y_in"], dg.at[pl.ds(0, T), pl.ds(0, D)]],
        y_part,
        y_out,
    )
    sum_ds.send_far()
    sum_ds.send_over()
    for run in early:
        unit_grads(*run[:3], 2 * T, 4 * T, add=True)
    unit_grads(mid[0], 1, 1, targets="U")
    for t in mid[1:]:
        unit_grads(t, 1, 1, targets="G")
    serve_scatter(2)
    for part in (slice(0, 256), slice(256, 512), slice(512, D)):
        rD[part, :] = tn(dO[:, part], hid[...]).astype(BF16)
    sDA.begin()
    sDB.begin()
    net.sent(gS.copies() + gO.copies())
    sum_ds.send_near()
    sum_ds.keep()
    back_w = net.local(v["spill"], W.at[:, pl.ds(0, D)])
    back_w.start()
    sum_ds.near.wait_recv()
    sum_y.send_far()
    sum_y.send_over(sum_ds.over)
    y_out[...] = res[:, 0:D]
    kv_acc = res
    kv_acc[...] = jnp.zeros_like(kv_acc)

    dm_at, dq_at, low_at = 2 * T, 3 * T, 3 * T
    gains = v["gains"]
    gains[...] = jnp.zeros_like(gains)

    def open_back(i):
        rows = slice(i * HB, (i + 1) * HB)
        r2 = stats[rows, 127:128]
        resid, dsec = y_out[rows, :], ds_out[rows, :]
        gains[2:3, :] += jnp.sum(dsec * resid * r2, axis=0, keepdims=True)
        scaled = dsec * vec[2:3, :]
        inner = jnp.mean(scaled * resid, axis=1, keepdims=True)
        dres = dO[rows, :].astype(F32) + scaled * r2 - resid * (r2 * r2 * r2 * inner)
        ds_out[rows, :] = dres
        low = dres.astype(BF16)
        dg[low_at + i * HB : low_at + (i + 1) * HB, 0:D] = low
        hid[dm_at + i * HB : dm_at + (i + 1) * HB, 0:D] = nn(low, W[WO : WO + D, 0:D]).astype(BF16)

    def attend_back(rb):
        rows, cols = slice(rb * HB, (rb + 1) * HB), (rb + 1) * HB

        def pair(p, _):
            lanes = pl.ds(pl.multiple_of(p * LANES, LANES), LANES)
            q_pair, dm = Q[rows, lanes], hid[dm_at + rb * HB : dm_at + (rb + 1) * HB, lanes]
            total = None
            for odd in range(2):
                h, idx = head_index(p, odd)
                lse = jnp.sum(
                    jnp.where(iota((HB, LANES), 1) == h, stats[rows, :], 0.0), axis=1, keepdims=True
                )
                prob = jnp.exp(scores(q_pair, idx, rb, cols) - lse)
                dp = nt(dm, VX[idx, 0:cols, :])
                t = prob * dp
                delta = jnp.sum(t, axis=1, keepdims=True)
                ds = ((t - prob * delta) * SCALE).astype(BF16)
                k_lanes = pl.ds(pl.multiple_of(idx * LANES, LANES), LANES)
                v_lanes = pl.ds(pl.multiple_of((4 + idx) * LANES, LANES), LANES)
                kv_acc[0:cols, v_lanes] += tn(prob.astype(BF16), dm)
                kv_acc[0:cols, k_lanes] += tn(ds, q_pair)
                part = nn(ds, KX[idx, 0:cols, :])
                total = part if total is None else total + part
            hid[dq_at + rb * HB : dq_at + (rb + 1) * HB, lanes] = rotate_back(total, rows).astype(BF16)
            return 0

        return pair

    serve_scatter(4)
    sum_ds.finish(1)
    back_w.wait()
    open_back(1)
    lax.fori_loop(0, PAIRS // 2, attend_back(1), 0)
    serve_scatter(6)
    lax.fori_loop(PAIRS // 2, PAIRS, attend_back(1), 0)
    sum_ds.finish(0)
    sum_ds.sent()
    open_back(0)
    wgrad = S
    for c in parts(0, D, 256):
        wgrad[D : 2 * D, c] = tn(dg[low_at : low_at + T, 0:D], mixed[:, c]).astype(BF16)

    def pack_first(gi, _):
        q_rows = wgrad[pl.ds(pl.multiple_of(gi * DP, 16), DP), :].astype(F32)
        o_rows = wgrad[pl.ds(pl.multiple_of(D + gi * DP, 16), DP), :].astype(F32)
        k_rows = wgrad[pl.ds(pl.multiple_of(WK + gi * K4, 16), K4), :].astype(F32)
        v_rows = wgrad[pl.ds(pl.multiple_of(WV + gi * K4, 16), K4), :].astype(F32)
        for i in range(4):
            tmp[0:DS, 0:D] = q_rows[i * DS : (i + 1) * DS]
            tmp[KO:VO, 0:D] = k_rows[i * KS : (i + 1) * KS]
            tmp[VO:OO, 0:D] = v_rows[i * KS : (i + 1) * KS]
            tmp[OO:PH, 0:D] = o_rows[i * DS : i * DS + PH - OO]
            AW[pl.ds(pl.multiple_of((i * R + gi) * AR, 16), PH), :] = tmp[0:PH, 0:D].astype(BF16)
        return 0

    def pack_rest(gi, _):
        o_rows = wgrad[pl.ds(pl.multiple_of(D + gi * DP, 16), DP), :].astype(F32)
        for i in range(4):
            tmp[0 : AR - PH, 0:D] = o_rows[i * DS + PH - OO : (i + 1) * DS]
            AW[pl.ds(pl.multiple_of((i * R + gi) * AR + PH, 16), AR - PH), :] = tmp[
                0 : AR - PH, 0:D
            ].astype(BF16)
        return 0

    def inbox_rows(i, k, lo, size):
        at = pl.multiple_of(T + (i * R + place_group(k)) * AR + lo, 16)
        return pl.ds(at, size)

    order = [k for s in range(long_way, 0, -1) for k in both(s)] + [0]

    class AttentionSum:
        def __init__(self, cls, lo, size, ring):
            self.lo, self.size = lo, size

            def at(dev_m, k):
                return AW.at[arow(dev_m, k, lo, size)]

            def inbox(i, k):
                if i == 2:
                    return v["stage"].at[self.rows(k)]
                return dg.at[inbox_rows(i, k, lo, size), pl.ds(0, D)]

            self.far = {k: net.copy(at(m3, k), inbox(0, k), core) for k in order}
            self.near = {k: net.copy(at(m1, k), inbox(1, k), core) for k in order}
            self.over = {k: net.copy(at(m2, k), inbox(2, k), beside) for k in order}

            def add(k, slot, forward):
                rows = arow(m, k, lo, size)
                AW[rows, :] = (AW[rows, :].astype(F32) + ring[slot].astype(F32)).astype(BF16)

            self.ring = Scatter(cls, lambda k: at(m, k), ring, add)

        def rows(self, k):
            return pl.ds(pl.multiple_of(place_group(k) * AR + self.lo, 16), self.size)

        def begin(self):
            for k in order:
                self.far[k].start()
            for k in order:
                self.near[k].start()

        def send_over(self, k):
            self.far[k].wait_recv()
            rows = arow(m2, k, self.lo, self.size)
            got = dg[inbox_rows(0, k, self.lo, self.size), 0:D]
            AW[rows, :] = (AW[rows, :].astype(F32) + got.astype(F32)).astype(BF16)
            self.over[k].start()

        def settle(self, k):
            self.near[k].wait_recv()
            self.over[k].wait_recv()
            rows = arow(m, k, self.lo, self.size)
            total = AW[rows, :].astype(F32)
            total = total + dg[inbox_rows(1, k, self.lo, self.size), 0:D].astype(F32)
            total = total + v["stage"][self.rows(k), :].astype(F32)
            AW[rows, :] = total.astype(BF16)

    sum_p = AttentionSum("A", 0, PH, v["ringP"])
    sum_o = AttentionSum("B", PH, AR - PH, v["ringO"])
    lax.fori_loop(0, R, pack_rest, 0)
    sum_o.begin()
    serve_scatter(8)
    lax.fori_loop(0, PAIRS, attend_back(0), 0)
    for i in (1, 0):
        sum_y.await_over(i)
    for k in order:
        sum_o.send_over(k)
    serve_scatter(10)

    low_half = iota((T, LANES), 1) < HD

    def joined(part):
        return jnp.where(
            low_half, part(0) + pltpu.roll(part(1), HD, 1), pltpu.roll(part(2), HD, 1) + part(3)
        )

    dkv = v["dkv"]
    dkv[:, 0:LANES] = rotate_back(
        joined(lambda i: kv_acc[:, i * LANES : (i + 1) * LANES]), slice(0, T)
    ).astype(BF16)
    dkv[:, LANES : 2 * LANES] = joined(lambda i: kv_acc[:, (4 + i) * LANES : (5 + i) * LANES]).astype(BF16)
    for c in parts(0, D, 256):
        wgrad[0:D, c] = tn(hid[dq_at : dq_at + T, 0:D], normed[:, c]).astype(BF16)
        wgrad[2 * D :, c] = tn(dkv[...], normed[:, c]).astype(BF16)
    lax.fori_loop(0, R, pack_first, 0)
    sum_p.begin()
    for k in order[:3]:
        sum_p.send_over(k)

    gains[1:2, :] = jnp.sum(hid[dq_at : dq_at + T, 0:D].astype(F32), axis=0, keepdims=True)
    gains[3:4, 0 : 2 * LANES] = jnp.sum(dkv[...].astype(F32), axis=0, keepdims=True)

    def close_back(i, _):
        rows = pl.ds(pl.multiple_of(i * HB, HB), HB)
        dn = nn(hid[pl.ds(pl.multiple_of(dq_at + i * HB, HB), HB), 0:D], W[WQ : WQ + D, 0:D])
        dn += nn(dkv[rows, :], W[WK : WK + 2 * KV * HD, 0:D])
        xb = v["tok"][rows, :].astype(F32)
        r1 = stats[rows, 126:127]
        gains[0:1, :] += jnp.sum(dn * xb * r1, axis=0, keepdims=True)
        scaled = dn * vec[0:1, :]
        inner = jnp.mean(scaled * xb, axis=1, keepdims=True)
        ds_out[rows, :] = ds_out[rows, :] + scaled * r1 - xb * (r1 * r1 * r1 * inner)
        return 0

    lax.fori_loop(0, 2, close_back, 0)
    keep_x = net.local(ds_out, v["x_out"])
    keep_x.start()

    SG = v["SG"]

    def collect_tile(i, _):
        start = pl.multiple_of(i * ST, ST)
        first = lax.rem(iota((ST, 1), 0), 8) == 0
        total = None
        for row, width, size, offset, stride in (
            (gains[0:1, :], D, DS, 0, 1),
            (gains[1:2, :], D, DS, DS, 1),
            (gains[2:3, :], D, DS, 2 * DS, 1),
            (gains[3:4, 0:LANES], LANES, KS, 3 * DS, 1),
            (gains[3:4, LANES : 2 * LANES], LANES, KS, 3 * DS + KS, 1),
        ):
            owner, _ = owner_of(iota((1, width), 1), size)
            _, inner = owner_of(iota((width, LANES), 0), size)
            pick = (iota((width, LANES), 1) == inner * stride + offset).astype(BF16)
            full = jnp.where((row_device(start) == owner) & first, row, 0.0)
            high = full.astype(BF16)
            part = nn(high, pick) + nn((full - high.astype(F32)).astype(BF16), pick)
            total = part if total is None else total + part
        SG[pl.ds(start, ST), :] = total
        return 0

    lax.fori_loop(0, rows_n // ST, collect_tile, 0)

    def sg_rows(dev_m):
        return pl.ds(pl.multiple_of(dev_m * R * 8, 8), R * 8)

    sg_in = v["sg_in"]
    s_far = net.copy(SG.at[sg_rows(m3)], sg_in.at[0], core)
    s_near = net.copy(SG.at[sg_rows(m1)], sg_in.at[1], core)
    s_over = net.copy(SG.at[sg_rows(m2)], sg_in.at[2], beside)
    s_far.start()
    s_near.start()
    s_far.wait_recv()
    SG[sg_rows(m2), :] = SG[sg_rows(m2), :] + sg_in[0]
    s_over.start()
    for k in order[3:]:
        sum_p.send_over(k)
    serve_scatter(11)

    def down_send():
        tmp[0:DA, :] = rD[drow(0, 0, DA), :].astype(F32) + sDA.last(
            lambda i, f: turn(v["bufA"][i], f)
        )
        tmp[DA:DP, :] = rD[drow(0, DA, DP - DA), :].astype(F32) + sDB.last(
            lambda i, f: turn(v["bufB"][i], f)
        )
        for i in range(4):
            dx[i, 0:DS, :] = tmp[i * DS : (i + 1) * DS, :].astype(BF16)
        for c in home:
            c.start()
        down_p[m] = dx[m]

    def down_home():
        for c in home:
            c.wait_recv()
        for i in range(4):
            full = turn_by_seat(down_p[i].astype(F32), True)
            for place in range(R):
                v["down_out"][:, owned_units(place, i)] = full[0:DS, place * FP : place * FP + FS]

    home = [
        net.copy(dx.at[dst_m], down_p.at[m], dev)
        for dst_m, dev in ((m1, core), (m2, beside), (m3, across))
    ]

    def small_add(k, slot, forward):
        SG[srow(m, k), :] = SG[srow(m, k), :] + v["sring"][slot]

    ssm = Scatter("A", lambda k: SG.at[srow(m, k)], v["sring"], small_add)

    def settle(s):
        for k in both(s) if s else (0,):
            sum_p.settle(k)
            sum_o.settle(k)

    def close_y(i):
        sum_y.finish(i)
        rows = slice(i * HB, (i + 1) * HB)
        y_out[rows, :] = y_out[rows, :] * stats[rows, 125:126]

    settle(long_way)
    settle(long_way - 1)
    sum_p.ring.begin()
    sum_o.ring.begin()
    sum_y.send_near()
    s_near.wait_recv()
    s_over.wait_recv()
    SG[sg_rows(m), :] = SG[sg_rows(m), :] + sg_in[1] + sg_in[2]
    ssm.begin()
    sum_y.keep(True)
    for t in range(1, long_way + 1):
        if t < long_way:
            settle(long_way - t - 1)
        for x in (sum_p.ring, sum_o.ring, ssm):
            x.serve(t)
        if t == 1:
            sum_y.near.wait_recv()
            close_y(1)
            close_y(0)
            sum_y.sent()
            keep_y = net.local(y_out, v["y_out"])
            keep_y.start()
            serve_scatter(12)
        if t == 2:
            serve_scatter(14)
            down_send()
    mine = arow(m, 0)
    low = AW[mine, :].astype(F32)
    first = low[0:PH] + sum_p.ring.last(lambda i, f: v["ringP"][i].astype(F32))
    rest = low[PH:AR] + sum_o.ring.last(lambda i, f: v["ringO"][i].astype(F32))
    v["small_out"][...] = SG[srow(m, 0), :] + ssm.last(lambda i, f: v["sring"][i])
    v["q_out"][...] = first[0:DS]
    v["k_out"][...] = first[KO:VO]
    v["v_out"][...] = first[VO:OO]
    v["o_out"][0 : PH - OO, :] = first[OO:PH]
    v["o_out"][PH - OO : DS, :] = rest

    serve_scatter(len(scatter_steps))
    mine = slice(own * FP, own * FP + FS)
    res[0:FS, 0:D] = rG[mine, :].astype(F32) + sG.last(
        lambda i, f: v["bufG"][i, 0:FS, :].astype(F32)
    )
    res[FS : 2 * FS, 0:D] = rU[mine, :].astype(F32) + sU.last(
        lambda i, f: v["bufU"][i, 0:FS, :].astype(F32)
    )
    keep_rows = net.local(res.at[pl.ds(0, 2 * FS), pl.ds(0, D)], v["rows_out"])
    keep_rows.start()
    down_home()
    net.sent(net.open)
    for c in (keep_y, keep_x, keep_rows):
        c.wait()


def layer(geo, ins):
    R, T, D, FP, U, DSP, DP, DA = geo.R, geo.T, geo.D, geo.FP, geo.U, geo.DSP, geo.DP, geo.DA
    AR = geo.AR
    outs = {
        "y_out": ((T, D), F32),
        "x_out": ((T, D), F32),
        "rows_out": ((2 * geo.FS, D), F32),
        "q_out": ((geo.DS, D), F32),
        "k_out": ((geo.KS, D), F32),
        "v_out": ((geo.KS, D), F32),
        "o_out": ((geo.DS, D), F32),
        "down_out": ((geo.DS, R * 4 * geo.FS), F32),
        "small_out": ((8, LANES), F32),
        "spill": ((2 * D + 2 * KV * HD, D), BF16),
    }
    scratch = {
        "down_p": ((4, DSP, U), BF16),
        "y": ((T, D), F32),
        "x": ((T, D), F32),
        "dx": ((4, DSP, U), BF16),
        "AW": ((4 * R * AR, D), BF16),
        "SM": ((4 * R * 8, LANES), F32),
        "SG": ((4 * R * 8, LANES), F32),
        "sg_in": ((3, R * 8, LANES), F32),
        "sring": ((4, 8, LANES), F32),
        "ringP": ((4, geo.PH, D), BF16),
        "ringO": ((4, AR - geo.PH, D), BF16),
        "stage": ((T, D), BF16),
        "y_in": ((T, D), BF16),
        "S": ((4 * T, D), BF16),
        "dO": ((4 * T, D), BF16),
        "tmp": ((DP, U), F32),
        "tmp3": ((8 * geo.KS, D), F32),
        "Wg": ((U, D), BF16),
        "Wu": ((U, D), BF16),
        "Wd": ((D, U), BF16),
        "hid": ((4 * T, U), BF16),
        "dg": ((4 * T, U), BF16),
        "du": ((4 * T, U), BF16),
        "gG": ((U, D), BF16),
        "gU": ((U, D), BF16),
        "gD": ((D, U), BF16),
        "bufG": ((4, FP, D), BF16),
        "bufU": ((4, FP, D), BF16),
        "bufA": ((4, DA, U), BF16),
        "bufB": ((4, DP - DA, U), BF16),
        "stats": ((T, LANES), F32),
        "bias": ((T, T), BF16),
        "cos": ((T, LANES), F32),
        "sin": ((T, LANES), F32),
        "vec": ((8, D), F32),
        "gains": ((8, D), F32),
        "normed": ((T, D), BF16),
        "Q": ((T, D), BF16),
        "mixed": ((T, D), BF16),
        "KX": ((4, T, LANES), BF16),
        "VX": ((4, T, LANES), BF16),
        "res": ((T, D + LANES), F32),
        "dkv": ((T, 2 * LANES), BF16),
    }
    alias = {"W": "du"}
    names = list(ins) + list(outs) + list(scratch) + ["send_sems", "recv_sems", "local_sems"]
    vm = pl.BlockSpec(memory_space=pltpu.VMEM)
    hbm = pl.BlockSpec(memory_space=pl.ANY)

    def body(*refs):
        table = dict(zip(names, refs))
        for new, old in alias.items():
            table[new] = table[old]
        kernel_body(geo, list(table), *table.values())

    res = pl.pallas_call(
        body,
        out_shape=[jax.ShapeDtypeStruct(s, d) for s, d in outs.values()],
        in_specs=[hbm if n == "cot" else vm for n in ins],
        out_specs=[hbm if n in ("y_out", "x_out", "rows_out", "spill") else vm for n in outs],
        scratch_shapes=[pltpu.VMEM(s, d) for s, d in scratch.values()]
        + [pltpu.SemaphoreType.DMA((28 * R + 16,))] * 2
        + [pltpu.SemaphoreType.DMA((6,))],
        compiler_params=pltpu.CompilerParams(
            collective_id=0, has_side_effects=True, vmem_limit_bytes=64 * 2**20
        ),
    )(*ins.values())
    return dict(zip(outs, res))


def hand_out(geo, res):
    whole = ["y_out", "x_out", "down_out", "q_out", "k_out", "v_out", "o_out"]
    rows = res["rows_out"].shape[0] // 2
    shapes = [res[n].shape for n in whole] + [(rows, geo.D)] * 2

    def body(*refs):
        count = len(shapes)
        sources, both, small = refs[: count - 2], refs[count - 2], refs[count - 1]
        results, vectors = refs[count : 2 * count], refs[2 * count : 2 * count + 4]
        held, sems = refs[2 * count + 4 : 3 * count + 4], refs[-1]
        sources += tuple(both.at[pl.ds(i * rows, rows)] for i in range(2))
        inward = [pltpu.make_async_copy(sources[i], held[i], sems.at[0, i]) for i in range(count)]
        outward = [pltpu.make_async_copy(held[i], results[i], sems.at[1, i]) for i in range(count)]
        for c in inward:
            c.start()
        DS, KS = geo.DS, geo.KS
        for i in range(3):
            vectors[i][...] = small[0:1, i * DS : (i + 1) * DS]
        for i in range(2):
            vectors[3][i : i + 1, :] = small[0:1, 3 * DS + i * KS : 3 * DS + (i + 1) * KS]
        for i in range(count):
            inward[i].wait()
            outward[i].start()
        for c in outward:
            c.wait()

    hbm, vm = pl.BlockSpec(memory_space=pltpu.HBM), pl.BlockSpec(memory_space=pltpu.VMEM)
    outs = pl.pallas_call(
        body,
        out_shape=[jax.ShapeDtypeStruct(s, F32) for s in shapes + [(1, geo.DS)] * 3 + [(2, geo.KS)]],
        in_specs=[hbm] * (len(shapes) - 1) + [vm],
        out_specs=[hbm] * len(shapes) + [vm] * 4,
        scratch_shapes=[pltpu.VMEM(s, F32) for s in shapes]
        + [pltpu.SemaphoreType.DMA((2, len(shapes)))],
        compiler_params=pltpu.CompilerParams(vmem_limit_bytes=64 * 2**20),
    )(*[res[n] for n in whole + ["rows_out", "small_out"]])
    results = ["y", "x", "down", "q", "k", "v", "o", "gate", "up", "g1", "qb", "g2", "kvb"]
    return dict(zip(results, outs))


D = 896
eps_norm = 1e-06
rope_base = 1000000.0
masked_value = -1e30


def apply_weight(left, weight):
    return lax.dot_general(
        left, weight, (((1,), (1,)), ((), ())), preferred_element_type=jnp.float32
    )


def apply_transpose(left, weight):
    return jnp.dot(left, weight, preferred_element_type=jnp.float32)


def weight_grad(grad_rows, input_rows):
    return lax.dot_general(
        grad_rows, input_rows, (((0,), (0,)), ((), ())), preferred_element_type=jnp.float32
    )


def rms_scale(field_rows):
    return lax.rsqrt(jnp.mean(field_rows * field_rows, axis=1, keepdims=True) + eps_norm)


def norm_backward(grad_rows, field_rows, scale_rows, gain_values):
    scaled = grad_rows * gain_values
    return scaled * scale_rows - field_rows * scale_rows**3 * jnp.mean(
        scaled * field_rows, axis=1, keepdims=True
    )


def rope_tables(block_segments):
    slot_index = jnp.arange(block_segments.shape[0])
    same_segment = block_segments[:, None] == block_segments[None, :]
    earlier = slot_index[None, :] < slot_index[:, None]
    positions = jnp.sum((same_segment & earlier).astype(jnp.float32), axis=1)
    frequency = jnp.exp(jnp.arange(HD // 2, dtype=jnp.float32) * (-2.0 * math.log(rope_base) / HD))
    angles = positions[:, None] * frequency[None, :]
    return (jnp.cos(angles)[:, None, :], jnp.sin(angles)[:, None, :])


def rotate(vectors, cosine_table, sine_table):
    first_half = vectors[..., : HD // 2]
    second_half = vectors[..., HD // 2 :]
    return jnp.concatenate(
        [
            first_half * cosine_table - second_half * sine_table,
            second_half * cosine_table + first_half * sine_table,
        ],
        axis=-1,
    )


def rotate_back(vectors, cosine_table, sine_table):
    first_half = vectors[..., : HD // 2]
    second_half = vectors[..., HD // 2 :]
    return jnp.concatenate(
        [
            first_half * cosine_table + second_half * sine_table,
            second_half * cosine_table - first_half * sine_table,
        ],
        axis=-1,
    )


def plain_local(
    tokens,
    segment_ids,
    live_counts,
    first_gain,
    query_weight,
    query_bias,
    key_weight,
    value_weight,
    key_value_bias,
    output_weight,
    second_gain,
    gate_weight,
    up_weight,
    down_weight,
    cotangent,
):
    attention_set = (
        lax.all_gather(first_gain, "dp", axis=0, tiled=True),
        lax.all_gather(query_weight, "dp", axis=0, tiled=True),
        lax.all_gather(query_bias, "dp", axis=0, tiled=True),
        lax.all_gather(key_weight, "dp", axis=0, tiled=True),
        lax.all_gather(value_weight, "dp", axis=0, tiled=True),
        lax.all_gather(key_value_bias, "dp", axis=0, tiled=True),
        lax.all_gather(output_weight, "dp", axis=0, tiled=True),
    )
    first_full, query_full, query_bias_full, key_full, value_full, pair_bias_full, output_full = (
        attention_set
    )
    slot_count = tokens.shape[0]
    group_size = HEADS // KV
    scale_factor = HD ** (-0.5)
    slot_index = jnp.arange(slot_count)
    live_rows = (slot_index < live_counts[0]).astype(jnp.float32)
    allowed = (segment_ids[:, None] == segment_ids[None, :]) & (
        slot_index[None, :] <= slot_index[:, None]
    ) & (live_rows[None, :] > 0.5) | (slot_index[None, :] == slot_index[:, None])
    cosine_table, sine_table = rope_tables(segment_ids)
    token_rows = tokens.astype(jnp.float32)
    first_scale = rms_scale(token_rows)
    normed = (token_rows * first_scale * first_full.astype(jnp.float32)).astype(jnp.bfloat16)
    pair_bias_values = pair_bias_full.astype(jnp.float32)
    query_pre = apply_weight(normed, query_full) + query_bias_full.astype(jnp.float32)
    key_pre = apply_weight(normed, key_full) + pair_bias_values[:, 0]
    values = (apply_weight(normed, value_full) + pair_bias_values[:, 1]).astype(jnp.bfloat16)
    values = values.reshape(slot_count, KV, HD)
    rotated_queries = rotate(query_pre.reshape(slot_count, HEADS, HD), cosine_table, sine_table)
    rotated_queries = rotated_queries.astype(jnp.bfloat16).reshape(slot_count, KV, group_size, HD)
    rotated_keys = rotate(key_pre.reshape(slot_count, KV, HD), cosine_table, sine_table).astype(
        jnp.bfloat16
    )

    def attention_logits():
        scores = jnp.einsum(
            "ikgd,jkd->kgij", rotated_queries, rotated_keys, preferred_element_type=jnp.float32
        )
        return jnp.where(allowed[None, None], scores * scale_factor, masked_value)

    logits = attention_logits()
    row_top = jnp.max(logits, axis=-1, keepdims=True)
    exponent = jnp.exp(logits - row_top)
    row_total = jnp.sum(exponent, axis=-1, keepdims=True)
    weights_low = (exponent / row_total).astype(jnp.bfloat16)
    mixed_heads = jnp.einsum(
        "kgij,jkd->ikgd", weights_low, values, preferred_element_type=jnp.float32
    )
    mixed_heads = mixed_heads.reshape(slot_count, D).astype(jnp.bfloat16)
    residual = token_rows + apply_weight(mixed_heads, output_full)
    feed_set = (
        lax.all_gather(second_gain, "dp", axis=0, tiled=True),
        lax.all_gather(gate_weight, "dp", axis=0, tiled=True),
        lax.all_gather(up_weight, "dp", axis=0, tiled=True),
        lax.all_gather(down_weight, "dp", axis=0, tiled=True),
    )
    second_full, gate_full, up_full, down_full = feed_set
    second_scale = rms_scale(residual)
    second = (residual * second_scale * second_full.astype(jnp.float32)).astype(jnp.bfloat16)
    gate_value = apply_weight(second, gate_full)
    up_value = apply_weight(second, up_full)
    hidden = (jax.nn.silu(gate_value) * up_value).astype(jnp.bfloat16)
    layer_out = (residual + apply_weight(hidden, down_full)) * live_rows[:, None]
    feed_back = (
        lax.all_gather(second_gain, "dp", axis=0, tiled=True),
        lax.all_gather(gate_weight, "dp", axis=0, tiled=True),
        lax.all_gather(up_weight, "dp", axis=0, tiled=True),
        lax.all_gather(down_weight, "dp", axis=0, tiled=True),
    )
    back_second, back_gate, back_up, back_down = feed_back
    out_grad = cotangent.astype(jnp.float32) * live_rows[:, None]
    out_grad_low = out_grad.astype(jnp.bfloat16)
    down_shard = lax.psum_scatter(
        weight_grad(out_grad_low, hidden), "dp", scatter_dimension=0, tiled=True
    )
    hidden_grad = apply_transpose(out_grad_low, back_down)
    sigmoid_gate = jax.nn.sigmoid(gate_value)
    up_grad_rows = (hidden_grad * (gate_value * sigmoid_gate)).astype(jnp.bfloat16)
    gate_grad_rows = (
        hidden_grad * up_value * sigmoid_gate * (1.0 + gate_value * (1.0 - sigmoid_gate))
    ).astype(jnp.bfloat16)
    gate_part = weight_grad(gate_grad_rows, second)
    up_part = weight_grad(up_grad_rows, second)
    gate_up_shard = lax.psum_scatter(
        jnp.concatenate([gate_part, up_part], axis=1), "dp", scatter_dimension=0, tiled=True
    )
    model_width = second.shape[1]
    gate_shard = gate_up_shard[:, :model_width]
    up_shard = gate_up_shard[:, model_width:]
    second_grad_rows = apply_transpose(gate_grad_rows, back_gate) + apply_transpose(
        up_grad_rows, back_up
    )
    second_gain_grad = jnp.sum(second_grad_rows * residual * second_scale, axis=0)
    residual_grad = out_grad + norm_backward(
        second_grad_rows, residual, second_scale, back_second.astype(jnp.float32)
    )
    attention_back = (
        lax.all_gather(first_gain, "dp", axis=0, tiled=True),
        lax.all_gather(query_weight, "dp", axis=0, tiled=True),
        lax.all_gather(query_bias, "dp", axis=0, tiled=True),
        lax.all_gather(key_weight, "dp", axis=0, tiled=True),
        lax.all_gather(value_weight, "dp", axis=0, tiled=True),
        lax.all_gather(key_value_bias, "dp", axis=0, tiled=True),
        lax.all_gather(output_weight, "dp", axis=0, tiled=True),
    )
    back_first = attention_back[0]
    back_query = attention_back[1]
    back_key = attention_back[3]
    back_value = attention_back[4]
    back_output = attention_back[6]
    branch_grad = residual_grad.astype(jnp.bfloat16)
    output_grad = weight_grad(branch_grad, mixed_heads)
    mixed_grad = apply_transpose(branch_grad, back_output).astype(jnp.bfloat16)
    mixed_grad = mixed_grad.reshape(slot_count, KV, group_size, HD)
    probs = jnp.exp(attention_logits() - row_top) / row_total
    probs_low = probs.astype(jnp.bfloat16)
    value_grad_rows = jnp.einsum(
        "kgij,ikgd->jkd", probs_low, mixed_grad, preferred_element_type=jnp.float32
    )
    prob_grad = jnp.einsum("ikgd,jkd->kgij", mixed_grad, values, preferred_element_type=jnp.float32)
    logit_grad = probs * (prob_grad - jnp.sum(probs * prob_grad, axis=-1, keepdims=True))
    score_grad = (logit_grad * scale_factor).astype(jnp.bfloat16)
    query_rot_grad = jnp.einsum(
        "kgij,jkd->ikgd", score_grad, rotated_keys, preferred_element_type=jnp.float32
    )
    key_rot_grad = jnp.einsum(
        "kgij,ikgd->jkd", score_grad, rotated_queries, preferred_element_type=jnp.float32
    )
    query_grad_rows = rotate_back(
        query_rot_grad.reshape(slot_count, HEADS, HD), cosine_table, sine_table
    )
    query_grad_rows = query_grad_rows.astype(jnp.bfloat16).reshape(slot_count, D)
    key_grad_rows = (
        rotate_back(key_rot_grad, cosine_table, sine_table)
        .astype(jnp.bfloat16)
        .reshape(slot_count, KV * HD)
    )
    value_grad_low = value_grad_rows.astype(jnp.bfloat16).reshape(slot_count, KV * HD)
    query_grad = weight_grad(query_grad_rows, normed)
    query_bias_grad = jnp.sum(query_grad_rows.astype(jnp.float32), axis=0)
    key_grad = weight_grad(key_grad_rows, normed)
    value_grad = weight_grad(value_grad_low, normed)
    pair_bias_grad = jnp.stack(
        [
            jnp.sum(key_grad_rows.astype(jnp.float32), axis=0),
            jnp.sum(value_grad_low.astype(jnp.float32), axis=0),
        ],
        axis=1,
    )
    first_grad_rows = (
        apply_transpose(query_grad_rows, back_query)
        + apply_transpose(key_grad_rows, back_key)
        + apply_transpose(value_grad_low, back_value)
    )
    first_gain_grad = jnp.sum(first_grad_rows * token_rows * first_scale, axis=0)
    input_grad = residual_grad + norm_backward(
        first_grad_rows, token_rows, first_scale, back_first.astype(jnp.float32)
    )
    attention_shards = (
        lax.psum_scatter(first_gain_grad, "dp", scatter_dimension=0, tiled=True),
        lax.psum_scatter(query_grad, "dp", scatter_dimension=0, tiled=True),
        lax.psum_scatter(query_bias_grad, "dp", scatter_dimension=0, tiled=True),
        lax.psum_scatter(key_grad, "dp", scatter_dimension=0, tiled=True),
        lax.psum_scatter(value_grad, "dp", scatter_dimension=0, tiled=True),
        lax.psum_scatter(pair_bias_grad, "dp", scatter_dimension=0, tiled=True),
        lax.psum_scatter(output_grad, "dp", scatter_dimension=0, tiled=True),
        lax.psum_scatter(second_gain_grad, "dp", scatter_dimension=0, tiled=True),
    )
    return (layer_out, input_grad) + tuple(attention_shards) + (gate_shard, up_shard, down_shard)


def fused_local(
    geo,
    tokens,
    segment_ids,
    live_counts,
    first_gain,
    query_weight,
    query_bias,
    key_weight,
    value_weight,
    key_value_bias,
    output_weight,
    second_gain,
    gate_weight,
    up_weight,
    down_weight,
    cotangent,
):
    T, DS = geo.T, geo.DS
    live = (jnp.arange(T) < live_counts[0]).astype(F32)
    vectors = jnp.concatenate(
        [first_gain, query_bias, second_gain, key_value_bias.reshape(-1)]
    ).astype(F32)
    aux = jnp.stack(
        [segment_ids.astype(F32), live, jnp.pad(vectors, (0, T - vectors.shape[0]))]
    )
    aux = jnp.pad(aux, ((0, 5), (0, 0)))
    res = layer(
        geo,
        {
            "tok": tokens,
            "cot": cotangent,
            "wq": query_weight,
            "wo": output_weight,
            "wk": key_weight,
            "wv": value_weight,
            "gate": gate_weight,
            "up": up_weight,
            "down": down_weight,
            "aux": aux,
        },
    )
    out = hand_out(geo, res)
    return (
        out["y"],
        out["x"],
        out["g1"].reshape(DS),
        out["q"],
        out["qb"].reshape(DS),
        out["k"],
        out["v"],
        out["kvb"].T,
        out["o"],
        out["g2"].reshape(DS),
        out["gate"],
        out["up"],
        out["down"],
    )


def local(tokens, segment_ids, live_counts, first_gain, *rest):
    geo = Geometry(
        lax.axis_size("dp"), tokens.shape[0], tokens.shape[1], rest[9].shape[1]
    )
    layer_of = functools.partial(fused_local, geo) if geo.fits() else plain_local
    return layer_of(tokens, segment_ids, live_counts, first_gain, *rest)


def solution(mesh):
    in_specs = (
        P("dp", None),
        P("dp"),
        P("dp"),
        P("dp"),
        P("dp", None),
        P("dp"),
        P("dp", None),
        P("dp", None),
        P("dp", None),
        P("dp", None),
        P("dp"),
        P("dp", None),
        P("dp", None),
        P("dp", None),
        P("dp", None),
    )
    out_specs = (
        P("dp", None),
        P("dp", None),
        P("dp"),
        P("dp", None),
        P("dp"),
        P("dp", None),
        P("dp", None),
        P("dp", None),
        P("dp", None),
        P("dp"),
        P("dp", None),
        P("dp", None),
        P("dp", None),
    )
    return jax.shard_map(local, mesh=mesh, in_specs=in_specs, out_specs=out_specs, check_vma=False)
```
